32 devices in a mesh: dp: 8 (over y, x, core), tensor: 4 (over z).
Axes of the slice: x: 2, y: 2, z: 4, core: 2. Of those that a mesh axis runs over, the one named last changes fastest.
Arguments:
- tokens: bfloat16 [13312, 1152], P(('dp', 'tensor')), may hold values from -6 to 6
- cotangent: bfloat16 [13312, 1152], P(('dp', 'tensor')), may hold values from -6 to 6
- item_bucket: int32 [13], replicated, may hold values from 0 to 2
- text_len: int32 [13], replicated, may hold values from 75 to 300
- t_mod: float32 [13, 6, 1152], replicated, may hold values from -1.75 to 1.75
- text_tokens: bfloat16 [300, 1152], P('tensor'), may hold values from -6 to 6
- shift_table: float32 [6, 1152], replicated, may hold values from 0.5 to 1.5
- w_qkv: bfloat16 [1152, 3, 1152], P(None, None, 'tensor'), may hold values from -0.1875 to 0.1875
- w_out: bfloat16 [1152, 1152], P('tensor'), may hold values from -0.1875 to 0.1875
- out_bias: float32 [1152], replicated, may hold values from -1.75 to 1.75
- w_xq: bfloat16 [1152, 1152], P(None, 'tensor'), may hold values from -0.1875 to 0.1875
- xq_bias: float32 [1152], P('tensor'), may hold values from -1.75 to 1.75
- w_xkv: bfloat16 [1152, 2, 1152], P(None, None, 'tensor'), may hold values from -0.1875 to 0.1875
- xv_bias: float32 [1152], P('tensor'), may hold values from -0.625 to 0.625
- w_xo: bfloat16 [1152, 1152], P('tensor'), may hold values from -1.5 to 1.5
- xo_bias: float32 [1152], replicated, may hold values from -1.75 to 1.75
- w_in: bfloat16 [1152, 2, 2880], P(None, None, 'tensor'), may hold values from -0.1875 to 0.1875
- in_bias: float32 [2, 2880], P(None, 'tensor'), may hold values from -1.75 to 1.75
- dw_weight: float32 [9, 2, 2880], P(None, None, 'tensor'), may hold values from -2 to 2
- dw_bias: float32 [2, 2880], P(None, 'tensor'), may hold values from -1.75 to 1.75
- w_pt: bfloat16 [2880, 1152], P('tensor'), may hold values from -0.109375 to 0.109375
Outputs:
- out_tokens: bfloat16 [13312, 1152], P(('dp', 'tensor'))
- d_tokens: float32 [13312, 1152], P(('dp', 'tensor'))
- d_t_mod: float32 [13, 6, 1152], replicated
- d_text: float32 [300, 1152], P('tensor')
- d_shift_table: float32 [6, 1152], replicated
- d_w_qkv: float32 [1152, 3, 1152], P(None, None, 'tensor')
- d_w_out: float32 [1152, 1152], P('tensor')
- d_out_bias: float32 [1152], replicated
- d_w_xq: float32 [1152, 1152], P(None, 'tensor')
- d_xq_bias: float32 [1152], P('tensor')
- d_w_xkv: float32 [1152, 2, 1152], P(None, None, 'tensor')
- d_xv_bias: float32 [1152], P('tensor')
- d_w_xo: float32 [1152, 1152], P('tensor')
- d_xo_bias: float32 [1152], replicated
- d_w_in: float32 [1152, 2, 2880], P(None, None, 'tensor')
- d_in_bias: float32 [2, 2880], P(None, 'tensor')
- d_dw_weight: float32 [9, 2, 2880], P(None, None, 'tensor')
- d_dw_bias: float32 [2, 2880], P(None, 'tensor')
- d_w_pt: float32 [2880, 1152], P('tensor')
The draws below stay inside these ranges and needn't reach their ends.
All inputs are finite; a program needn't handle non-finite values.
Results may differ from the reference program's by a relative error of at most 0.035.
Values may be sent and summed in bfloat16 or wider, within the bound.
No kernel may reach another device: no remote copies, remote signals or barrier semaphores. Data moves between devices by JAX's collectives and lax.ppermute only.
A program may use at most 320 MiB of HBM per device.

```python
import jax
import jax.numpy as jnp
from jax import lax

D = 1152
HEAD = 32
HEADS = 36
XHEADS = 16
XHEAD = 72
FF = 2880
TXT = 300
SIDE = 32
ITEM_SLOTS = 1024
HALO = 41
ITEMS = 13
SLOTS = 13312


def plant(entries, stream_key, low, high):
    longest = entries.shape.index(max(entries.shape))
    spots = []
    for shift in (0, 1):
        where = [jax.random.randint(jax.random.fold_in(stream_key, axis), (), 0, length) for axis, length in enumerate(entries.shape)]
        where[longest] = (where[longest] + shift) % entries.shape[longest]
        spots.append(tuple(where))
    return entries.at[spots[0]].set(low).at[spots[1]].set(high)


def block_scale(stream_key, shape, pieces, low, top_value):
    loudness = 1.0
    for dim, blocks in pieces:
        steps = jax.random.uniform(jax.random.fold_in(jax.random.fold_in(stream_key, 6), dim), (blocks,), jnp.float32, low / len(pieces), top_value / len(pieces))
        loudness = loudness * jnp.repeat(jnp.exp(steps), shape[dim] // blocks).reshape((-1,) + (1,) * (len(shape) - 1 - dim))
    return loudness


def normal_values(key, shape, scale, reach, pieces=(), kind=jnp.bfloat16):
    level = block_scale(key, shape, pieces, -0.22, 0.18) if pieces else 1.0
    entries = jax.random.normal(key, shape, jnp.float32) * scale * level
    return jnp.minimum(jnp.maximum(entries, -reach), reach).astype(kind)


def setup_inputs(seed: int = 0) -> dict:
    arg_keys = jax.random.split(jax.random.key(seed), 22)
    tokens = normal_values(arg_keys[0], (SLOTS, D), 1.0, 6.0, ((0, 32),))
    cotangent = normal_values(arg_keys[1], (SLOTS, D), 1.0, 6.0, ((0, 32),))
    item_bucket = plant(jax.random.randint(arg_keys[2], (ITEMS,), 0, 3), jax.random.fold_in(arg_keys[2], 1), 0, 2).astype(jnp.int32)
    text_len = plant(jax.random.randint(arg_keys[3], (ITEMS,), TXT // 4, TXT + 1), jax.random.fold_in(arg_keys[3], 1), TXT // 4, TXT).astype(jnp.int32)
    t_mod = normal_values(arg_keys[4], (ITEMS, 6, D), 0.3, 1.75, (), jnp.float32)
    text_tokens = normal_values(arg_keys[5], (TXT, D), 1.0, 6.0, ((0, 4),))
    shift_table = jnp.clip(1.0 + 0.1 * jax.random.normal(arg_keys[6], (6, D), jnp.float32), 0.5, 1.5)
    w_qkv = normal_values(arg_keys[7], (D, 3, D), D ** -0.5, 0.1875, ((2, 4),))
    w_out = normal_values(arg_keys[8], (D, D), D ** -0.5, 0.1875, ((0, 4),))
    out_bias = normal_values(arg_keys[9], (D,), 0.3, 1.75, (), jnp.float32)
    w_xq = normal_values(arg_keys[10], (D, D), D ** -0.5, 0.1875, ((1, 4),))
    xq_bias = normal_values(arg_keys[11], (D,), 0.3, 1.75, ((0, 4),), jnp.float32)
    w_xkv = normal_values(arg_keys[12], (D, 2, D), D ** -0.5, 0.1875, ((2, 4),))
    xv_bias = normal_values(arg_keys[13], (D,), 0.1, 0.625, ((0, 4),), jnp.float32)
    w_xo = normal_values(arg_keys[14], (D, D), (max(2, D // 64)) ** -0.5, 1.5, ((0, 4),))
    xo_bias = normal_values(arg_keys[15], (D,), 0.3, 1.75, (), jnp.float32)
    w_in = normal_values(arg_keys[16], (D, 2, FF), D ** -0.5, 0.1875, ((2, 4),))
    in_bias = normal_values(arg_keys[17], (2, FF), 0.3, 1.75, ((1, 4),), jnp.float32)
    dw_weight = normal_values(arg_keys[18], (9, 2, FF), 9 ** -0.5, 2.0, ((2, 4),), jnp.float32)
    dw_bias = normal_values(arg_keys[19], (2, FF), 0.3, 1.75, ((1, 4),), jnp.float32)
    w_pt = normal_values(arg_keys[20], (FF, D), FF ** -0.5, 0.109375, ((0, 4),))
    return dict(tokens=tokens, cotangent=cotangent, item_bucket=item_bucket, text_len=text_len, t_mod=t_mod, text_tokens=text_tokens, shift_table=shift_table, w_qkv=w_qkv, w_out=w_out, out_bias=out_bias, w_xq=w_xq, xq_bias=xq_bias, w_xkv=w_xkv, xv_bias=xv_bias, w_xo=w_xo, xo_bias=xo_bias, w_in=w_in, in_bias=in_bias, dw_weight=dw_weight, dw_bias=dw_bias, w_pt=w_pt)


norm_eps = 1e-06
highest = lax.Precision.HIGHEST

@jax.custom_vjp
def low(v):
    return lax.optimization_barrier(v.astype(jnp.bfloat16)).astype(jnp.float32)

@jax.custom_vjp
def low_back(v):
    return v

def low_keep(v):
    return (low(v), None)

def low_pass(kept, grad):
    return (grad,)

def back_keep(v):
    return (v, None)

def back_low(kept, grad):
    return (low(grad),)
low.defvjp(low_keep, low_pass)
low_back.defvjp(back_keep, back_low)

def grid_table(bucket):
    grid_height = jnp.where(bucket == 0, SIDE, jnp.where(bucket == 1, 3 * SIDE // 4, 3 * SIDE // 2)).astype(jnp.int32)
    grid_width = jnp.where(bucket == 0, SIDE, jnp.where(bucket == 1, 5 * SIDE // 4, 5 * SIDE // 8)).astype(jnp.int32)
    return (grid_height, grid_width)

def inside_tap(inner_pos, grid_height, grid_width, row_step, col_step):
    grid_row = inner_pos // grid_width
    grid_col = inner_pos % grid_width
    return (inner_pos < grid_height * grid_width) & (grid_row + row_step >= 0) & (grid_row + row_step < grid_height) & (grid_col + col_step >= 0) & (grid_col + col_step < grid_width)

def layer_norm(values):
    centred = values - lax.optimization_barrier(jnp.mean(values, axis=-1, keepdims=True))
    return centred * lax.rsqrt(lax.optimization_barrier(jnp.mean(centred * centred, axis=-1, keepdims=True)) + norm_eps)

def depthwise(active, weight, bucket):
    grid_height, grid_width = grid_table(bucket)
    inner_pos = jnp.arange(ITEM_SLOTS, dtype=jnp.int32)
    padded = jnp.pad(active, ((HALO, HALO), (0, 0)))
    summed = jnp.zeros_like(active)
    for row_step in (-1, 0, 1):
        for col_step in (-1, 0, 1):
            begin = (HALO + row_step * grid_width + col_step).astype(jnp.int32)
            moved = lax.dynamic_slice_in_dim(padded, begin, ITEM_SLOTS, 0)
            inside = inside_tap(inner_pos, grid_height, grid_width, row_step, col_step)
            summed = summed + jnp.where(inside[:, None], moved, 0.0) * weight[3 * row_step + col_step + 4]
    return summed

def item_forward(x_item, item_mod, params, xkeys, xvals, bucket, length):
    shift_table, w_qkv, w_out, out_bias, w_xq, xq_bias, w_xo, xo_bias, w_in, in_bias, dw_weight, dw_bias, w_pt = params
    row_mod = shift_table + item_mod
    grid_height, grid_width = grid_table(bucket)
    live = (jnp.arange(ITEM_SLOTS, dtype=jnp.int32) < grid_height * grid_width).astype(jnp.float32)[:, None]
    normed = low(layer_norm(x_item) * (1.0 + row_mod[1]) + row_mod[0])
    qkv = low_back(jnp.einsum('nd,dke->nke', normed, w_qkv, precision=highest))
    query_h = low(jax.nn.softplus(qkv[:, 0])).reshape(ITEM_SLOTS, HEADS, HEAD)
    keys_h = low(jax.nn.softplus(qkv[:, 1])).reshape(ITEM_SLOTS, HEADS, HEAD)
    values_h = low(qkv[:, 2]).reshape(ITEM_SLOTS, HEADS, HEAD)
    keys_live = keys_h * live[:, :, None]
    kv_state = jnp.einsum('nhd,nhe->hde', keys_live, values_h, precision=highest)
    key_total = lax.optimization_barrier(jnp.sum(keys_live, axis=0))
    numerator = jnp.einsum('nhd,hde->nhe', query_h, kv_state, precision=highest)
    denominator = jnp.einsum('nhd,hd->nh', query_h, key_total, precision=highest)
    attn = low((numerator / denominator[:, :, None]).reshape(ITEM_SLOTS, D))
    attn_out = low_back(jnp.dot(attn, w_out, precision=highest)) + out_bias
    after_attn = x_item + live * row_mod[2] * attn_out
    cross_in = low(after_attn)
    xquery = low(low_back(jnp.dot(cross_in, w_xq, precision=highest)) + xq_bias).reshape(ITEM_SLOTS, XHEADS, XHEAD)
    raw_scores = low_back(jnp.einsum('nhd,thd->nht', xquery, xkeys, precision=highest)) * XHEAD ** (-0.5)
    key_live = jnp.arange(TXT, dtype=jnp.int32) < length
    raw_scores = jnp.where(key_live[None, None, :], raw_scores, -1e+30)
    attn_probs = low(jax.nn.softmax(raw_scores, axis=-1))
    cross_mix = low(low_back(jnp.einsum('nht,thd->nhd', attn_probs, xvals, precision=highest))).reshape(ITEM_SLOTS, D)
    cross_out = low_back(jnp.dot(cross_mix, w_xo, precision=highest)) + xo_bias
    after_cross = after_attn + live * cross_out
    normed_ffn = low(layer_norm(after_cross) * (1.0 + row_mod[4]) + row_mod[3])
    expand = low_back(jnp.einsum('nd,dkf->nkf', normed_ffn, w_in, precision=highest)) + in_bias
    active = low(jax.nn.silu(expand)).reshape(ITEM_SLOTS, 2 * FF)
    conv_out = low_back(depthwise(active, dw_weight.reshape(9, 2 * FF), bucket) + dw_bias.reshape(2 * FF))
    conv_out = conv_out.reshape(ITEM_SLOTS, 2, FF)
    glu_out = low(conv_out[:, 0] * jax.nn.silu(conv_out[:, 1]))
    ffn_out = low_back(jnp.dot(glu_out, w_pt, precision=highest))
    return after_cross + live * row_mod[5] * ffn_out

def reference(tokens, cotangent, item_bucket, text_len, t_mod, text_tokens, shift_table, w_qkv, w_out, out_bias, w_xq, xq_bias, w_xkv, xv_bias, w_xo, xo_bias, w_in, in_bias, dw_weight, dw_bias, w_pt):
    params = tuple((weight.astype(jnp.float32) for weight in (shift_table, w_qkv, w_out, out_bias, w_xq, xq_bias, w_xo, xo_bias, w_in, in_bias, dw_weight, dw_bias, w_pt)))

    def text_side(text_all, kv_weight, value_bias):
        both = low_back(jnp.einsum('td,dke->tke', text_all, kv_weight, precision=highest))
        keys_x = low(both[:, 0]).reshape(TXT, XHEADS, XHEAD)
        values_x = low(both[:, 1] + value_bias).reshape(TXT, XHEADS, XHEAD)
        return (keys_x, values_x)
    (xkeys, xvals), text_back = jax.vjp(text_side, text_tokens.astype(jnp.float32), w_xkv.astype(jnp.float32), xv_bias.astype(jnp.float32))
    inputs = (tokens.astype(jnp.float32).reshape(ITEMS, ITEM_SLOTS, D), cotangent.astype(jnp.float32).reshape(ITEMS, ITEM_SLOTS, D), t_mod.astype(jnp.float32), item_bucket, text_len)

    def one_item(totals, columns):
        x_item, cot_item, item_mod, bucket, length = columns

        def forward(x_arg, mod_arg, param_arg, key_arg, value_arg):
            return item_forward(x_arg, mod_arg, param_arg, key_arg, value_arg, bucket, length)
        result, pullback = jax.vjp(forward, x_item, item_mod, params, xkeys, xvals)
        d_x, d_mod, d_params, d_keys, d_vals = pullback(cot_item)
        totals = jax.tree.map(jnp.add, totals, (d_params, d_keys, d_vals))
        return (totals, (result.astype(jnp.bfloat16), d_x, d_mod))
    start_sums = jax.tree.map(jnp.zeros_like, (params, xkeys, xvals))
    (d_params, d_keys, d_vals), (outputs, d_tokens, d_tmod) = lax.scan(one_item, start_sums, inputs)
    d_text, d_w_xkv, d_xv_bias = text_back((d_keys, d_vals))
    return (outputs.reshape(ITEMS * ITEM_SLOTS, D), d_tokens.reshape(ITEMS * ITEM_SLOTS, D), d_tmod, d_text, d_params[0], d_params[1], d_params[2], d_params[3], d_params[4], d_params[5], d_w_xkv, d_xv_bias, d_params[6], d_params[7], d_params[8], d_params[9], d_params[10], d_params[11], d_params[12])
```

```python
import functools

import jax
import jax.numpy as jnp
from jax import lax
from jax.experimental import pallas as pl
from jax.experimental.pallas import tpu as pltpu
from jax.sharding import PartitionSpec as P

HEAD = 32
XHEAD = 72
XLANE = 128
TXT = 300
TXT_PAD = 384
SIDE = 32
ITEM_SLOTS = 1024
REACH = 48
BLOCK = 128

norm_eps = 1e-06
bfloat = jnp.bfloat16
single = jnp.float32
VMEM_BYTES = 60 * 1024 * 1024


def dot_nn(a, b):
    return lax.dot_general(a, b, (((1,), (0,)), ((), ())), preferred_element_type=single)


def dot_nt(a, b):
    return lax.dot_general(a, b, (((1,), (1,)), ((), ())), preferred_element_type=single)


def dot_tn(a, b):
    return lax.dot_general(a, b, (((0,), (0,)), ((), ())), preferred_element_type=single)


def swap(values, axis, bit):
    count = lax.axis_size(axis)
    return lax.ppermute(values, axis, [(i, i ^ bit) for i in range(count)])


def shift_devices(values, step):
    count = lax.axis_size("dp") * lax.axis_size("tensor")
    pairs = [(i, i + step) for i in range(count) if 0 <= i + step < count]
    return lax.ppermute(values, ("dp", "tensor"), pairs)


def bit_set(axis, bit):
    return (lax.axis_index(axis) // bit) % 2


def upper_bits():
    count = lax.axis_size("dp")
    bits = []
    bit = 2
    while bit < count:
        bits.append(bit)
        bit *= 2
    return bits


def turns(core):
    bits = upper_bits()
    cut = len(bits) // 2
    return bits[cut:] + bits[:cut] if core else bits


def turn_bit(number, sibling=False):
    core = lax.axis_index("dp") % 2
    first, second = turns(0)[number], turns(1)[number]
    return jnp.where(core == (1 if sibling else 0), first, second)


def swap_path(values, number):
    count = lax.axis_size("dp")
    return lax.ppermute(
        values, "dp", [(i, i ^ turns(i % 2)[number]) for i in range(count)]
    )


def turn_axes(values, place):
    count = len(upper_bits())
    axes = list(range(values.ndim))
    axes[place : place + count] = [place + turns(1).index(bit) for bit in turns(0)]
    return values.transpose(axes)


def own_turns(values, place, sibling=False):
    core = lax.axis_index("dp") % 2
    return jnp.where(core == (1 if sibling else 0), values, turn_axes(values, place))


def rank_of(step, parts):
    core = step % 2
    rank = jnp.bitwise_xor(lax.axis_index("dp"), core)
    for number in range(len(upper_bits())):
        if parts[number]:
            rank = jnp.bitwise_xor(rank, turn_bit(number, core == 1))
    return rank


def tie(*arrays):
    return lax.optimization_barrier(arrays)


def grow(values, axis, bit, place, absolute):
    other = swap(values, axis, bit)
    if absolute:
        high = bit_set(axis, bit) == 1
        return jnp.stack(
            [jnp.where(high, other, values), jnp.where(high, values, other)], axis=place
        )
    return jnp.stack([values, other], axis=place)


def grow_bits(values, axis, bits, absolute):
    have = []
    for bit in bits:
        values = grow(values, axis, bit, sum(h > bit for h in have), absolute)
        have.append(bit)
    return values


def total(terms):
    summed = terms[0].astype(single)
    for term in terms[1:]:
        summed = summed + term.astype(single)
    return summed.astype(bfloat)


def pick_at(terms, place, number):
    return [lax.index_in_dim(term, number, place, keepdims=False) for term in terms]


def gather_z(piece, absolute):
    return grow_bits(piece, "tensor", [2, 1], absolute)


def grow_path(values):
    for number in range(len(upper_bits())):
        values = jnp.stack([values, swap_path(values, number)])
    return values


def reduce_z(values):
    for bit, place in ((1, 1), (2, 0)):
        own = bit_set("tensor", bit)
        keep = lax.dynamic_index_in_dim(values, own, place, keepdims=False)
        send = lax.dynamic_index_in_dim(values, 1 - own, place, keepdims=False)
        values = total([keep, swap(send, "tensor", bit)])
    return values


def halve_path(terms, number, place):
    other = swap_path(total(pick_at(terms, place, 1)), number)
    return pick_at(terms, place, 0) + [other]


def halve_z(terms, place):
    for bit, spot in ((1, place + 1), (2, place)):
        other = swap(total(pick_at(terms, spot, 1)), "tensor", bit)
        terms = pick_at(terms, spot, 0) + [other]
    return total(terms)


def attention_rows(cols):
    rows = -(-3 * cols // lax.axis_size("dp"))
    return -(-rows // 16) * 16


def bits_of(number, count):
    return [(number >> place) % 2 for place in range(count)]


def row_cuts(rows, cols):
    return sorted({0, rows} | {end % rows for end in (cols, 2 * cols, 3 * cols)})


def assemble_kernel(ranks, group, rows, cols, own, first, second, *refs):
    *outs, out, sems, out_sems = refs
    me_z = lax.axis_index("tensor")
    cuts = row_cuts(rows, cols)
    count = len(upper_bits())
    copies = []

    def put(source, rank, peer, low, high):
        place = rank * rows + low
        kind = place // cols
        target = out.at[kind, peer, pl.ds(pl.multiple_of(place - kind * cols, 16), high - low)]
        copy = pltpu.make_async_copy(source, target, sems.at[len(copies)])
        copies.append((place < 3 * cols, copy))

    for low, high in zip(cuts[:-1], cuts[1:]):
        for rank in range(ranks):
            put(own.at[rank, low:high], rank, me_z, low, high)
        for step in range(ranks):
            source = (first, second)[step % 2]
            rank = rank_of(step, bits_of(step // 2, count))
            for peer in range(1, group):
                put(
                    source.at[step // 2, peer - 1, low:high],
                    rank,
                    jnp.bitwise_xor(me_z, peer),
                    low,
                    high,
                )
    for move in ("start", "wait"):
        for live, copy in copies:

            @pl.when(live)
            def _():
                getattr(copy, move)()

    stores = [
        pltpu.make_async_copy(out.at[kind], outs[kind], out_sems.at[kind]) for kind in range(3)
    ]
    for copy in stores:
        copy.start()
    for copy in stores:
        copy.wait()


def assemble(own, first, second, cols):
    ranks, rows, features = own.shape
    group = first.shape[1] + 1
    count = (len(row_cuts(rows, cols)) - 1) * ranks * group
    anywhere = pl.BlockSpec(memory_space=pl.ANY)
    return pl.pallas_call(
        functools.partial(assemble_kernel, ranks, group, rows, cols),
        in_specs=[anywhere] * 3,
        out_specs=[anywhere] * 3,
        out_shape=[jax.ShapeDtypeStruct((group, cols, features), own.dtype)] * 3,
        scratch_shapes=[
            pltpu.VMEM((3, group, cols, features), own.dtype),
            pltpu.SemaphoreType.DMA((count,)),
            pltpu.SemaphoreType.DMA((3,)),
        ],
        compiler_params=pltpu.CompilerParams(vmem_limit_bytes=VMEM_BYTES),
        cost_estimate=pl.CostEstimate(
            flops=0, bytes_accessed=4 * ranks * rows * group * features, transcendentals=0
        ),
    )(own, first, second)


def grads_kernel(ranks, group, rows, cols, pairs, *refs):
    inputs, (extra, keep, send, whole, sems) = refs[:-5], refs[-5:]
    me_z = lax.axis_index("tensor")
    count = len(upper_bits())
    for kind, (left, right) in enumerate(pairs):
        grad = dot_tn(inputs[left][...], inputs[right][...]).astype(bfloat)
        for peer in range(group):
            whole[peer, kind * cols : (kind + 1) * cols, :] = grad[peer * cols : (peer + 1) * cols]
    begin = len(pairs) * cols
    used = begin + extra.shape[1]
    for peer in range(group):
        whole[peer, begin:used, :] = extra[peer]
        if used < rows * ranks:
            whole[peer, used:, :] = jnp.zeros((rows * ranks - used, extra.shape[2]), bfloat)
    copies = []
    for step in range(ranks):
        parts = bits_of(step // 2, count)[::-1]
        place = pl.multiple_of(rank_of(step, parts) * rows, 16)
        for peer in range(group):
            source = whole.at[jnp.bitwise_xor(me_z, peer), pl.ds(place, rows)]
            target = (keep, send)[step % 2].at[step // 2, peer]
            copies.append(pltpu.make_async_copy(source, target, sems.at[len(copies)]))
    for copy in copies:
        copy.start()
    for copy in copies:
        copy.wait()


def grads_call(arrays, pairs, extra, rows, cols):
    ranks, group = lax.axis_size("dp"), lax.axis_size("tensor")
    features = extra.shape[-1]
    height = arrays[0].shape[0]
    inside = pl.BlockSpec(memory_space=pltpu.VMEM)
    anywhere = pl.BlockSpec(memory_space=pl.ANY)
    out = jax.ShapeDtypeStruct((ranks // 2, group, rows, features), bfloat)
    return pl.pallas_call(
        functools.partial(grads_kernel, ranks, group, rows, cols, pairs),
        in_specs=[inside] * (len(arrays) + 1),
        out_specs=[anywhere] * 2,
        out_shape=[out, out],
        scratch_shapes=[
            pltpu.VMEM((group, rows * ranks, features), bfloat),
            pltpu.SemaphoreType.DMA((ranks * group,)),
        ],
        compiler_params=pltpu.CompilerParams(vmem_limit_bytes=VMEM_BYTES),
        cost_estimate=pl.CostEstimate(
            flops=6 * height * features * features,
            bytes_accessed=2 * group * rows * ranks * features,
            transcendentals=0,
        ),
    )(*arrays, extra)


def core_terms(keep, send):
    shape = (2,) * (len(upper_bits()) + 2) + keep.shape[2:]
    return [keep.reshape(shape), swap(send, "dp", 1).reshape(shape)]


def flip_z(values, place):
    for number, bit in enumerate((2, 1)):
        values = jnp.where(
            bit_set("tensor", bit) == 1, jnp.flip(values, place + number), values
        )
    return values


def share_dp(piece):
    me_d = lax.axis_index("dp")
    shape = piece.shape
    count = len(upper_bits())
    for number in range(count):
        other = swap_path(piece, number)
        high = jnp.bitwise_and(me_d, turn_bit(number)) != 0
        piece = jnp.stack([jnp.where(high, other, piece), jnp.where(high, piece, other)])
    other = turn_axes(swap(piece, "dp", 1), 0)
    high = me_d % 2 == 1
    piece = jnp.stack([jnp.where(high, other, piece), jnp.where(high, piece, other)], axis=count)
    return own_turns(piece, 0).reshape((lax.axis_size("dp"),) + shape)


def flip_dp(values, place):
    ranks = lax.axis_size("dp")
    shape = values.shape
    bits = upper_bits() + [1]
    bits.sort(reverse=True)
    values = values.reshape(shape[:place] + (2,) * len(bits) + shape[place + 1 :])
    for number, bit in enumerate(bits):
        values = jnp.where(
            bit_set("dp", bit) == 1, jnp.flip(values, place + number), values
        )
    return values.reshape(shape[:place] + (ranks,) + shape[place + 1 :])


def grid_table(bucket):
    grid_height = jnp.where(
        bucket == 0, SIDE, jnp.where(bucket == 1, 3 * SIDE // 4, 3 * SIDE // 2)
    ).astype(jnp.int32)
    grid_width = jnp.where(
        bucket == 0, SIDE, jnp.where(bucket == 1, 5 * SIDE // 4, 5 * SIDE // 8)
    ).astype(jnp.int32)
    return (grid_height, grid_width)


def inside_tap(inner_pos, grid_height, grid_width, row_step, col_step):
    grid_row = inner_pos // grid_width
    grid_col = inner_pos % grid_width
    return (
        (inner_pos < grid_height * grid_width)
        & (grid_row + row_step >= 0)
        & (grid_row + row_step < grid_height)
        & (grid_col + col_step >= 0)
        & (grid_col + col_step < grid_width)
    )


def look_up(table, item):
    known = item[:, None] == jnp.arange(table.shape[0], dtype=jnp.int32)[None, :]
    return jnp.sum(jnp.where(known, table[None, :], 0), axis=1)


def shift_blocks(slots, total, item_bucket, sign, limit):
    item = slots // ITEM_SLOTS
    inner = slots % ITEM_SLOTS
    height, width = grid_table(look_up(item_bucket, item))
    index = jnp.arange(slots.shape[0], dtype=jnp.int32)
    known = (slots >= 0) & (slots < total) & (index < limit)
    columns = jnp.arange(BLOCK + 2 * REACH, dtype=jnp.int32)
    taps = []
    for row_step in (-1, 0, 1):
        for col_step in (-1, 0, 1):
            down, right = sign * row_step, sign * col_step
            inside = known & inside_tap(inner, height, width, down, right)
            target = index % BLOCK + REACH + down * width + right
            taps.append(
                (columns[None, :] == target[:, None]) & inside[:, None]
            )
    return jnp.stack(taps, axis=0).astype(bfloat)


def fetch_weights(core, sources, held, sems):
    own, others = sources
    rows = held.shape[-2]
    chunks = []
    for chunk in range(4):
        first, second = chunk // 2, chunk % 2
        slot = chunk % 2
        rank = rank_of(core, (first, second))
        place = pl.multiple_of(rank * rows, 16)
        copies = []
        for kind in range(3):
            target = held.at[slot, kind]
            copies.append((own.at[kind, pl.ds(place, rows)], target.at[0]))
            copies.append(
                (others.at[first + 2 * second, :, kind * rows : (kind + 1) * rows], target.at[1:4])
            )
        chunks.append(
            [
                pltpu.make_async_copy(source, target, sems.at[slot, number])
                for number, (source, target) in enumerate(copies)
            ]
        )
    for chunk in range(4):

        @pl.when(pl.program_id(0) == chunk)
        def _():
            if chunk == 0:
                for copy in chunks[0]:
                    copy.start()
            if chunk < 3:
                for copy in chunks[chunk + 1]:
                    copy.start()
            for copy in chunks[chunk]:
                copy.wait()


def ffn_kernel(
    core,
    own_rows,
    own_pad,
    normed_ref,
    grad_ref,
    reach_ref,
    back_ref,
    last_ref,
    small_ref,
    *refs,
):
    count = 2 if core is not None else 1
    sources = refs[:count]
    ffn_ref, dnormed_ref, dweight_ref, dsmall_ref = refs[count : count + 4]
    active, slope, dconv, glu, dexpand, *buffers = refs[count + 4 :]
    if core is None:
        weight = lambda kind: sources[0][0, kind]
    else:
        held, sems = buffers
        fetch_weights(core, sources, held, sems)
        slot = lax.rem(pl.program_id(0), 2)
        weight = lambda kind: held[slot, kind].reshape(-1, held.shape[-1])
    @pl.when(pl.program_id(0) == 0)
    def _():
        ffn_ref[...] = jnp.zeros_like(ffn_ref)
        dnormed_ref[...] = jnp.zeros_like(dnormed_ref)

    normed = normed_ref[...]
    channels = small_ref.shape[2]
    for half in range(2):
        expand = dot_nt(normed, weight(half)) + small_ref[half, 10:11, :]
        sig = jax.nn.sigmoid(expand)
        active[half] = (expand * sig).astype(bfloat)
        mid, sig_mid = expand[2 * REACH : 2 * REACH + own_pad], sig[2 * REACH : 2 * REACH + own_pad]
        slope[half] = sig_mid * (1.0 + mid * (1.0 - sig_mid))
    dglu = dot_nt(grad_ref[...], weight(2))
    blocks = grad_ref.shape[0] // BLOCK
    for block in range(blocks):
        begin = block * BLOCK
        convs = []
        for half in range(2):
            moved = dot_nn(
                reach_ref[block], active[half, begin : begin + BLOCK + 2 * REACH, :]
            )
            total = small_ref[half, 9:10, :]
            for tap in range(9):
                total = total + moved[tap * BLOCK : (tap + 1) * BLOCK] * small_ref[half, tap : tap + 1, :]
            convs.append(total)
        value, gate = convs
        sig = jax.nn.sigmoid(gate)
        act = gate * sig
        grad = dglu[begin : begin + BLOCK]
        glu[begin : begin + BLOCK, :] = (value * act).astype(bfloat)
        dconv[0, begin : begin + BLOCK, :] = (grad * act).astype(bfloat)
        dconv[1, begin : begin + BLOCK, :] = (
            grad * value * (sig * (1.0 + gate * (1.0 - sig)))
        ).astype(bfloat)

    glu_own = glu[REACH : REACH + own_pad, :]
    if own_rows != own_pad:
        here = lax.broadcasted_iota(jnp.int32, (own_pad, channels), 0) < own_rows
        glu_own = jnp.where(here, glu_own.astype(single), 0.0).astype(bfloat)
    grad_own = grad_ref[REACH : REACH + own_pad, :]
    ffn_ref[...] += dot_nn(glu_own, weight(2))
    dweight_ref[0, 2] = dot_tn(glu_own, grad_own).astype(bfloat)
    normed_own = normed_ref[2 * REACH : 2 * REACH + own_pad, :]
    for half in range(2):
        dconv_own = dconv[half, REACH : REACH + own_pad, :].astype(single)
        if own_rows != own_pad:
            dconv_own = jnp.where(here, dconv_own, 0.0)
        dsmall_ref[half, 9:10, :] = jnp.sum(dconv_own, axis=0, keepdims=True)
        sums = [jnp.zeros((8, channels), single) for _ in range(9)]
        dbias = jnp.zeros((8, channels), single)
        for block in range(pl.cdiv(own_pad, BLOCK)):
            begin = block * BLOCK
            height = min(BLOCK, own_pad - begin)
            picks = back_ref[block] if height == BLOCK else last_ref[...]
            moved = dot_nn(picks, dconv[half, begin : begin + height + 2 * REACH, :])
            here_active = active[half, 2 * REACH + begin : 2 * REACH + begin + height, :].astype(single)
            total = jnp.zeros((height, channels), single)
            for tap in range(9):
                part = moved[tap * height : (tap + 1) * height]
                total = total + part * small_ref[half, tap : tap + 1, :]
                sums[tap] = sums[tap] + jnp.sum(
                    (part * here_active).reshape(height // 8, 8, channels), axis=0
                )
            grad = total * slope[half, begin : begin + height, :]
            dbias = dbias + jnp.sum(grad.reshape(height // 8, 8, channels), axis=0)
            dexpand[half, begin : begin + height, :] = grad.astype(bfloat)
        for tap in range(9):
            dsmall_ref[half, tap : tap + 1, :] = jnp.sum(sums[tap], axis=0, keepdims=True)
        dsmall_ref[half, 10:11, :] = jnp.sum(dbias, axis=0, keepdims=True)
        dsmall_ref[half, 11:16, :] = jnp.zeros((5, channels), single)
    for half in range(2):
        grad = dexpand[half]
        dnormed_ref[...] += dot_nn(grad, weight(half))
        dweight_ref[0, half] = dot_tn(grad, normed_own).astype(bfloat)


def ffn_call(core, own_rows, own_pad, normed, grad, reach, back, last, weights, small):
    wide, features = normed.shape
    tall = grad.shape[0]
    count = small.shape[2]
    steps = 4
    channels = count // steps
    direct = len(weights) > 1
    whole = lambda array: pl.BlockSpec(array.shape, lambda i: (0,) * array.ndim)
    rows = pl.BlockSpec((1, 3, channels, features), lambda i: (i, 0, 0, 0))
    tiny = pl.BlockSpec((2, 16, channels), lambda i: (0, 0, i))
    held = pl.BlockSpec((own_pad, features), lambda i: (0, 0))
    flops = 2 * count * features * (2 * wide + tall + 6 * own_pad) + 2 * count * 9 * 256 * 2 * (
        tall + own_pad
    )
    scratch = [
        pltpu.VMEM((2, wide, channels), bfloat),
        pltpu.VMEM((2, own_pad, channels), single),
        pltpu.VMEM((2, tall, channels), bfloat),
        pltpu.VMEM((tall, channels), bfloat),
        pltpu.VMEM((2, own_pad, channels), bfloat),
    ]
    if direct:
        group = weights[1].shape[1] + 1
        piece = weights[1].shape[2] // 3
        scratch += [
            pltpu.VMEM((2, 3, group, piece, features), bfloat),
            pltpu.SemaphoreType.DMA((2, 6)),
        ]
    return pl.pallas_call(
        functools.partial(ffn_kernel, core if direct else None, own_rows, own_pad),
        grid=(steps,),
        in_specs=[whole(normed), whole(grad), whole(reach), whole(back), whole(last), tiny]
        + ([pl.BlockSpec(memory_space=pl.ANY)] * 2 if direct else [rows]),
        out_specs=[held, held, rows, tiny],
        out_shape=[
            jax.ShapeDtypeStruct((own_pad, features), single),
            jax.ShapeDtypeStruct((own_pad, features), single),
            jax.ShapeDtypeStruct((steps, 3, channels, features), bfloat),
            jax.ShapeDtypeStruct((2, 16, count), single),
        ],
        scratch_shapes=scratch,
        compiler_params=pltpu.CompilerParams(vmem_limit_bytes=VMEM_BYTES),
        cost_estimate=pl.CostEstimate(
            flops=flops, bytes_accessed=12 * count * features, transcendentals=2 * count * tall
        ),
    )(normed, grad, reach, back, last, small, *weights)


def head_probs(query, keys, lengths):
    scores = dot_nt(query, keys) * (XHEAD ** (-0.5))
    place = lax.broadcasted_iota(jnp.int32, scores.shape, 1)
    live = place < lengths
    scores = jnp.where(live, scores, -1e30)
    top = jnp.max(scores, axis=-1, keepdims=True)
    powers = jnp.exp(scores - top)
    return powers / jnp.sum(powers, axis=-1, keepdims=True)


def cross_kernel(query_ref, keys_ref, vals_ref, length_ref, mix_ref):
    probs = head_probs(query_ref[...], keys_ref[0], length_ref[...])
    mix_ref[...] = dot_nn(probs.astype(bfloat), vals_ref[0]).astype(bfloat)


def cross_back_kernel(
    query_ref, keys_ref, vals_ref, length_ref, dmix_ref, dquery_ref, dkeys_ref, dvals_ref, dbias_ref
):
    query, keys, dmix = query_ref[...], keys_ref[0], dmix_ref[...]
    probs = head_probs(query, keys, length_ref[...])
    dprobs = dot_nt(dmix, vals_ref[0])
    dvals_ref[0] = dot_tn(dmix, probs.astype(bfloat))[:XHEAD].astype(bfloat)
    row_dot = jnp.sum(probs * dprobs, axis=-1, keepdims=True)
    dscores = (probs * (dprobs - row_dot) * (XHEAD ** (-0.5))).astype(bfloat)
    dquery = dot_nn(dscores, keys)
    dbias_ref[...] = jnp.sum(dquery, axis=0, keepdims=True)
    dquery_ref[...] = dquery.astype(bfloat)
    dkeys_ref[0] = dot_tn(query, dscores)[:XHEAD].astype(bfloat)


def cross_specs(rows):
    lane = pl.BlockSpec((rows, XLANE), lambda h: (0, h))
    text = pl.BlockSpec((1, TXT_PAD, XLANE), lambda h: (h, 0, 0))
    length = pl.BlockSpec((rows, 1), lambda h: (0, 0))
    return lane, text, length


def cross_call(query, keys, vals, lengths):
    rows, heads = query.shape[0], keys.shape[0]
    lane, text, length = cross_specs(rows)
    return pl.pallas_call(
        cross_kernel,
        grid=(heads,),
        in_specs=[lane, text, text, length],
        out_specs=lane,
        out_shape=jax.ShapeDtypeStruct((rows, heads * XLANE), bfloat),
        compiler_params=pltpu.CompilerParams(vmem_limit_bytes=VMEM_BYTES),
        cost_estimate=pl.CostEstimate(
            flops=4 * heads * rows * TXT_PAD * XLANE,
            bytes_accessed=8 * rows * heads * XLANE,
            transcendentals=heads * rows * TXT_PAD,
        ),
    )(query, keys, vals, lengths)


def cross_back_call(query, keys, vals, lengths, dmix):
    rows, heads = query.shape[0], keys.shape[0]
    lane, text, length = cross_specs(rows)
    return pl.pallas_call(
        cross_back_kernel,
        grid=(heads,),
        in_specs=[lane, text, text, length, lane],
        out_specs=[
            lane,
            pl.BlockSpec((1, XHEAD, TXT_PAD), lambda h: (h, 0, 0)),
            pl.BlockSpec((1, XHEAD, TXT_PAD), lambda h: (h, 0, 0)),
            pl.BlockSpec((1, XLANE), lambda h: (0, h)),
        ],
        out_shape=[
            jax.ShapeDtypeStruct((rows, heads * XLANE), bfloat),
            jax.ShapeDtypeStruct((heads, XHEAD, TXT_PAD), bfloat),
            jax.ShapeDtypeStruct((heads, XHEAD, TXT_PAD), bfloat),
            jax.ShapeDtypeStruct((1, heads * XLANE), single),
        ],
        compiler_params=pltpu.CompilerParams(vmem_limit_bytes=VMEM_BYTES),
        cost_estimate=pl.CostEstimate(
            flops=12 * heads * rows * TXT_PAD * XLANE,
            bytes_accessed=12 * rows * heads * XLANE,
            transcendentals=heads * rows * TXT_PAD,
        ),
    )(query, keys, vals, lengths, dmix)


def norm_parts(values):
    centred = values - jnp.mean(values, axis=-1, keepdims=True)
    inv_std = lax.rsqrt(jnp.mean(centred * centred, axis=-1, keepdims=True) + norm_eps)
    return (centred * inv_std, inv_std)


def norm_back(grad_in, normal, inv_std, scale):
    scaled = grad_in * (1.0 + scale)
    return (
        scaled
        - jnp.mean(scaled, axis=-1, keepdims=True)
        - normal * jnp.mean(scaled * normal, axis=-1, keepdims=True)
    ) * inv_std


def pad_rows(values, rows):
    return jnp.pad(values, ((0, rows - values.shape[0]),) + ((0, 0),) * (values.ndim - 1))


def pad_heads(rows, heads):
    features = rows.shape[1]
    shaped = rows.reshape(heads, XHEAD, features)
    return jnp.pad(shaped, ((0, 0), (0, XLANE - XHEAD), (0, 0))).reshape(heads * XLANE, features)


def drop_lanes(values, heads):
    return values.reshape(-1, heads, XLANE)[:, :, :XHEAD].reshape(-1, heads * XHEAD)


def local(
    tokens,
    cotangent,
    item_bucket,
    text_len,
    t_mod,
    text_tokens,
    shift_table,
    w_qkv,
    w_out,
    out_bias,
    w_xq,
    xq_bias,
    w_xkv,
    xv_bias,
    w_xo,
    xo_bias,
    w_in,
    in_bias,
    dw_weight,
    dw_bias,
    w_pt,
):
    group = lax.axis_size("tensor")
    ranks = lax.axis_size("dp")
    me_z = lax.axis_index("tensor")
    me_d = lax.axis_index("dp")
    own_rows, width = tokens.shape
    own_pad = -(-own_rows // 32) * 32
    tall = -(-(own_rows + 2 * REACH) // BLOCK) * BLOCK
    wide = tall + 2 * REACH
    total_rows = own_rows * group * ranks
    item_count = t_mod.shape[0]
    heads = width // HEAD
    xheads = width // XHEAD
    cols = w_xq.shape[1]
    channels = w_in.shape[2]
    padded_channels = -(-channels // 384) * 384
    own_start = (me_d * group + me_z) * own_rows
    first_item = own_start // ITEM_SLOTS
    last_item = (own_start + own_rows - 1) // ITEM_SLOTS
    two_items = last_item != first_item

    bits = upper_bits()
    att_piece = attention_rows(cols)
    att_pad = att_piece * ranks
    att_rows = 3 * cols
    rows_qkv = pad_rows(w_qkv.transpose(1, 2, 0).reshape(att_rows, width), att_pad)
    rows_mix = pad_rows(jnp.concatenate([w_out, w_xq.T, w_xo], axis=0), att_pad)
    ffn_piece = padded_channels // ranks
    half_count = padded_channels * group // 2
    rows_ffn = jnp.stack(
        [pad_rows(rows, padded_channels) for rows in (w_in[:, 0].T, w_in[:, 1].T, w_pt)]
    )
    own_qkv = rows_qkv.reshape(ranks, att_piece, width)
    own_mix = rows_mix.reshape(ranks, att_piece, width)
    piece_1 = lax.dynamic_index_in_dim(own_qkv, me_d, 0, keepdims=False)
    piece_2 = lax.dynamic_index_in_dim(own_mix, me_d, 0, keepdims=False)
    piece_3 = lax.dynamic_slice_in_dim(rows_ffn, me_d * ffn_piece, ffn_piece, 1)
    piece_3 = piece_3.reshape(3 * ffn_piece, width)

    def near_z(piece, far):
        near = swap(jnp.stack([piece, far]), "tensor", 1)
        return jnp.stack([near[0], far, near[1]])

    def turn(values, number):
        return jnp.stack([values, swap_path(values, number)])

    def rest_turns(values):
        for number in range(1, len(bits)):
            values = turn(values, number)
        return values.reshape((-1,) + values.shape[-3:])

    wave_1 = near_z(piece_1, swap(piece_1, "tensor", 2))
    piece_2, wave_1 = tie(piece_2, wave_1)
    far_2 = swap(piece_2, "tensor", 2)
    wave_1 = turn(wave_1, 0)
    far_2, wave_1 = tie(far_2, wave_1)
    wave_1 = rest_turns(wave_1)
    wave_2 = near_z(piece_2, far_2)
    wave_1, wave_2, piece_3, text_tokens = tie(wave_1, wave_2, piece_3, text_tokens)
    other_1 = swap(wave_1, "dp", 1)
    wave_2 = turn(wave_2, 0)
    far_3 = swap(piece_3, "tensor", 2)
    text_all = gather_z(text_tokens, True).reshape(TXT, width)
    wave_2, other_1 = tie(wave_2, other_1)
    wave_2 = rest_turns(wave_2)
    far_3, wave_2 = tie(far_3, wave_2)
    wave_3 = near_z(piece_3, far_3)
    other_2 = swap(wave_2, "dp", 1)
    wave_3, other_2 = tie(wave_3, other_2)
    wave_3 = turn(wave_3, 0)
    wave_3 = rest_turns(wave_3)
    other_3 = swap(wave_3, "dp", 1)

    wq, wk, wv = [
        part.reshape(width, width) for part in assemble(own_qkv, wave_1, other_1, cols)
    ]
    wo, wxq, wxo = [
        part.reshape(width, width) for part in assemble(own_mix, wave_2, other_2, cols)
    ]
    wxq_pad = pad_heads(wxq, xheads)
    wxo_pad = pad_heads(wxo, xheads)

    def ffn_half(core):
        count = len(bits)
        own = flip_dp(rows_ffn.reshape(3, ranks, ffn_piece, width), 1)
        own = own.reshape((3,) + (2,) * (count + 1) + (ffn_piece, width))
        own = jnp.moveaxis(lax.index_in_dim(own, core, count + 1, keepdims=False), 0, count)
        own = own_turns(own.transpose(tuple(range(count))[::-1] + (count, count + 1, count + 2)), 0, core == 1)
        others = (wave_3, other_3)[core]
        others = others.reshape((2,) * count + (group - 1, 3, ffn_piece, width))
        others = others.transpose(tuple(range(count))[::-1] + tuple(range(count, count + 4)))
        joined = jnp.concatenate([jnp.expand_dims(own, count), others], axis=count)
        joined = jnp.moveaxis(joined, count + 1, 2)
        return joined.reshape(4, 3, half_count // 4, width)

    direct = ffn_piece % 16 == 0 and len(bits) == 2
    weights_ffn = [
        [rows_ffn, (wave_3, other_3)[core]] if direct else [ffn_half(core)] for core in (0, 1)
    ]

    text_kv = jnp.einsum("td,dke->tke", text_all, w_xkv, preferred_element_type=single)
    xkv_own = jnp.stack([text_kv[:, 0], text_kv[:, 1] + xv_bias], axis=0).astype(bfloat)
    xkv_all = gather_z(xkv_own, True).reshape(group, 2, TXT, cols // XHEAD, XHEAD)
    xkv_all = xkv_all.transpose(1, 0, 3, 2, 4).reshape(2, xheads, TXT, XHEAD)
    xkv_all = jnp.pad(xkv_all, ((0, 0), (0, 0), (0, TXT_PAD - TXT), (0, XLANE - XHEAD)))
    xkeys, xvals = xkv_all[0], xkv_all[1]

    small = jnp.concatenate([dw_weight, dw_bias[None], in_bias[None]], axis=0)
    small = jnp.pad(small, ((0, 5), (0, 0), (0, padded_channels - channels)))
    small = flip_dp(small.reshape(16, 2, ranks, ffn_piece), 2)
    sizes = small.size
    small = jnp.concatenate([small.reshape(-1), xq_bias])
    small, other_1 = tie(small, other_1)
    small = gather_z(small, False).reshape(group, -1)
    xq_rel = small[:, sizes:]
    small = small[:, :sizes].reshape((group, 16, 2) + (2,) * (len(bits) + 1) + (ffn_piece,))
    small = jnp.moveaxis(small, 0, len(bits) + 3)
    down = tuple(range(2, 2 + len(bits)))
    small = small.transpose((len(bits) + 2, 1, 0) + down[::-1] + (len(bits) + 3, len(bits) + 4))
    small = [
        own_turns(small[core], 2, core == 1).reshape(2, 16, half_count) for core in (0, 1)
    ]
    xq_bias_all = jnp.stack(
        [lax.dynamic_index_in_dim(xq_rel, me_z ^ peer, 0, keepdims=False) for peer in range(group)]
    ).reshape(xheads, XHEAD)
    xq_bias_all = jnp.pad(xq_bias_all, ((0, 0), (0, XLANE - XHEAD))).reshape(xheads * XLANE)

    slots = own_start + jnp.arange(own_rows, dtype=jnp.int32)
    item = slots // ITEM_SLOTS
    inner = slots % ITEM_SLOTS
    bucket = look_up(item_bucket, item)
    grid_h, grid_w = grid_table(bucket)
    valid = inner < grid_h * grid_w
    live = valid.astype(single)[:, None]
    lengths = look_up(text_len, item)[:, None]
    in_first = (item == first_item)[:, None]
    in_second = jnp.logical_not(in_first)
    mod_first = shift_table + lax.dynamic_index_in_dim(t_mod, first_item, 0, keepdims=False)
    mod_second = shift_table + lax.dynamic_index_in_dim(t_mod, last_item, 0, keepdims=False)
    row_mod = lambda number: jnp.where(in_first, mod_first[number][None], mod_second[number][None])
    shift_a, scale_a, gate_a, shift_f, scale_f, gate_f = [row_mod(number) for number in range(6)]
    tokens_f = tokens.astype(single)
    grad_out = cotangent.astype(single)

    tall_slots = own_start - REACH + jnp.arange(tall, dtype=jnp.int32)
    reach = shift_blocks(tall_slots, total_rows, item_bucket, 1, tall)
    reach = reach.reshape(9, tall // BLOCK, BLOCK, -1).transpose(1, 0, 2, 3)
    reach = reach.reshape(tall // BLOCK, 9 * BLOCK, -1)
    pad_slots = own_start + jnp.arange(own_pad, dtype=jnp.int32)
    back = shift_blocks(pad_slots, total_rows, item_bucket, -1, own_rows)
    full_blocks = own_pad // BLOCK
    rest = own_pad - full_blocks * BLOCK
    back_full = back[:, : full_blocks * BLOCK].reshape(9, full_blocks, BLOCK, -1).transpose(1, 0, 2, 3)
    back_full = back_full.reshape(full_blocks, 9 * BLOCK, -1)
    rest = max(rest, 32)
    back_last = back[:, own_pad - rest :, : rest + 2 * REACH].reshape(9 * rest, -1)

    d_ffn = (grad_out * live * gate_f).astype(bfloat)
    above = shift_devices(d_ffn[own_rows - REACH :], 1)
    below = shift_devices(d_ffn[:REACH], -1)
    d_ffn_ext = pad_rows(jnp.concatenate([above, d_ffn, below], axis=0), tall)

    normal_a, inv_std_a = norm_parts(tokens_f)
    normed = (normal_a * (1.0 + scale_a) + shift_a).astype(bfloat)
    pre_q = dot_nt(normed, wq)
    pre_k = dot_nt(normed, wk)
    query = jax.nn.softplus(pre_q).astype(bfloat)
    keys = jax.nn.softplus(pre_k).astype(bfloat)
    values = dot_nt(normed, wv).astype(bfloat)
    lane = jnp.arange(width, dtype=jnp.int32) // HEAD
    same_head = lane[:, None] == lane[None, :]
    head_ones = same_head.astype(bfloat)
    zero = jnp.zeros((), bfloat)
    first_live = in_first & valid[:, None]
    second_live = in_second & valid[:, None]

    def packed(left, right, extra):
        full = jnp.where(same_head, dot_tn(left, right), 0.0)
        block = jnp.sum(full.reshape(heads, HEAD, width), axis=0)
        return jnp.concatenate([block, extra[None]], axis=0)

    def unpacked(block):
        return jnp.where(same_head, jnp.tile(block[:HEAD].astype(bfloat), (heads, 1)), zero)

    span_rows = own_rows * group
    span_start = me_d * span_rows
    span_first = span_start // ITEM_SLOTS
    span_last = (span_start + span_rows - 1) // ITEM_SLOTS
    span_items = (span_rows - 2) // ITEM_SLOTS + 2

    def over_items(first_part, second_part):
        parts = []
        for number in range(span_items):
            chosen = jnp.where(first_item - span_first == number, first_part, 0.0)
            also = two_items & (last_item - span_first == number)
            parts.append(chosen + jnp.where(also, second_part, 0.0))
        table = jnp.stack(parts)
        for bit in (1, 2):
            table = table + swap(table.astype(bfloat), "tensor", bit).astype(single)
        count = ranks - 1
        head_part = table[0].astype(bfloat)
        tail_part = lax.dynamic_index_in_dim(table, span_last - span_first, 0, keepdims=False)
        below = lax.ppermute(tail_part.astype(bfloat), "dp", [(i, i + 1) for i in range(count)])
        above = lax.ppermute(head_part, "dp", [(i + 1, i) for i in range(count)])
        below_same = (span_start - 1) // ITEM_SLOTS == span_first
        above_same = (span_start + span_rows) // ITEM_SLOTS == span_last
        sums = []
        for number in (first_item, last_item):
            part = lax.dynamic_index_in_dim(table, number - span_first, 0, keepdims=False)
            part = part + jnp.where(below_same & (number == span_first), below.astype(single), 0.0)
            part = part + jnp.where(above_same & (number == span_last), above.astype(single), 0.0)
            sums.append(part)
        return sums

    keys_1 = jnp.where(first_live, keys, zero)
    keys_2 = jnp.where(second_live, keys, zero)
    state_1, state_2 = over_items(
        packed(keys_1, values, jnp.sum(keys_1, axis=0, dtype=single)),
        packed(keys_2, values, jnp.sum(keys_2, axis=0, dtype=single)),
    )
    dense_1, dense_2 = unpacked(state_1), unpacked(state_2)
    total_row = jnp.where(in_first, state_1[HEAD][None], state_2[HEAD][None])
    query_1 = jnp.where(in_first, query, zero)
    query_2 = jnp.where(in_second, query, zero)
    numerator = dot_nn(query_1, dense_1) + dot_nn(query_2, dense_2)
    denominator = dot_nn((query.astype(single) * total_row).astype(bfloat), head_ones)
    attn_ratio = numerator / denominator
    attn = attn_ratio.astype(bfloat)
    attn_out = dot_nn(attn, wo) + out_bias
    after_attn = tokens_f + live * gate_a * attn_out

    cross_in = after_attn.astype(bfloat)
    xquery = (dot_nt(cross_in, wxq_pad) + xq_bias_all).astype(bfloat)
    cross_mix = cross_call(xquery, xkeys, xvals, lengths)
    cross_out = dot_nn(cross_mix, wxo_pad) + xo_bias
    after_cross = after_attn + live * cross_out

    normal_f, inv_std_f = norm_parts(after_cross)
    normed_ffn = (normal_f * (1.0 + scale_f) + shift_f).astype(bfloat)
    above = shift_devices(normed_ffn[own_rows - 2 * REACH :], 1)
    below = shift_devices(normed_ffn[: 2 * REACH], -1)
    normed_ext = pad_rows(jnp.concatenate([above, normed_ffn, below], axis=0), wide)
    tables = (reach, back_full, back_last)
    part_1 = ffn_call(
        1, own_rows, own_pad, normed_ext, d_ffn_ext, *tables, weights_ffn[1], small[1]
    )
    normed_ext, *part_1 = tie(normed_ext, *part_1)
    part_0 = ffn_call(
        0, own_rows, own_pad, normed_ext, d_ffn_ext, *tables, weights_ffn[0], small[0]
    )
    ffn_out = (part_0[0] + part_1[0])[:own_rows]
    d_normed_ffn = (part_0[1] + part_1[1])[:own_rows]
    ffn_other = swap(part_1[2], "dp", 1)
    d_normed_ffn, ffn_other = tie(d_normed_ffn, ffn_other)
    ffn_shape = (2, 2, 3) + (2,) * len(bits) + (ffn_piece, width)
    ffn_terms = [part_0[2].reshape(ffn_shape), ffn_other.reshape(ffn_shape)]
    ffn_terms = halve_path(ffn_terms, 0, 0)

    d_small = jnp.stack(
        [
            own_turns(
                part[3].astype(bfloat).reshape((2, 16) + (2,) * (len(bits) + 2) + (ffn_piece,)),
                2,
                core == 1,
            )
            for core, part in ((0, part_0), (1, part_1))
        ],
        axis=len(bits) + 2,
    )
    order = (len(bits) + 3, len(bits) + 4, 0, 1) + down[::-1] + (len(bits) + 2, len(bits) + 5)
    d_small = flip_z(d_small.transpose(order), 0)
    d_small = d_small.reshape(group, 2, 16, ranks, ffn_piece)[:, :, :11]
    d_small = flip_dp(d_small, 3).reshape(group, -1)
    small_rows = -(-d_small.shape[1] // (16 * width)) * 16
    d_small = jnp.pad(d_small, ((0, 0), (0, small_rows * width - d_small.shape[1])))
    d_small = d_small.reshape(group, small_rows, width)

    out_tokens = (after_cross + live * gate_f * ffn_out).astype(bfloat)
    d_gate_f = grad_out * live * ffn_out
    grad_cross = grad_out + norm_back(d_normed_ffn, normal_f, inv_std_f, scale_f)

    d_cross = grad_cross * live
    d_xo_bias = jnp.sum(d_cross, axis=0)
    d_cross_low = d_cross.astype(bfloat)
    d_mix = dot_nt(d_cross_low, wxo_pad).astype(bfloat)
    d_query_low, d_keys, d_vals, d_xq_part = cross_back_call(xquery, xkeys, xvals, lengths, d_mix)
    grad_attn = grad_cross + dot_nn(d_query_low, wxq_pad)
    grad_attn, ffn_terms[-1] = tie(grad_attn, ffn_terms[-1])
    for stage in range(1, len(bits)):
        ffn_terms = halve_path(ffn_terms, stage, 0 if stage == 1 else 1)

    d_attn_out = grad_attn * live * gate_a
    d_gate_a = grad_attn * live * attn_out
    d_out_bias = jnp.sum(d_attn_out, axis=0)
    d_attn_low = d_attn_out.astype(bfloat)
    d_ratio = dot_nt(d_attn_low, wo)

    text_rows = 2 * cols * TXT_PAD // width
    mix_rows = -(-(att_rows + text_rows + small_rows) // (16 * ranks)) * 16
    lanes = width // TXT_PAD
    d_kv = jnp.concatenate(
        [d_keys.reshape(group, cols, TXT_PAD), d_vals.reshape(group, cols, TXT_PAD)], axis=1
    )
    d_kv = jnp.concatenate(
        [d_kv[:, number * text_rows : (number + 1) * text_rows] for number in range(lanes)], axis=2
    )
    mix_grads = grads_call(
        [attn, d_attn_low, drop_lanes(d_query_low, xheads), cross_in, drop_lanes(cross_mix, xheads), d_cross_low],
        ((0, 1), (2, 3), (4, 5)),
        jnp.concatenate([d_kv, d_small], axis=1),
        mix_rows,
        cols,
    )
    mix_terms = core_terms(*mix_grads)
    d_numer = (d_ratio / denominator).astype(bfloat)
    d_denom = -dot_nn((d_ratio * attn_ratio).astype(bfloat), head_ones) / denominator
    d_numer_1 = jnp.where(in_first, d_numer, zero)
    d_numer_2 = jnp.where(in_second, d_numer, zero)
    query_f = query.astype(single)
    weighted = query_f * d_denom
    d_state_1, d_state_2 = over_items(
        packed(query, d_numer_1, jnp.sum(jnp.where(in_first, weighted, 0.0), axis=0)),
        packed(query, d_numer_2, jnp.sum(jnp.where(in_second, weighted, 0.0), axis=0)),
    )
    d_state_1, d_state_2, ffn_terms[-1], mix_terms[1] = tie(
        d_state_1, d_state_2, ffn_terms[-1], mix_terms[1]
    )
    for stage in range(len(bits)):
        mix_terms = halve_path(mix_terms, stage, 0)
    d_query = dot_nt(d_numer_1, dense_1) + dot_nt(d_numer_2, dense_2) + total_row * d_denom
    d_dense_1, d_dense_2 = unpacked(d_state_1), unpacked(d_state_2)
    values_1 = jnp.where(first_live, values, zero)
    values_2 = jnp.where(second_live, values, zero)
    d_total_row = jnp.where(in_first, d_state_1[HEAD][None], d_state_2[HEAD][None])
    d_keys_h = dot_nt(values_1, d_dense_1) + dot_nt(values_2, d_dense_2) + live * d_total_row
    d_values_low = (dot_nn(keys_1, d_dense_1) + dot_nn(keys_2, d_dense_2)).astype(bfloat)
    d_query_in = (d_query * jax.nn.sigmoid(pre_q)).astype(bfloat)
    d_keys_in = (d_keys_h * jax.nn.sigmoid(pre_k)).astype(bfloat)
    d_normed = dot_nn(d_query_in, wq) + dot_nn(d_keys_in, wk) + dot_nn(d_values_low, wv)
    d_tokens = grad_attn + norm_back(d_normed, normal_a, inv_std_a, scale_a)

    def mod_sum(rows):
        return jnp.stack(
            [
                jnp.sum(jnp.where(in_first, rows, 0.0), axis=0),
                jnp.sum(jnp.where(in_second, rows, 0.0), axis=0),
            ]
        )

    sums = jnp.stack(
        [
            mod_sum(rows)
            for rows in (
                d_normed,
                d_normed * normal_a,
                d_gate_a,
                d_normed_ffn,
                d_normed_ffn * normal_f,
                d_gate_f,
            )
        ],
        axis=1,
    )
    items = jnp.arange(item_count, dtype=jnp.int32)[:, None, None]
    mod_table = jnp.where(items == first_item, sums[0][None], 0.0) + jnp.where(
        (items == first_item + 1), sums[1][None], 0.0
    )
    xq_row = d_xq_part.reshape(xheads, XLANE)[:, :XHEAD].reshape(width)
    rows_all = jnp.concatenate(
        [mod_table.reshape(-1, width), jnp.stack([d_out_bias, d_xo_bias, xq_row], axis=0)], axis=0
    )
    spare = att_pad - att_rows
    rows_count = rows_all.shape[0]
    rows_all = pad_rows(rows_all.astype(bfloat), spare * group).reshape(group, spare, width)

    qkv_grads = grads_call(
        [d_query_in, d_keys_in, d_values_low, normed],
        ((0, 3), (1, 3), (2, 3)),
        rows_all,
        att_piece,
        cols,
    )
    qkv_terms = core_terms(*qkv_grads)
    qkv_terms[1], mix_terms[-1] = tie(qkv_terms[1], mix_terms[-1])
    for stage in range(len(bits)):
        qkv_terms = halve_path(qkv_terms, stage, 0)

    d_ffn_all = share_dp(halve_z(ffn_terms, 1)).transpose(1, 0, 2, 3)
    d_ffn_all = d_ffn_all.reshape(3, padded_channels, width)[:, :channels]
    d_w_in = jnp.stack([d_ffn_all[0].T, d_ffn_all[1].T], axis=1).astype(single)
    d_w_pt = d_ffn_all[2].astype(single)

    d_mix_all = share_dp(halve_z(mix_terms, 0)).reshape(-1, width)
    d_w_out = d_mix_all[:cols].astype(single)
    d_w_xq = d_mix_all[cols : 2 * cols].T.astype(single)
    d_w_xo = d_mix_all[2 * cols : 3 * cols].astype(single)
    d_kv = d_mix_all[att_rows : att_rows + text_rows]
    d_kv = jnp.concatenate(
        [d_kv[:, number * TXT_PAD : (number + 1) * TXT_PAD] for number in range(lanes)], axis=0
    )
    d_kv = d_kv.reshape(2, cols, TXT_PAD)[:, :, :TXT]
    d_xv_bias = jnp.sum(d_kv[1].astype(single), axis=1)
    d_w_xkv = jnp.einsum("td,ket->dke", text_all, d_kv, preferred_element_type=single)
    d_text = jnp.einsum("ket,dke->td", d_kv, w_xkv, preferred_element_type=single)
    d_text = reduce_z(d_text.astype(bfloat).reshape(2, 2, TXT // group, width)).astype(single)
    d_small = d_mix_all[att_rows + text_rows : att_rows + text_rows + small_rows].reshape(-1)
    d_small = d_small[: 22 * padded_channels].reshape(2, 11, padded_channels)[:, :, :channels]
    d_small = d_small.swapaxes(0, 1).astype(single)
    d_dw_weight, d_dw_bias, d_in_bias = d_small[:9], d_small[9], d_small[10]

    d_qkv_all = share_dp(halve_z(qkv_terms, 0)).reshape(-1, width)
    d_w_qkv = d_qkv_all[:att_rows].reshape(3, cols, width).transpose(2, 0, 1).astype(single)
    rows_all = gather_z(d_qkv_all[att_rows:], True).reshape(-1, width)[:rows_count].astype(single)
    d_t_mod = rows_all[:-3].reshape(mod_table.shape)
    d_out_bias, d_xo_bias = rows_all[-3], rows_all[-2]
    d_xq_bias = lax.dynamic_slice_in_dim(rows_all[-1], me_z * cols, cols, 0)
    d_shift_table = jnp.sum(d_t_mod, axis=0)
    return (
        out_tokens,
        d_tokens,
        d_t_mod,
        d_text,
        d_shift_table,
        d_w_qkv,
        d_w_out,
        d_out_bias,
        d_w_xq,
        d_xq_bias,
        d_w_xkv,
        d_xv_bias,
        d_w_xo,
        d_xo_bias,
        d_w_in,
        d_in_bias,
        d_dw_weight,
        d_dw_bias,
        d_w_pt,
    )


def solution(mesh):
    rows = P(("dp", "tensor"), None)
    placed = (
        rows,
        rows,
        P(),
        P(),
        P(),
        P("tensor", None),
        P(),
        P(None, None, "tensor"),
        P("tensor", None),
        P(),
        P(None, "tensor"),
        P("tensor"),
        P(None, None, "tensor"),
        P("tensor"),
        P("tensor", None),
        P(),
        P(None, None, "tensor"),
        P(None, "tensor"),
        P(None, None, "tensor"),
        P(None, "tensor"),
        P("tensor", None),
    )
    return jax.shard_map(
        local,
        mesh=mesh,
        in_specs=placed,
        out_specs=(
            rows,
            rows,
            P(),
            P("tensor", None),
            P(),
            P(None, None, "tensor"),
            P("tensor", None),
            P(),
            P(None, "tensor"),
            P("tensor"),
            P(None, None, "tensor"),
            P("tensor"),
            P("tensor", None),
            P(),
            P(None, None, "tensor"),
            P(None, "tensor"),
            P(None, None, "tensor"),
            P(None, "tensor"),
            P("tensor", None),
        ),
        check_vma=False,
    )
```

```python
import functools

import jax
import jax.numpy as jnp
from jax import lax
from jax.experimental import pallas as pl
from jax.experimental.pallas import tpu as pltpu
from jax.sharding import PartitionSpec as P

HEAD = 32
XHEAD = 72
XLANE = 128
TXT = 300
TXT_PAD = 384
SIDE = 32
ITEM_SLOTS = 1024
REACH = 48
BLOCK = 128
LANES = 384
TABLE = 40

norm_eps = 1e-06
bfloat = jnp.bfloat16
single = jnp.float32
VMEM_BYTES = 60 * 1024 * 1024


def dot_nn(a, b):
    return lax.dot_general(a, b, (((1,), (0,)), ((), ())), preferred_element_type=single)


def dot_nt(a, b):
    return lax.dot_general(a, b, (((1,), (1,)), ((), ())), preferred_element_type=single)


def dot_tn(a, b):
    return lax.dot_general(a, b, (((0,), (0,)), ((), ())), preferred_element_type=single)


def swap(values, axis, bit):
    count = lax.axis_size(axis)
    return lax.ppermute(values, axis, [(i, i ^ bit) for i in range(count)])


def shift_devices(values, step):
    count = lax.axis_size("dp") * lax.axis_size("tensor")
    pairs = [(i, i + step) for i in range(count) if 0 <= i + step < count]
    return lax.ppermute(values, ("dp", "tensor"), pairs)


def bit_set(axis, bit):
    return (lax.axis_index(axis) // bit) % 2


def upper_bits():
    count = lax.axis_size("dp")
    bits = []
    bit = 2
    while bit < count:
        bits.append(bit)
        bit *= 2
    return bits


def turns(core):
    bits = upper_bits()
    cut = len(bits) // 2
    return bits[cut:] + bits[:cut] if core else bits


def turn_bit(number, sibling=False):
    core = lax.axis_index("dp") % 2
    first, second = turns(0)[number], turns(1)[number]
    return jnp.where(core == (1 if sibling else 0), first, second)


def swap_path(values, number):
    count = lax.axis_size("dp")
    return lax.ppermute(
        values, "dp", [(i, i ^ turns(i % 2)[number]) for i in range(count)]
    )


def turn_axes(values, place):
    count = len(upper_bits())
    axes = list(range(values.ndim))
    axes[place : place + count] = [place + turns(1).index(bit) for bit in turns(0)]
    return values.transpose(axes)


def own_turns(values, place, sibling=False):
    core = lax.axis_index("dp") % 2
    return jnp.where(core == (1 if sibling else 0), values, turn_axes(values, place))


def rank_of(step, parts):
    core = step % 2
    rank = jnp.bitwise_xor(lax.axis_index("dp"), core)
    for number in range(len(upper_bits())):
        if parts[number]:
            rank = jnp.bitwise_xor(rank, turn_bit(number, core == 1))
    return rank


def tie(*arrays):
    return lax.optimization_barrier(arrays)


def grow(values, axis, bit, place, absolute):
    other = swap(values, axis, bit)
    if absolute:
        high = bit_set(axis, bit) == 1
        return jnp.stack(
            [jnp.where(high, other, values), jnp.where(high, values, other)], axis=place
        )
    return jnp.stack([values, other], axis=place)


def grow_bits(values, axis, bits, absolute):
    have = []
    for bit in bits:
        values = grow(values, axis, bit, sum(h > bit for h in have), absolute)
        have.append(bit)
    return values


def total(terms):
    summed = terms[0].astype(single)
    for term in terms[1:]:
        summed = summed + term.astype(single)
    return summed.astype(bfloat)


def pick_at(terms, place, number):
    return [lax.index_in_dim(term, number, place, keepdims=False) for term in terms]


def gather_z(piece, absolute):
    return grow_bits(piece, "tensor", [2, 1], absolute)


def grow_path(values):
    for number in range(len(upper_bits())):
        values = jnp.stack([values, swap_path(values, number)])
    return values


def reduce_z(values):
    for bit, place in ((1, 1), (2, 0)):
        own = bit_set("tensor", bit)
        keep = lax.dynamic_index_in_dim(values, own, place, keepdims=False)
        send = lax.dynamic_index_in_dim(values, 1 - own, place, keepdims=False)
        values = total([keep, swap(send, "tensor", bit)])
    return values


def halve_path(terms, number, place):
    other = swap_path(total(pick_at(terms, place, 1)), number)
    return pick_at(terms, place, 0) + [other]


def halve_z_once(terms, bit, place):
    place = place + 1 if bit == 1 else place
    other = swap(total(pick_at(terms, place, 1)), "tensor", bit)
    return pick_at(terms, place, 0) + [other]


def attention_rows(cols):
    rows = -(-3 * cols // lax.axis_size("dp"))
    return -(-rows // 16) * 16


def bits_of(number, count):
    return [(number >> place) % 2 for place in range(count)]


def row_cuts(rows, cols):
    return sorted({0, rows} | {end % rows for end in (cols, 2 * cols, 3 * cols)})


def assemble_kernel(ranks, group, rows, cols, own, *refs):
    sources, refs = refs[:4], refs[4:]
    *outs, out, sems, out_sems = refs
    me_z = lax.axis_index("tensor")
    cuts = row_cuts(rows, cols)
    count = len(upper_bits())
    copies = []

    def put(source, rank, peer, low, high):
        place = rank * rows + low
        if isinstance(place, int) and place >= 3 * cols:
            return
        kind = place // cols
        target = out.at[kind, peer, pl.ds(pl.multiple_of(place - kind * cols, 16), high - low)]
        copy = pltpu.make_async_copy(source, target, sems.at[len(copies)])
        copies.append((place < 3 * cols, copy))

    for low, high in zip(cuts[:-1], cuts[1:]):
        for rank in range(ranks):
            put(own.at[rank, low:high], rank, me_z, low, high)
        for step in range(ranks):
            place, upper = step // 2 // (ranks // 4), step // 2 % (ranks // 4)
            source = sources[2 * (step % 2) + place]
            rank = rank_of(step, bits_of(step // 2, count))
            for peer in range(1, group):
                put(
                    source.at[upper, peer - 1, low:high],
                    rank,
                    jnp.bitwise_xor(me_z, peer),
                    low,
                    high,
                )
    for move in ("start", "wait"):
        for live, copy in copies:

            @pl.when(live)
            def _():
                getattr(copy, move)()

    stores = [
        pltpu.make_async_copy(out.at[kind], outs[kind], out_sems.at[kind]) for kind in range(3)
    ]
    for copy in stores:
        copy.start()
    for copy in stores:
        copy.wait()


def assemble(own, parts, cols):
    ranks, rows, features = own.shape
    group = parts[0].shape[1] + 1
    count = (len(row_cuts(rows, cols)) - 1) * ranks * group
    anywhere = pl.BlockSpec(memory_space=pl.ANY)
    return pl.pallas_call(
        functools.partial(assemble_kernel, ranks, group, rows, cols),
        in_specs=[anywhere] * 5,
        out_specs=[anywhere] * 3,
        out_shape=[jax.ShapeDtypeStruct((group, cols, features), own.dtype)] * 3,
        scratch_shapes=[
            pltpu.VMEM((3, group, cols, features), own.dtype),
            pltpu.SemaphoreType.DMA((count,)),
            pltpu.SemaphoreType.DMA((3,)),
        ],
        compiler_params=pltpu.CompilerParams(vmem_limit_bytes=VMEM_BYTES),
        cost_estimate=pl.CostEstimate(
            flops=0, bytes_accessed=ranks * rows * group * features, transcendentals=0
        ),
    )(own, *parts)


def grads_kernel(ranks, group, rows, cols, pairs, *refs):
    inputs, (extra, keep, send, whole, block, sems) = refs[:-6], refs[-6:]
    me_z = lax.axis_index("tensor")
    count = len(upper_bits())
    for kind, (left, right) in enumerate(pairs):
        grad = dot_tn(inputs[left][...], inputs[right][...])
        each = cols // XHEAD
        for peer in range(group):
            if grad.shape[0] == group * cols:
                rows_here = grad[peer * cols : (peer + 1) * cols]
            else:
                for head in range(each):
                    place = (peer * each + head) * XLANE
                    block[head * XHEAD : (head + 1) * XHEAD, :] = grad[place : place + XHEAD]
                rows_here = block[...]
            whole[peer, kind * cols : (kind + 1) * cols, :] = rows_here.astype(bfloat)
    begin = len(pairs) * cols
    used = begin + extra.shape[1]
    for peer in range(group):
        whole[peer, begin:used, :] = extra[peer]
        if used < rows * ranks:
            whole[peer, used:, :] = jnp.zeros((rows * ranks - used, extra.shape[2]), bfloat)
    copies = []
    for step in range(ranks):
        parts = bits_of(step // 2, count)[::-1]
        place = pl.multiple_of(rank_of(step, parts) * rows, 16)
        for peer in range(group):
            source = whole.at[jnp.bitwise_xor(me_z, peer), pl.ds(place, rows)]
            target = (keep, send)[step % 2].at[step // 2, peer]
            copies.append(pltpu.make_async_copy(source, target, sems.at[len(copies)]))
    for copy in copies:
        copy.start()
    for copy in copies:
        copy.wait()


def grads_call(arrays, pairs, extra, rows, cols):
    ranks, group = lax.axis_size("dp"), lax.axis_size("tensor")
    features = extra.shape[-1]
    height = arrays[0].shape[0]
    inside = pl.BlockSpec(memory_space=pltpu.VMEM)
    anywhere = pl.BlockSpec(memory_space=pl.ANY)
    out = jax.ShapeDtypeStruct((ranks // 2, group, rows, features), bfloat)
    return list(pl.pallas_call(
        functools.partial(grads_kernel, ranks, group, rows, cols, pairs),
        in_specs=[inside] * (len(arrays) + 1),
        out_specs=[anywhere] * 2,
        out_shape=[out, out],
        scratch_shapes=[
            pltpu.VMEM((group, rows * ranks, features), bfloat),
            pltpu.VMEM((cols, features), single),
            pltpu.SemaphoreType.DMA((ranks * group,)),
        ],
        compiler_params=pltpu.CompilerParams(vmem_limit_bytes=VMEM_BYTES),
        cost_estimate=pl.CostEstimate(
            flops=height * features * features,
            bytes_accessed=group * rows * ranks * features // 2,
            transcendentals=0,
        ),
    )(*arrays, extra))


def core_terms(keep, send):
    shape = (2,) * (len(upper_bits()) + 2) + keep.shape[2:]
    return [keep.reshape(shape), swap(send, "dp", 1).reshape(shape)]


def flip_z(values, place):
    for number, bit in enumerate((2, 1)):
        values = jnp.where(
            bit_set("tensor", bit) == 1, jnp.flip(values, place + number), values
        )
    return values


def share_turn(piece, number):
    other = swap_path(piece, number)
    high = jnp.bitwise_and(lax.axis_index("dp"), turn_bit(number)) != 0
    return jnp.stack([jnp.where(high, other, piece), jnp.where(high, piece, other)])


def share_core(piece):
    count = len(upper_bits())
    other = turn_axes(swap(piece, "dp", 1), 0)
    high = lax.axis_index("dp") % 2 == 1
    piece = jnp.stack([jnp.where(high, other, piece), jnp.where(high, piece, other)], axis=count)
    return own_turns(piece, 0).reshape((lax.axis_size("dp"),) + piece.shape[count + 1 :])


def flip_dp(values, place):
    ranks = lax.axis_size("dp")
    shape = values.shape
    bits = upper_bits() + [1]
    bits.sort(reverse=True)
    values = values.reshape(shape[:place] + (2,) * len(bits) + shape[place + 1 :])
    for number, bit in enumerate(bits):
        values = jnp.where(
            bit_set("dp", bit) == 1, jnp.flip(values, place + number), values
        )
    return values.reshape(shape[:place] + (ranks,) + shape[place + 1 :])


def grid_table(bucket):
    grid_height = jnp.where(
        bucket == 0, SIDE, jnp.where(bucket == 1, 3 * SIDE // 4, 3 * SIDE // 2)
    ).astype(jnp.int32)
    grid_width = jnp.where(
        bucket == 0, SIDE, jnp.where(bucket == 1, 5 * SIDE // 4, 5 * SIDE // 8)
    ).astype(jnp.int32)
    return (grid_height, grid_width)


def inside_tap(inner_pos, grid_height, grid_width, row_step, col_step):
    grid_row = inner_pos // grid_width
    grid_col = inner_pos % grid_width
    return (
        (inner_pos < grid_height * grid_width)
        & (grid_row + row_step >= 0)
        & (grid_row + row_step < grid_height)
        & (grid_col + col_step >= 0)
        & (grid_col + col_step < grid_width)
    )


def look_up(table, item):
    known = item[:, None] == jnp.arange(table.shape[0], dtype=jnp.int32)[None, :]
    return jnp.sum(jnp.where(known, table[None, :], 0), axis=1)


def shift_blocks(slots, total, item_bucket, sign, limit):
    item = slots // ITEM_SLOTS
    inner = slots % ITEM_SLOTS
    height, width = grid_table(look_up(item_bucket, item))
    index = jnp.arange(slots.shape[0], dtype=jnp.int32)
    known = (slots >= 0) & (slots < total) & (index < limit)
    columns = jnp.arange(BLOCK + 2 * REACH, dtype=jnp.int32)
    taps = []
    for row_step in (-1, 0, 1):
        for col_step in (-1, 0, 1):
            down, right = sign * row_step, sign * col_step
            inside = known & inside_tap(inner, height, width, down, right)
            target = index % BLOCK + REACH + down * width + right
            taps.append(
                (columns[None, :] == target[:, None]) & inside[:, None]
            )
    return jnp.stack(taps, axis=0).astype(bfloat)


def fetch_weights(core, begin, steps, sources, held, sems):
    own, *others = sources
    rows = held.shape[-2]
    chunks = []
    for step in range(steps):
        first, second = (begin + step) // 2, (begin + step) % 2
        slot = step % 2
        rank = rank_of(core, (first, second))
        place = pl.multiple_of(rank * rows, 16)
        copies = []
        for kind in range(3):
            target = held.at[slot, kind]
            copies.append((own.at[kind, pl.ds(place, rows)], target.at[0]))
            copies.append(
                (others[second].at[first, :, kind * rows : (kind + 1) * rows], target.at[1:4])
            )
        chunks.append(
            [
                pltpu.make_async_copy(source, target, sems.at[slot, number])
                for number, (source, target) in enumerate(copies)
            ]
        )
    for step in range(steps):

        @pl.when(pl.program_id(0) == step)
        def _():
            if step == 0:
                for copy in chunks[0]:
                    copy.start()
            if step + 1 < steps:
                for copy in chunks[step + 1]:
                    copy.start()
            for copy in chunks[step]:
                copy.wait()


def ffn_kernel(
    core,
    begin,
    steps,
    adds,
    own_rows,
    own_pad,
    normed_ref,
    grad_ref,
    reach_ref,
    back_ref,
    last_ref,
    small_ref,
    *refs,
):
    count = 3 if core is not None else 1
    sources = refs[:count]
    added = None
    if adds:
        added = refs[count]
        count += 1
    ffn_ref, dnormed_ref, dweight_ref, dsmall_ref = refs[count : count + 4]
    active, slope, dconv, glu, dexpand, *buffers = refs[count + 4 :]

    def store_grad(kind, grad):
        if added is not None:
            grad = grad + added[0, kind].astype(single)
        dweight_ref[0, kind] = grad.astype(bfloat)

    if core is None:
        weight = lambda kind: sources[0][0, kind]
    else:
        held, sems = buffers
        fetch_weights(core, begin, steps, sources, held, sems)
        slot = lax.rem(pl.program_id(0), 2)
        weight = lambda kind: held[slot, kind].reshape(-1, held.shape[-1])
    @pl.when(pl.program_id(0) == 0)
    def _():
        ffn_ref[...] = jnp.zeros_like(ffn_ref)
        dnormed_ref[...] = jnp.zeros_like(dnormed_ref)

    normed = normed_ref[...]
    channels = small_ref.shape[2]
    for half in range(2):
        expand = dot_nt(normed, weight(half)) + small_ref[half, 10:11, :]
        sig = jax.nn.sigmoid(expand)
        active[half] = (expand * sig).astype(bfloat)
        mid, sig_mid = expand[2 * REACH : 2 * REACH + own_pad], sig[2 * REACH : 2 * REACH + own_pad]
        slope[half] = sig_mid * (1.0 + mid * (1.0 - sig_mid))
    dglu = dot_nt(grad_ref[...], weight(2))
    blocks = grad_ref.shape[0] // BLOCK
    for block in range(blocks):
        begin = block * BLOCK
        convs = []
        for half in range(2):
            moved = dot_nn(
                reach_ref[block], active[half, begin : begin + BLOCK + 2 * REACH, :]
            )
            total = small_ref[half, 9:10, :]
            for tap in range(9):
                total = total + moved[tap * BLOCK : (tap + 1) * BLOCK] * small_ref[half, tap : tap + 1, :]
            convs.append(total)
        value, gate = convs
        sig = jax.nn.sigmoid(gate)
        act = gate * sig
        grad = dglu[begin : begin + BLOCK]
        glu[begin : begin + BLOCK, :] = (value * act).astype(bfloat)
        dconv[0, begin : begin + BLOCK, :] = (grad * act).astype(bfloat)
        dconv[1, begin : begin + BLOCK, :] = (
            grad * value * (sig * (1.0 + gate * (1.0 - sig)))
        ).astype(bfloat)

    glu_own = glu[REACH : REACH + own_pad, :]
    if own_rows != own_pad:
        here = lax.broadcasted_iota(jnp.int32, (own_pad, channels), 0) < own_rows
        glu_own = jnp.where(here, glu_own.astype(single), 0.0).astype(bfloat)
    grad_own = grad_ref[REACH : REACH + own_pad, :]
    ffn_ref[...] += dot_nn(glu_own, weight(2))
    store_grad(2, dot_tn(glu_own, grad_own))
    normed_own = normed_ref[2 * REACH : 2 * REACH + own_pad, :]
    for half in range(2):
        dconv_own = dconv[half, REACH : REACH + own_pad, :].astype(single)
        if own_rows != own_pad:
            dconv_own = jnp.where(here, dconv_own, 0.0)
        dsmall_ref[half, 9:10, :] = jnp.sum(dconv_own, axis=0, keepdims=True)
        sums = [jnp.zeros((8, channels), single) for _ in range(9)]
        dbias = jnp.zeros((8, channels), single)
        for block in range(pl.cdiv(own_pad, BLOCK)):
            begin = block * BLOCK
            height = min(BLOCK, own_pad - begin)
            picks = back_ref[block] if height == BLOCK else last_ref[...]
            moved = dot_nn(picks, dconv[half, begin : begin + height + 2 * REACH, :])
            here_active = active[half, 2 * REACH + begin : 2 * REACH + begin + height, :].astype(single)
            total = jnp.zeros((height, channels), single)
            for tap in range(9):
                part = moved[tap * height : (tap + 1) * height]
                total = total + part * small_ref[half, tap : tap + 1, :]
                sums[tap] = sums[tap] + jnp.sum(
                    (part * here_active).reshape(height // 8, 8, channels), axis=0
                )
            grad = total * slope[half, begin : begin + height, :]
            dbias = dbias + jnp.sum(grad.reshape(height // 8, 8, channels), axis=0)
            dexpand[half, begin : begin + height, :] = grad.astype(bfloat)
        for tap in range(9):
            dsmall_ref[half, tap : tap + 1, :] = jnp.sum(sums[tap], axis=0, keepdims=True)
        dsmall_ref[half, 10:11, :] = jnp.sum(dbias, axis=0, keepdims=True)
        dsmall_ref[half, 11:16, :] = jnp.zeros((5, channels), single)
    for half in range(2):
        grad = dexpand[half]
        dnormed_ref[...] += dot_nn(grad, weight(half))
        store_grad(half, dot_tn(grad, normed_own))


def ffn_call(core, begin, steps, added, own_rows, own_pad, normed, grad, reach, back, last, weights, small):
    wide, features = normed.shape
    tall = grad.shape[0]
    channels = small.shape[2] // 4
    count = channels * steps
    direct = len(weights) > 1
    whole = lambda array: pl.BlockSpec(array.shape, lambda i: (0,) * array.ndim)
    rows = lambda base: pl.BlockSpec((1, 3, channels, features), lambda i: (i + base, 0, 0, 0))
    tiny = lambda base: pl.BlockSpec((2, 16, channels), lambda i: (0, 0, i + base))
    held = pl.BlockSpec((own_pad, features), lambda i: (0, 0))
    flops = 2 * count * features * (2 * wide + tall + 6 * own_pad) + 2 * count * 9 * 256 * 2 * (
        tall + own_pad
    )
    scratch = [
        pltpu.VMEM((2, wide, channels), bfloat),
        pltpu.VMEM((2, own_pad, channels), single),
        pltpu.VMEM((2, tall, channels), bfloat),
        pltpu.VMEM((tall, channels), bfloat),
        pltpu.VMEM((2, own_pad, channels), bfloat),
    ]
    if direct:
        group = weights[1].shape[1] + 1
        piece = weights[1].shape[2] // 3
        scratch += [
            pltpu.VMEM((2, 3, group, piece, features), bfloat),
            pltpu.SemaphoreType.DMA((2, 6)),
        ]
    return pl.pallas_call(
        functools.partial(
            ffn_kernel, core if direct else None, begin, steps, len(added) > 0, own_rows, own_pad
        ),
        grid=(steps,),
        in_specs=[whole(normed), whole(grad), whole(reach), whole(back), whole(last), tiny(begin)]
        + ([pl.BlockSpec(memory_space=pl.ANY)] * 3 if direct else [rows(begin)])
        + [rows(0)] * len(added),
        out_specs=[held, held, rows(0), tiny(0)],
        out_shape=[
            jax.ShapeDtypeStruct((own_pad, features), single),
            jax.ShapeDtypeStruct((own_pad, features), single),
            jax.ShapeDtypeStruct((steps, 3, channels, features), bfloat),
            jax.ShapeDtypeStruct((2, 16, count), single),
        ],
        scratch_shapes=scratch,
        compiler_params=pltpu.CompilerParams(vmem_limit_bytes=VMEM_BYTES),
        cost_estimate=pl.CostEstimate(
            flops=flops // 8, bytes_accessed=2 * count * features, transcendentals=count * tall // 4
        ),
    )(normed, grad, reach, back, last, small, *weights, *added)


def same_head():
    row = lax.broadcasted_iota(jnp.int32, (LANES, LANES), 0) // HEAD
    column = lax.broadcasted_iota(jnp.int32, (LANES, LANES), 1) // HEAD
    return row == column


def head_sums(left, right, extra):
    full = jnp.where(same_head(), dot_tn(left, right), 0.0)
    block = jnp.sum(full.reshape(LANES // HEAD, HEAD, LANES), axis=0)
    rest = jnp.zeros((TABLE - HEAD - 1, LANES), single)
    return jnp.concatenate([block, extra, rest], axis=0)


def head_blocks(table):
    tall = jnp.concatenate([table[:HEAD]] * (LANES // HEAD), axis=0)
    return jnp.where(same_head(), tall, 0.0).astype(bfloat)


def masked(values, column):
    return (values.astype(single) * column).astype(bfloat)


def softplus(values):
    return jnp.maximum(values, 0.0) + jnp.log1p(jnp.exp(-jnp.abs(values)))


def project_kernel(
    normed, wq, wk, wv, first, second, pre_q, pre_k, query, keys, values, table_1, table_2
):
    rows = normed[...]
    pre_q[...] = dot_nt(rows, wq[...])
    query[...] = softplus(pre_q[...]).astype(bfloat)
    pre_k[...] = dot_nt(rows, wk[...])
    key = softplus(pre_k[...]).astype(bfloat)
    keys[...] = key
    value = dot_nt(rows, wv[...]).astype(bfloat)
    values[...] = value
    for column, table in ((first, table_1), (second, table_2)):
        chosen = masked(key, column[...])
        table[...] = head_sums(
            chosen, value, jnp.sum(chosen.astype(single), axis=0, keepdims=True)
        )


def attend_kernel(query, state_1, state_2, first, second, wo, ratio, den, attn, out):
    @pl.when(pl.program_id(0) == 0)
    def _():
        out[...] = jnp.zeros_like(out)

    rows = query[...]
    parts = ((first[...], state_1[...]), (second[...], state_2[...]))
    numerator, weights = 0.0, 0.0
    for column, state in parts:
        numerator = numerator + dot_nn(masked(rows, column), head_blocks(state))
        weights = weights + column * state[HEAD : HEAD + 1]
    ones = same_head().astype(single).astype(bfloat)
    den[...] = dot_nn((rows.astype(single) * weights).astype(bfloat), ones)
    ratio[...] = numerator / den[...]
    attn[...] = ratio[...].astype(bfloat)
    out[...] += dot_nn(attn[...], wo[...])


def attend_back_kernel(
    grad, wo, ratio, den, query, pre_q, state_1, state_2, first, second, dquery, table_1, table_2
):
    dratio = dot_nt(grad[...], wo[...])
    ones = same_head().astype(single).astype(bfloat)
    dnumer = dratio / den[...]
    dden = -dot_nn((dratio * ratio[...]).astype(bfloat), ones) / den[...]
    rows = query[...]
    total_grad, weights = 0.0, 0.0
    for column, state, table in (
        (first[...], state_1[...], table_1),
        (second[...], state_2[...], table_2),
    ):
        chosen = (dnumer * column).astype(bfloat)
        total_grad = total_grad + dot_nt(chosen, head_blocks(state))
        weights = weights + column * state[HEAD : HEAD + 1]
        extra = jnp.sum(rows.astype(single) * dden * column, axis=0, keepdims=True)
        table[...] = head_sums(rows, chosen, extra)
    total_grad = total_grad + weights * dden
    dquery[...] = (total_grad * jax.nn.sigmoid(pre_q[...])).astype(bfloat)


def project_back_kernel(
    dquery, keys, values, pre_k, state_1, state_2, first, second, wq, wk, wv, dkeys, dvalues, dnormed
):
    @pl.when(pl.program_id(0) == 0)
    def _():
        dnormed[...] = jnp.zeros_like(dnormed)

    key_grad, value_grad = 0.0, 0.0
    for column, state in ((first[...], state_1[...]), (second[...], state_2[...])):
        block = head_blocks(state)
        key_grad = key_grad + dot_nt(masked(values[...], column), block)
        key_grad = key_grad + column * state[HEAD : HEAD + 1]
        value_grad = value_grad + dot_nn(masked(keys[...], column), block)
    dkeys[...] = (key_grad * jax.nn.sigmoid(pre_k[...])).astype(bfloat)
    dvalues[...] = value_grad.astype(bfloat)
    dnormed[...] += (
        dot_nn(dquery[...], wq[...]) + dot_nn(dkeys[...], wk[...]) + dot_nn(dvalues[...], wv[...])
    )


def lane_call(kernel, kinds, arrays, outs, rows, features):
    specs = {
        "l": pl.BlockSpec((rows, LANES), lambda g: (0, g)),
        "w": pl.BlockSpec((LANES, features), lambda g: (g, 0)),
        "t": pl.BlockSpec((TABLE, LANES), lambda g: (0, g)),
        "c": pl.BlockSpec((rows, 1), lambda g: (0, 0)),
        "a": pl.BlockSpec((rows, features), lambda g: (0, 0)),
    }
    shape = {"l": (rows, features), "t": (TABLE, features), "a": (rows, features)}
    return pl.pallas_call(
        kernel,
        grid=(features // LANES,),
        in_specs=[specs[kind] for kind in kinds],
        out_specs=[specs[kind] for kind, _ in outs],
        out_shape=[jax.ShapeDtypeStruct(shape[kind], dtype) for kind, dtype in outs],
        compiler_params=pltpu.CompilerParams(vmem_limit_bytes=VMEM_BYTES),
        cost_estimate=pl.CostEstimate(
            flops=rows * features * features, bytes_accessed=rows * features, transcendentals=0
        ),
    )(*arrays)


def head_probs(query, keys, lengths):
    scores = dot_nt(query, keys) * (XHEAD ** (-0.5))
    place = lax.broadcasted_iota(jnp.int32, scores.shape, 1)
    live = place < lengths
    scores = jnp.where(live, scores, -1e30)
    top = jnp.max(scores, axis=-1, keepdims=True)
    powers = jnp.exp(scores - top)
    return powers / jnp.sum(powers, axis=-1, keepdims=True)


def cross_kernel(query_ref, keys_ref, vals_ref, length_ref, mix_ref):
    probs = head_probs(query_ref[...], keys_ref[0], length_ref[...])
    mix_ref[...] = dot_nn(probs.astype(bfloat), vals_ref[0]).astype(bfloat)


def cross_back_kernel(
    query_ref, keys_ref, vals_ref, length_ref, dmix_ref, dquery_ref, dkeys_ref, dvals_ref, dbias_ref
):
    query, keys, dmix = query_ref[...], keys_ref[0], dmix_ref[...]
    probs = head_probs(query, keys, length_ref[...])
    dprobs = dot_nt(dmix, vals_ref[0])
    dvals_ref[0] = dot_tn(dmix, probs.astype(bfloat))[:XHEAD].astype(bfloat)
    row_dot = jnp.sum(probs * dprobs, axis=-1, keepdims=True)
    dscores = (probs * (dprobs - row_dot) * (XHEAD ** (-0.5))).astype(bfloat)
    dquery = dot_nn(dscores, keys)
    dbias_ref[...] = jnp.sum(dquery, axis=0, keepdims=True)
    dquery_ref[...] = dquery.astype(bfloat)
    dkeys_ref[0] = dot_tn(query, dscores)[:XHEAD].astype(bfloat)


def cross_specs(rows):
    lane = pl.BlockSpec((rows, XLANE), lambda h: (0, h))
    text = pl.BlockSpec((1, TXT_PAD, XLANE), lambda h: (h, 0, 0))
    length = pl.BlockSpec((rows, 1), lambda h: (0, 0))
    return lane, text, length


def cross_call(query, keys, vals, lengths):
    rows, heads = query.shape[0], keys.shape[0]
    lane, text, length = cross_specs(rows)
    return pl.pallas_call(
        cross_kernel,
        grid=(heads,),
        in_specs=[lane, text, text, length],
        out_specs=lane,
        out_shape=jax.ShapeDtypeStruct((rows, heads * XLANE), bfloat),
        compiler_params=pltpu.CompilerParams(vmem_limit_bytes=VMEM_BYTES),
        cost_estimate=pl.CostEstimate(
            flops=heads * rows * TXT_PAD * XLANE,
            bytes_accessed=2 * rows * heads * XLANE,
            transcendentals=heads * rows * TXT_PAD // 8,
        ),
    )(query, keys, vals, lengths)


def cross_back_call(query, keys, vals, lengths, dmix):
    rows, heads = query.shape[0], keys.shape[0]
    lane, text, length = cross_specs(rows)
    return pl.pallas_call(
        cross_back_kernel,
        grid=(heads,),
        in_specs=[lane, text, text, length, lane],
        out_specs=[
            lane,
            pl.BlockSpec((1, XHEAD, TXT_PAD), lambda h: (h, 0, 0)),
            pl.BlockSpec((1, XHEAD, TXT_PAD), lambda h: (h, 0, 0)),
            pl.BlockSpec((1, XLANE), lambda h: (0, h)),
        ],
        out_shape=[
            jax.ShapeDtypeStruct((rows, heads * XLANE), bfloat),
            jax.ShapeDtypeStruct((heads, XHEAD, TXT_PAD), bfloat),
            jax.ShapeDtypeStruct((heads, XHEAD, TXT_PAD), bfloat),
            jax.ShapeDtypeStruct((1, heads * XLANE), single),
        ],
        compiler_params=pltpu.CompilerParams(vmem_limit_bytes=VMEM_BYTES),
        cost_estimate=pl.CostEstimate(
            flops=heads * rows * TXT_PAD * XLANE,
            bytes_accessed=2 * rows * heads * XLANE,
            transcendentals=heads * rows * TXT_PAD // 8,
        ),
    )(query, keys, vals, lengths, dmix)


def norm_parts(values):
    centred = values - jnp.mean(values, axis=-1, keepdims=True)
    inv_std = lax.rsqrt(jnp.mean(centred * centred, axis=-1, keepdims=True) + norm_eps)
    return (centred * inv_std, inv_std)


def norm_back(grad_in, normal, inv_std, scale):
    scaled = grad_in * (1.0 + scale)
    return (
        scaled
        - jnp.mean(scaled, axis=-1, keepdims=True)
        - normal * jnp.mean(scaled * normal, axis=-1, keepdims=True)
    ) * inv_std


def pad_rows(values, rows):
    return jnp.pad(values, ((0, rows - values.shape[0]),) + ((0, 0),) * (values.ndim - 1))


def pad_heads(rows, heads):
    features = rows.shape[1]
    shaped = rows.reshape(heads, XHEAD, features)
    return jnp.pad(shaped, ((0, 0), (0, XLANE - XHEAD), (0, 0))).reshape(heads * XLANE, features)


def local(
    tokens,
    cotangent,
    item_bucket,
    text_len,
    t_mod,
    text_tokens,
    shift_table,
    w_qkv,
    w_out,
    out_bias,
    w_xq,
    xq_bias,
    w_xkv,
    xv_bias,
    w_xo,
    xo_bias,
    w_in,
    in_bias,
    dw_weight,
    dw_bias,
    w_pt,
):
    group = lax.axis_size("tensor")
    ranks = lax.axis_size("dp")
    me_z = lax.axis_index("tensor")
    me_d = lax.axis_index("dp")
    own_rows, width = tokens.shape
    own_pad = -(-own_rows // 32) * 32
    tall = -(-(own_rows + 2 * REACH) // BLOCK) * BLOCK
    wide = tall + 2 * REACH
    total_rows = own_rows * group * ranks
    item_count = t_mod.shape[0]
    heads = width // HEAD
    xheads = width // XHEAD
    cols = w_xq.shape[1]
    channels = w_in.shape[2]
    padded_channels = -(-channels // 384) * 384
    own_start = (me_d * group + me_z) * own_rows
    first_item = own_start // ITEM_SLOTS
    last_item = (own_start + own_rows - 1) // ITEM_SLOTS
    two_items = last_item != first_item

    bits = upper_bits()
    att_piece = attention_rows(cols)
    att_pad = att_piece * ranks
    att_rows = 3 * cols
    rows_qkv = pad_rows(w_qkv.transpose(1, 2, 0).reshape(att_rows, width), att_pad)
    rows_mix = pad_rows(jnp.concatenate([w_out, w_xq.T, w_xo], axis=0), att_pad)
    ffn_piece = padded_channels // ranks
    half_count = padded_channels * group // 2
    rows_ffn = jnp.stack(
        [pad_rows(rows, padded_channels) for rows in (w_in[:, 0].T, w_in[:, 1].T, w_pt)]
    )
    own_qkv = rows_qkv.reshape(ranks, att_piece, width)
    own_mix = rows_mix.reshape(ranks, att_piece, width)
    piece_1 = lax.dynamic_index_in_dim(own_qkv, me_d, 0, keepdims=False)
    piece_2 = lax.dynamic_index_in_dim(own_mix, me_d, 0, keepdims=False)

    def near_z(piece, far):
        near = swap(jnp.stack([piece, far]), "tensor", 1)
        return jnp.stack([near[0], far, near[1]])

    def turn(values, number):
        return jnp.stack([values, swap_path(values, number)])

    def mid_turns(values):
        for number in range(1, len(bits) - 1):
            values = turn(values, number)
        return values.reshape((-1,) + values.shape[-3:])

    def last_turn(values):
        return swap_path(values, len(bits) - 1)

    own_slots = own_start + jnp.arange(own_rows, dtype=jnp.int32)
    item = own_slots // ITEM_SLOTS
    in_first = (item == first_item)[:, None]
    in_second = jnp.logical_not(in_first)
    mod_first = shift_table + lax.dynamic_index_in_dim(t_mod, first_item, 0, keepdims=False)
    mod_second = shift_table + lax.dynamic_index_in_dim(t_mod, last_item, 0, keepdims=False)
    row_mod = lambda number: jnp.where(in_first, mod_first[number][None], mod_second[number][None])
    shift_a, scale_a, gate_a, shift_f, scale_f, gate_f = [row_mod(number) for number in range(6)]
    tokens_f = tokens.astype(single)
    grad_out = cotangent.astype(single)
    normal_a, inv_std_a = norm_parts(tokens_f)
    normed = (normal_a * (1.0 + scale_a) + shift_a).astype(bfloat)

    far_1 = swap(piece_1, "tensor", 2)
    far_1, normed = tie(far_1, normed)
    wave_1 = near_z(piece_1, far_1)
    wave_1, rows_ffn, item_bucket, piece_2 = tie(wave_1, rows_ffn, item_bucket, piece_2)
    far_2 = swap(piece_2, "tensor", 2)
    wave_1 = turn(wave_1, 0)
    inner = own_slots % ITEM_SLOTS
    grid_h, grid_w = grid_table(look_up(item_bucket, item))
    valid = inner < grid_h * grid_w
    live = valid.astype(single)[:, None]
    tall_slots = own_start - REACH + jnp.arange(tall, dtype=jnp.int32)
    reach = shift_blocks(tall_slots, total_rows, item_bucket, 1, tall)
    reach = reach.reshape(9, tall // BLOCK, BLOCK, -1).transpose(1, 0, 2, 3)
    reach = reach.reshape(tall // BLOCK, 9 * BLOCK, -1)
    far_2, wave_1, reach, text_tokens = tie(far_2, wave_1, reach, text_tokens)
    wave_1 = mid_turns(wave_1)
    last_1 = last_turn(wave_1)
    core_1 = swap(wave_1, "dp", 1)
    wave_2 = near_z(piece_2, far_2)
    text_rows_here = text_tokens.shape[0]
    text_half = pad_rows(text_tokens, -(-text_rows_here // 16) * 16)
    text_half = lax.dynamic_index_in_dim(
        text_half.reshape(2, -1, width), me_d % 2, 0, keepdims=False
    )
    text_far = swap(text_half, "tensor", 2)
    pad_slots = own_start + jnp.arange(own_pad, dtype=jnp.int32)
    back = shift_blocks(pad_slots, total_rows, item_bucket, -1, own_rows)
    full_blocks = own_pad // BLOCK
    rest = own_pad - full_blocks * BLOCK
    back_full = back[:, : full_blocks * BLOCK].reshape(9, full_blocks, BLOCK, -1).transpose(1, 0, 2, 3)
    back_full = back_full.reshape(full_blocks, 9 * BLOCK, -1)
    rest = max(rest, 32)
    back_last = back[:, own_pad - rest :, : rest + 2 * REACH].reshape(9 * rest, -1)
    d_ffn = (grad_out * live * gate_f).astype(bfloat)
    wave_1, last_1, core_1, wave_2, back_full, back_last, d_ffn, text_far = tie(
        wave_1, last_1, core_1, wave_2, back_full, back_last, d_ffn, text_far
    )
    core_last_1 = swap(last_1, "dp", 1)
    piece_3 = lax.dynamic_slice_in_dim(rows_ffn, me_d * ffn_piece, ffn_piece, 1)
    piece_3 = piece_3.reshape(3 * ffn_piece, width)
    core_last_1, wave_2, piece_3 = tie(core_last_1, wave_2, piece_3)
    wave_2 = turn(wave_2, 0)
    far_3 = swap(piece_3, "tensor", 2)
    text_near = swap(jnp.stack([text_half, text_far]), "tensor", 1)
    wq, wk, wv = [
        part.reshape(width, width) for part in assemble(own_qkv, (wave_1, last_1, core_1, core_last_1), cols)
    ]
    wq, wk, wv, wave_2 = tie(wq, wk, wv, wave_2)
    wave_2 = mid_turns(wave_2)
    last_2 = last_turn(wave_2)
    core_2 = swap(wave_2, "dp", 1)
    first_live = (in_first & valid[:, None]).astype(single)
    second_live = (in_second & valid[:, None]).astype(single)
    first_all, second_all = in_first.astype(single), in_second.astype(single)
    over_lanes = functools.partial(lane_call, rows=own_rows, features=width)
    pre_q, pre_k, query, keys, values, table_1, table_2 = over_lanes(
        project_kernel,
        "awwwcc",
        (normed, wq, wk, wv, first_live, second_live),
        (("l", single), ("l", single), ("l", bfloat), ("l", bfloat), ("l", bfloat), ("t", single), ("t", single)),
    )

    span_rows = own_rows * group
    span_start = me_d * span_rows
    span_first = span_start // ITEM_SLOTS
    span_last = (span_start + span_rows - 1) // ITEM_SLOTS
    span_items = (span_rows - 2) // ITEM_SLOTS + 2

    def item_table(first_part, second_part):
        parts = []
        for number in range(span_items):
            chosen = jnp.where(first_item - span_first == number, first_part, 0.0)
            also = two_items & (last_item - span_first == number)
            parts.append(chosen + jnp.where(also, second_part, 0.0))
        return jnp.stack(parts).astype(bfloat)

    def item_sums(table):
        count = ranks - 1
        tail_part = lax.dynamic_index_in_dim(table, span_last - span_first, 0, keepdims=False)
        below = lax.ppermute(tail_part, "dp", [(i, i + 1) for i in range(count)])
        above = lax.ppermute(table[0], "dp", [(i + 1, i) for i in range(count)])
        below_same = (span_start - 1) // ITEM_SLOTS == span_first
        above_same = (span_start + span_rows) // ITEM_SLOTS == span_last
        sums = []
        for number in (first_item, last_item):
            part = lax.dynamic_index_in_dim(table, number - span_first, 0, keepdims=False)
            part = part.astype(single)
            part = part + jnp.where(below_same & (number == span_first), below.astype(single), 0.0)
            part = part + jnp.where(above_same & (number == span_last), above.astype(single), 0.0)
            sums.append(part)
        return sums

    small_rel = jnp.concatenate([dw_weight, dw_bias[None], in_bias[None]], axis=0)
    small_rel = jnp.pad(small_rel, ((0, 5), (0, 0), (0, padded_channels - channels)))
    sizes = small_rel.size
    small_rel = jnp.concatenate([small_rel.reshape(-1), xq_bias])
    down = tuple(range(2, 2 + len(bits)))

    table = item_table(table_1, table_2)
    table, far_3, text_near = tie(table, far_3, text_near)
    table = total([table, swap(table, "tensor", 1)])
    wave_3 = near_z(piece_3, far_3)
    in_order = lambda rel: [
        lax.dynamic_index_in_dim(rel, me_z ^ peer, 0, keepdims=False) for peer in range(group)
    ]
    by_core = lambda one, two: jnp.stack(
        [jnp.where(me_d % 2 == 0, one, two), jnp.where(me_d % 2 == 0, two, one)]
    )
    text_rel = jnp.stack([text_half, text_near[0], text_far, text_near[1]])
    text_other = swap(text_rel, "dp", 1)
    table, last_2, core_2, text_other = tie(table, last_2, core_2, text_other)
    table = total([table, swap(table, "tensor", 2)])
    core_last_2 = swap(last_2, "dp", 1)
    text_rel = by_core(text_rel, text_other).swapaxes(0, 1).reshape(group, -1, width)
    text_all = jnp.concatenate(in_order(text_rel[:, :text_rows_here]))
    text_kv = jnp.einsum("td,dke->tke", text_all, w_xkv, preferred_element_type=single)
    xkv_own = jnp.stack([text_kv[:, 0], text_kv[:, 1] + xv_bias], axis=0).astype(bfloat)
    xkv_half = lax.dynamic_index_in_dim(xkv_own, me_d % 2, 0, keepdims=False)
    table, core_last_2, xkv_half = tie(table, core_last_2, xkv_half)
    wo, wxq, wxo = [
        part.reshape(width, width) for part in assemble(own_mix, (wave_2, last_2, core_2, core_last_2), cols)
    ]
    wxq_pad = pad_heads(wxq, xheads)
    wxo_pad = pad_heads(wxo, xheads)

    state_1, state_2 = item_sums(table)
    xkv_far = swap(xkv_half, "tensor", 2)
    state_1, state_2, wo, wxq_pad, wxo_pad, wave_3, d_ffn = tie(
        state_1, state_2, wo, wxq_pad, wxo_pad, wave_3, d_ffn
    )
    wave_3 = turn(wave_3, 0)
    above = shift_devices(d_ffn[own_rows - REACH :], 1)
    below = shift_devices(d_ffn[:REACH], -1)
    attn_ratio, denominator, attn, attn_sum = over_lanes(
        attend_kernel,
        "lttccw",
        (query, state_1, state_2, first_all, second_all, wo),
        (("l", single), ("l", single), ("l", bfloat), ("a", single)),
    )
    attn_out = attn_sum + out_bias
    after_attn = tokens_f + live * gate_a * attn_out

    cross_in = after_attn.astype(bfloat)
    xq_product = dot_nt(cross_in, wxq_pad)
    wave_3, xkv_far, xq_product, above, below, small_rel = tie(
        wave_3, xkv_far, xq_product, above, below, small_rel
    )
    d_ffn_ext = pad_rows(jnp.concatenate([above, d_ffn, below], axis=0), tall)
    wave_3 = mid_turns(wave_3)
    last_3 = last_turn(wave_3)
    core_3 = swap(wave_3, "dp", 1)
    xkv_near = swap(jnp.stack([xkv_half, xkv_far]), "tensor", 1)
    xkv_rel = jnp.stack([xkv_half, xkv_near[0], xkv_far, xkv_near[1]])
    small_half = lax.dynamic_index_in_dim(small_rel.reshape(2, -1), me_d % 2, 0, keepdims=False)
    small_far = swap(small_half, "tensor", 2)
    xkv_rel, small_far = tie(xkv_rel, small_far)
    xkv_other = swap(xkv_rel, "dp", 1)
    small_near = swap(jnp.stack([small_half, small_far]), "tensor", 1)
    small = jnp.stack([small_half, small_near[0], small_far, small_near[1]])
    small_other = swap(small, "dp", 1)
    xkv_all = by_core(xkv_rel, xkv_other).swapaxes(0, 1)
    xkv_all = jnp.stack(in_order(xkv_all)).reshape(group, 2, TXT, cols // XHEAD, XHEAD)
    xkv_all = xkv_all.transpose(1, 0, 3, 2, 4).reshape(2, xheads, TXT, XHEAD)
    xkv_all = jnp.pad(xkv_all, ((0, 0), (0, 0), (0, TXT_PAD - TXT), (0, XLANE - XHEAD)))
    xkeys, xvals = xkv_all[0], xkv_all[1]
    small = by_core(small, small_other).swapaxes(0, 1).reshape(group, -1)
    xq_rel = small[:, sizes:]
    small = flip_dp(small[:, :sizes].reshape(group, 16, 2, ranks, ffn_piece), 3)
    small = small.reshape((group, 16, 2) + (2,) * (len(bits) + 1) + (ffn_piece,))
    small = jnp.moveaxis(small, 0, len(bits) + 3)
    small = small.transpose((len(bits) + 2, 1, 0) + down[::-1] + (len(bits) + 3, len(bits) + 4))
    small = [
        own_turns(small[core], 2, core == 1).reshape(2, 16, half_count) for core in (0, 1)
    ]
    xq_bias_all = jnp.stack(in_order(xq_rel)).reshape(xheads, XHEAD)
    xq_bias_all = jnp.pad(xq_bias_all, ((0, 0), (0, XLANE - XHEAD))).reshape(xheads * XLANE)
    lengths = look_up(text_len, item)[:, None]
    xquery = (xq_product + xq_bias_all).astype(bfloat)
    cross_mix = cross_call(xquery, xkeys, xvals, lengths)
    cross_out = dot_nn(cross_mix, wxo_pad) + xo_bias
    after_cross = after_attn + live * cross_out

    normal_f, inv_std_f = norm_parts(after_cross)
    normed_ffn = (normal_f * (1.0 + scale_f) + shift_f).astype(bfloat)
    normed_ffn, wave_3, last_3, core_3, *small = tie(normed_ffn, wave_3, last_3, core_3, *small)
    core_last_3 = swap(last_3, "dp", 1)
    def ffn_half(core):
        count = len(bits)
        own = flip_dp(rows_ffn.reshape(3, ranks, ffn_piece, width), 1)
        own = own.reshape((3,) + (2,) * (count + 1) + (ffn_piece, width))
        own = jnp.moveaxis(lax.index_in_dim(own, core, count + 1, keepdims=False), 0, count)
        own = own_turns(own.transpose(tuple(range(count))[::-1] + (count, count + 1, count + 2)), 0, core == 1)
        others = jnp.concatenate(((wave_3, last_3), (core_3, core_last_3))[core])
        others = others.reshape((2,) * count + (group - 1, 3, ffn_piece, width))
        others = others.transpose(tuple(range(count))[::-1] + tuple(range(count, count + 4)))
        joined = jnp.concatenate([jnp.expand_dims(own, count), others], axis=count)
        joined = jnp.moveaxis(joined, count + 1, 2)
        return joined.reshape(4, 3, half_count // 4, width)

    direct = ffn_piece % 16 == 0 and len(bits) == 2
    weights_ffn = [
        [rows_ffn, *((wave_3, last_3), (core_3, core_last_3))[core]] if direct else [ffn_half(core)]
        for core in (0, 1)
    ]

    above = shift_devices(normed_ffn[own_rows - 2 * REACH :], 1)
    below = shift_devices(normed_ffn[: 2 * REACH], -1)
    normed_ext = pad_rows(jnp.concatenate([above, normed_ffn, below], axis=0), wide)
    tables = (reach, back_full, back_last)
    def ffn_part(core, begin, *added):
        return ffn_call(
            core, begin, 2, added, own_rows, own_pad, normed_ext, d_ffn_ext, *tables, weights_ffn[core], small[core]
        )

    part_3 = ffn_part(1, 2)
    normed_ext, *part_3 = tie(normed_ext, *part_3)
    other_3 = swap(part_3[2], "dp", 1)
    part_2 = ffn_part(1, 0)
    normed_ext, other_3, *part_2 = tie(normed_ext, other_3, *part_2)
    other_2 = swap(part_2[2], "dp", 1)
    part_1 = ffn_part(0, 2, other_3)
    normed_ext, other_2, *part_1 = tie(normed_ext, other_2, *part_1)
    turn_shape = (2, 3) + (2,) * len(bits) + (ffn_piece, width)
    ffn_got = swap_path(part_1[2].reshape(turn_shape), 0)
    part_0 = ffn_part(0, 0, other_2)
    parts = (part_0, part_1, part_2, part_3)
    ffn_out = sum(part[0] for part in parts)[:own_rows]
    d_normed_ffn = sum(part[1] for part in parts)[:own_rows]
    ffn_terms = [part_0[2].reshape(turn_shape), ffn_got]
    d_small_half = [
        jnp.concatenate([low[3], high[3]], axis=2) for low, high in ((part_0, part_1), (part_2, part_3))
    ]

    d_small = jnp.stack(
        [
            own_turns(
                part.astype(bfloat).reshape((2, 16) + (2,) * (len(bits) + 2) + (ffn_piece,)),
                2,
                core == 1,
            )
            for core, part in enumerate(d_small_half)
        ],
        axis=len(bits) + 2,
    )
    order = (len(bits) + 3, len(bits) + 4, 0, 1) + down[::-1] + (len(bits) + 2, len(bits) + 5)
    d_small = flip_z(d_small.transpose(order), 0)
    d_small = d_small.reshape(group, 2, 16, ranks, ffn_piece)[:, :, :11]
    d_small = flip_dp(d_small, 3).reshape(group, -1)
    small_rows = -(-d_small.shape[1] // (16 * width)) * 16
    d_small = jnp.pad(d_small, ((0, 0), (0, small_rows * width - d_small.shape[1])))
    d_small = d_small.reshape(group, small_rows, width)

    out_tokens = (after_cross + live * gate_f * ffn_out).astype(bfloat)
    d_gate_f = grad_out * live * ffn_out
    grad_cross = grad_out + norm_back(d_normed_ffn, normal_f, inv_std_f, scale_f)

    d_cross = grad_cross * live
    d_xo_bias = jnp.sum(d_cross, axis=0)
    d_cross_low = d_cross.astype(bfloat)
    d_cross_low, ffn_terms[-1] = tie(d_cross_low, ffn_terms[-1])
    for stage in range(1, len(bits)):
        ffn_terms = halve_path(ffn_terms, stage, 0 if stage == 1 else 1)
    d_mix = dot_nt(d_cross_low, wxo_pad).astype(bfloat)
    d_query_low, d_keys, d_vals, d_xq_part = cross_back_call(xquery, xkeys, xvals, lengths, d_mix)
    d_query_low, ffn_terms[-1] = tie(d_query_low, ffn_terms[-1])
    ffn_terms = halve_z_once(ffn_terms, 1, 1)
    grad_attn = grad_cross + dot_nn(d_query_low, wxq_pad)

    d_attn_out = grad_attn * live * gate_a
    d_gate_a = grad_attn * live * attn_out
    d_out_bias = jnp.sum(d_attn_out, axis=0)
    d_attn_low = d_attn_out.astype(bfloat)

    text_rows = 2 * cols * TXT_PAD // width
    mix_rows = -(-(att_rows + text_rows + small_rows) // (16 * ranks)) * 16
    lanes = width // TXT_PAD
    d_kv = jnp.concatenate(
        [d_keys.reshape(group, cols, TXT_PAD), d_vals.reshape(group, cols, TXT_PAD)], axis=1
    )
    d_kv = jnp.concatenate(
        [d_kv[:, number * text_rows : (number + 1) * text_rows] for number in range(lanes)], axis=2
    )
    mix_arrays = [
        attn,
        d_attn_low,
        d_query_low,
        cross_in,
        cross_mix,
        d_cross_low,
    ]
    mix_extra = jnp.concatenate([d_kv, d_small], axis=1)
    d_query_in, table_1, table_2 = over_lanes(
        attend_back_kernel,
        "awllllttcc",
        (d_attn_low, wo, attn_ratio, denominator, query, pre_q, state_1, state_2, first_all, second_all),
        (("l", bfloat), ("t", single), ("t", single)),
    )
    d_table = item_table(table_1, table_2)
    def mod_sum(rows):
        return jnp.stack(
            [
                jnp.sum(jnp.where(in_first, rows, 0.0), axis=0),
                jnp.sum(jnp.where(in_second, rows, 0.0), axis=0),
            ]
        )

    d_table, mix_extra = tie(d_table, mix_extra)
    d_table = total([d_table, swap(d_table, "tensor", 1)])
    mod_sums = [
        mod_sum(rows) for rows in (d_gate_a, d_normed_ffn, d_normed_ffn * normal_f, d_gate_f)
    ]
    d_table, d_out_bias, d_xo_bias, *mod_sums = tie(d_table, d_out_bias, d_xo_bias, *mod_sums)
    d_table = total([d_table, swap(d_table, "tensor", 2)])
    mix_grads = grads_call(mix_arrays, ((0, 1), (2, 3), (4, 5)), mix_extra, mix_rows, cols)
    d_table, mix_grads[1], ffn_terms[-1] = tie(d_table, mix_grads[1], ffn_terms[-1])
    mix_terms = core_terms(*mix_grads)
    d_state_1, d_state_2 = item_sums(d_table)
    d_state_1, d_state_2, mix_terms[1] = tie(d_state_1, d_state_2, mix_terms[1])
    mix_terms = halve_path(mix_terms, 0, 0)
    ffn_terms = halve_z_once(ffn_terms, 2, 1)
    d_keys_in, d_values_low, d_normed = over_lanes(
        project_back_kernel,
        "llllttccwww",
        (d_query_in, keys, values, pre_k, d_state_1, d_state_2, first_live, second_live, wq, wk, wv),
        (("l", bfloat), ("l", bfloat), ("a", single)),
    )
    d_tokens = grad_attn + norm_back(d_normed, normal_a, inv_std_a, scale_a)

    sums = jnp.stack([mod_sum(d_normed), mod_sum(d_normed * normal_a)] + mod_sums, axis=1)
    items = jnp.arange(item_count, dtype=jnp.int32)[:, None, None]
    mod_table = jnp.where(items == first_item, sums[0][None], 0.0) + jnp.where(
        (items == first_item + 1), sums[1][None], 0.0
    )
    xq_row = d_xq_part.reshape(xheads, XLANE)[:, :XHEAD].reshape(width)
    rows_all = jnp.concatenate(
        [mod_table.reshape(-1, width), jnp.stack([d_out_bias, d_xo_bias, xq_row], axis=0)], axis=0
    )
    rows_count = rows_all.shape[0]
    last_rows = -(-(att_rows + rows_count) // (16 * ranks)) * 16
    spare = -(-rows_count // 16) * 16
    rows_all = pad_rows(rows_all.astype(bfloat), spare)
    rows_all = jnp.broadcast_to(rows_all[None], (group, spare, width))

    qkv_grads = grads_call(
        [d_query_in, d_keys_in, d_values_low, normed],
        ((0, 3), (1, 3), (2, 3)),
        rows_all,
        last_rows,
        cols,
    )
    qkv_grads[1], mix_terms[-1] = tie(qkv_grads[1], mix_terms[-1])
    qkv_terms = core_terms(*qkv_grads)
    for stage in range(1, len(bits)):
        mix_terms = halve_path(mix_terms, stage, 0)
    qkv_terms[1], mix_terms[-1], ffn_terms[-1] = tie(qkv_terms[1], mix_terms[-1], ffn_terms[-1])
    qkv_terms = halve_path(qkv_terms, 0, 0)
    mix_terms = halve_z_once(mix_terms, 1, 0)
    qkv_terms[-1], mix_terms[-1] = tie(qkv_terms[-1], mix_terms[-1])
    for stage in range(1, len(bits)):
        qkv_terms = halve_path(qkv_terms, stage, 0)
    mix_terms = halve_z_once(mix_terms, 2, 0)
    qkv_terms[-1], mix_terms[-1] = tie(qkv_terms[-1], mix_terms[-1])
    qkv_terms = halve_z_once(qkv_terms, 1, 0)
    d_mix_all = share_turn(total(mix_terms), 0)
    d_ffn_all = share_turn(total(ffn_terms), 0)
    qkv_terms[-1], d_mix_all, d_ffn_all = tie(qkv_terms[-1], d_mix_all, d_ffn_all)
    qkv_terms = halve_z_once(qkv_terms, 2, 0)
    for stage in range(1, len(bits)):
        d_mix_all = share_turn(d_mix_all, stage)
    qkv_terms[-1], d_mix_all = tie(qkv_terms[-1], d_mix_all)
    d_qkv_all = share_turn(total(qkv_terms), 0)
    d_mix_all = share_core(d_mix_all)
    for stage in range(1, len(bits)):
        d_ffn_all = share_turn(d_ffn_all, stage)
    d_qkv_all, d_mix_all, d_ffn_all = tie(d_qkv_all, d_mix_all, d_ffn_all)
    for stage in range(1, len(bits)):
        d_qkv_all = share_turn(d_qkv_all, stage)
    d_ffn_all = share_core(d_ffn_all)
    d_qkv_all = share_core(d_qkv_all)
    d_ffn_all = d_ffn_all.transpose(1, 0, 2, 3)
    d_ffn_all = d_ffn_all.reshape(3, padded_channels, width)[:, :channels]
    d_w_in = jnp.stack([d_ffn_all[0].T, d_ffn_all[1].T], axis=1).astype(single)
    d_w_pt = d_ffn_all[2].astype(single)

    d_mix_all = d_mix_all.reshape(-1, width)
    d_w_out = d_mix_all[:cols].astype(single)
    d_w_xq = d_mix_all[cols : 2 * cols].T.astype(single)
    d_w_xo = d_mix_all[2 * cols : 3 * cols].astype(single)
    d_kv = d_mix_all[att_rows : att_rows + text_rows]
    d_kv = jnp.concatenate(
        [d_kv[:, number * TXT_PAD : (number + 1) * TXT_PAD] for number in range(lanes)], axis=0
    )
    d_kv = d_kv.reshape(2, cols, TXT_PAD)[:, :, :TXT]
    d_xv_bias = jnp.sum(d_kv[1].astype(single), axis=1)
    d_w_xkv = jnp.einsum("td,ket->dke", text_all, d_kv, preferred_element_type=single)
    d_text = jnp.einsum("ket,dke->td", d_kv, w_xkv, preferred_element_type=single)
    d_text = reduce_z(d_text.astype(bfloat).reshape(2, 2, TXT // group, width)).astype(single)
    d_small = d_mix_all[att_rows + text_rows : att_rows + text_rows + small_rows].reshape(-1)
    d_small = d_small[: 22 * padded_channels].reshape(2, 11, padded_channels)[:, :, :channels]
    d_small = d_small.swapaxes(0, 1).astype(single)
    d_dw_weight, d_dw_bias, d_in_bias = d_small[:9], d_small[9], d_small[10]

    d_qkv_all = d_qkv_all.reshape(-1, width)
    d_w_qkv = d_qkv_all[:att_rows].reshape(3, cols, width).transpose(2, 0, 1).astype(single)
    rows_all = d_qkv_all[att_rows : att_rows + rows_count].astype(single)
    d_t_mod = rows_all[:-3].reshape(mod_table.shape)
    d_out_bias, d_xo_bias = rows_all[-3], rows_all[-2]
    d_xq_bias = lax.dynamic_slice_in_dim(rows_all[-1], me_z * cols, cols, 0)
    d_shift_table = jnp.sum(d_t_mod, axis=0)
    return (
        out_tokens,
        d_tokens,
        d_t_mod,
        d_text,
        d_shift_table,
        d_w_qkv,
        d_w_out,
        d_out_bias,
        d_w_xq,
        d_xq_bias,
        d_w_xkv,
        d_xv_bias,
        d_w_xo,
        d_xo_bias,
        d_w_in,
        d_in_bias,
        d_dw_weight,
        d_dw_bias,
        d_w_pt,
    )


def solution(mesh):
    rows = P(("dp", "tensor"), None)
    placed = (
        rows,
        rows,
        P(),
        P(),
        P(),
        P("tensor", None),
        P(),
        P(None, None, "tensor"),
        P("tensor", None),
        P(),
        P(None, "tensor"),
        P("tensor"),
        P(None, None, "tensor"),
        P("tensor"),
        P("tensor", None),
        P(),
        P(None, None, "tensor"),
        P(None, "tensor"),
        P(None, None, "tensor"),
        P(None, "tensor"),
        P("tensor", None),
    )
    return jax.shard_map(
        local,
        mesh=mesh,
        in_specs=placed,
        out_specs=(
            rows,
            rows,
            P(),
            P("tensor", None),
            P(),
            P(None, None, "tensor"),
            P("tensor", None),
            P(),
            P(None, "tensor"),
            P("tensor"),
            P(None, None, "tensor"),
            P("tensor"),
            P("tensor", None),
            P(),
            P(None, None, "tensor"),
            P(None, "tensor"),
            P(None, None, "tensor"),
            P(None, "tensor"),
            P("tensor", None),
        ),
        check_vma=False,
    )
```

```python
import functools

import jax
import jax.numpy as jnp
from jax import lax
from jax.experimental import pallas as pl
from jax.experimental.pallas import tpu as pltpu
from jax.sharding import PartitionSpec as P

HEAD = 32
XHEAD = 72
XLANE = 128
TXT = 300
TXT_PAD = 384
SIDE = 32
ITEM_SLOTS = 1024
REACH = 48
BLOCK = 128
LANES = 384
TABLE = 40

norm_eps = 1e-06
bfloat = jnp.bfloat16
single = jnp.float32
VMEM_BYTES = 60 * 1024 * 1024


def dot_nn(a, b):
    return lax.dot_general(a, b, (((1,), (0,)), ((), ())), preferred_element_type=single)


def dot_nt(a, b):
    return lax.dot_general(a, b, (((1,), (1,)), ((), ())), preferred_element_type=single)


def dot_tn(a, b):
    return lax.dot_general(a, b, (((0,), (0,)), ((), ())), preferred_element_type=single)


def swap(values, axis, bit):
    count = lax.axis_size(axis)
    return lax.ppermute(values, axis, [(i, i ^ bit) for i in range(count)])


def shift_devices(values, step):
    count = lax.axis_size("dp") * lax.axis_size("tensor")
    pairs = [(i, i + step) for i in range(count) if 0 <= i + step < count]
    return lax.ppermute(values, ("dp", "tensor"), pairs)


def bit_set(axis, bit):
    return (lax.axis_index(axis) // bit) % 2


def upper_bits():
    count = lax.axis_size("dp")
    bits = []
    bit = 2
    while bit < count:
        bits.append(bit)
        bit *= 2
    return bits


def turns(core):
    bits = upper_bits()
    cut = len(bits) // 2
    return bits[cut:] + bits[:cut] if core else bits


def turn_bit(number, sibling=False):
    core = lax.axis_index("dp") % 2
    first, second = turns(0)[number], turns(1)[number]
    return jnp.where(core == (1 if sibling else 0), first, second)


def swap_path(values, number):
    count = lax.axis_size("dp")
    return lax.ppermute(
        values, "dp", [(i, i ^ turns(i % 2)[number]) for i in range(count)]
    )


def swap_z(values, number):
    ranks, group = lax.axis_size("dp"), lax.axis_size("tensor")
    pairs = []
    for rank in range(ranks):
        bit = (2, 1)[(rank + number) % 2]
        pairs += [(rank * group + peer, rank * group + (peer ^ bit)) for peer in range(group)]
    return lax.ppermute(values, ("dp", "tensor"), pairs)


def peer_of(place, sibling=False):
    core = lax.axis_index("dp") % 2
    if place in (1, 2):
        place = jnp.where(core == (1 if sibling else 0), place, 3 - place)
    return jnp.bitwise_xor(lax.axis_index("tensor"), place)


def turn_z(values, place, sibling=False):
    core = lax.axis_index("dp") % 2
    return jnp.where(
        core == (1 if sibling else 0), values, jnp.swapaxes(values, place, place + 1)
    )


def turn_axes(values, place):
    count = len(upper_bits())
    axes = list(range(values.ndim))
    axes[place : place + count] = [place + turns(1).index(bit) for bit in turns(0)]
    return values.transpose(axes)


def own_turns(values, place, sibling=False):
    core = lax.axis_index("dp") % 2
    return jnp.where(core == (1 if sibling else 0), values, turn_axes(values, place))


def rank_of(step, parts):
    core = step % 2
    rank = jnp.bitwise_xor(lax.axis_index("dp"), core)
    for number in range(len(upper_bits())):
        if parts[number]:
            rank = jnp.bitwise_xor(rank, turn_bit(number, core == 1))
    return rank


def tie(*arrays):
    return lax.optimization_barrier(arrays)


def grow(values, axis, bit, place, absolute):
    other = swap(values, axis, bit)
    if absolute:
        high = bit_set(axis, bit) == 1
        return jnp.stack(
            [jnp.where(high, other, values), jnp.where(high, values, other)], axis=place
        )
    return jnp.stack([values, other], axis=place)


def grow_bits(values, axis, bits, absolute):
    have = []
    for bit in bits:
        values = grow(values, axis, bit, sum(h > bit for h in have), absolute)
        have.append(bit)
    return values


def total(terms):
    summed = terms[0].astype(single)
    for term in terms[1:]:
        summed = summed + term.astype(single)
    return summed.astype(bfloat)


def pick_at(terms, place, number):
    return [lax.index_in_dim(term, number, place, keepdims=False) for term in terms]


def gather_z(piece, absolute):
    return grow_bits(piece, "tensor", [2, 1], absolute)


def grow_path(values):
    for number in range(len(upper_bits())):
        values = jnp.stack([values, swap_path(values, number)])
    return values


def reduce_z(values):
    for bit, place in ((1, 1), (2, 0)):
        own = bit_set("tensor", bit)
        keep = lax.dynamic_index_in_dim(values, own, place, keepdims=False)
        send = lax.dynamic_index_in_dim(values, 1 - own, place, keepdims=False)
        values = total([keep, swap(send, "tensor", bit)])
    return values


def halve_path(terms, number, place):
    other = swap_path(total(pick_at(terms, place, 1)), number)
    return pick_at(terms, place, 0) + [other]


def halve_z_once(terms, bit, place):
    place = place + 1 if bit == 1 else place
    other = swap_z(total(pick_at(terms, place, 1)), 1 if bit == 1 else 0)
    return pick_at(terms, place, 0) + [other]


def attention_rows(cols):
    rows = -(-3 * cols // lax.axis_size("dp"))
    return -(-rows // 16) * 16


def bits_of(number, count):
    return [(number >> place) % 2 for place in range(count)]


def row_cuts(rows, cols):
    return sorted({0, rows} | {end % rows for end in (cols, 2 * cols, 3 * cols)})


def assemble_kernel(ranks, group, rows, cols, own, *refs):
    sources, refs = refs[:4], refs[4:]
    *outs, out, sems, out_sems = refs
    me_z = lax.axis_index("tensor")
    cuts = row_cuts(rows, cols)
    count = len(upper_bits())
    copies = []

    def put(source, rank, peer, low, high):
        place = rank * rows + low
        if isinstance(place, int) and place >= 3 * cols:
            return
        kind = place // cols
        target = out.at[kind, peer, pl.ds(pl.multiple_of(place - kind * cols, 16), high - low)]
        copy = pltpu.make_async_copy(source, target, sems.at[len(copies)])
        copies.append((place < 3 * cols, copy))

    for low, high in zip(cuts[:-1], cuts[1:]):
        for rank in range(ranks):
            put(own.at[rank, low:high], rank, me_z, low, high)
        for step in range(ranks):
            place, upper = step // 2 // (ranks // 4), step // 2 % (ranks // 4)
            source = sources[2 * (step % 2) + place]
            rank = rank_of(step, bits_of(step // 2, count))
            for peer in range(1, group):
                put(
                    source.at[upper, peer - 1, low:high],
                    rank,
                    peer_of(peer, step % 2 == 1),
                    low,
                    high,
                )
    for move in ("start", "wait"):
        for live, copy in copies:

            @pl.when(live)
            def _():
                getattr(copy, move)()

    stores = [
        pltpu.make_async_copy(out.at[kind], outs[kind], out_sems.at[kind]) for kind in range(3)
    ]
    for copy in stores:
        copy.start()
    for copy in stores:
        copy.wait()


def assemble(own, parts, cols):
    ranks, rows, features = own.shape
    group = parts[0].shape[1] + 1
    count = (len(row_cuts(rows, cols)) - 1) * ranks * group
    anywhere = pl.BlockSpec(memory_space=pl.ANY)
    return pl.pallas_call(
        functools.partial(assemble_kernel, ranks, group, rows, cols),
        in_specs=[anywhere] * 5,
        out_specs=[anywhere] * 3,
        out_shape=[jax.ShapeDtypeStruct((group, cols, features), own.dtype)] * 3,
        scratch_shapes=[
            pltpu.VMEM((3, group, cols, features), own.dtype),
            pltpu.SemaphoreType.DMA((count,)),
            pltpu.SemaphoreType.DMA((3,)),
        ],
        compiler_params=pltpu.CompilerParams(vmem_limit_bytes=VMEM_BYTES),
        cost_estimate=pl.CostEstimate(
            flops=0, bytes_accessed=ranks * rows * group * features, transcendentals=0
        ),
    )(own, *parts)


def grads_kernel(ranks, group, rows, cols, pairs, *refs):
    inputs, (extra, keep, send, whole, block, sems) = refs[:-6], refs[-6:]
    count = len(upper_bits())
    for kind, (left, right) in enumerate(pairs):
        grad = dot_tn(inputs[left][...], inputs[right][...])
        each = cols // XHEAD
        for peer in range(group):
            if grad.shape[0] == group * cols:
                rows_here = grad[peer * cols : (peer + 1) * cols]
            else:
                for head in range(each):
                    place = (peer * each + head) * XLANE
                    block[head * XHEAD : (head + 1) * XHEAD, :] = grad[place : place + XHEAD]
                rows_here = block[...]
            whole[peer, kind * cols : (kind + 1) * cols, :] = rows_here.astype(bfloat)
    begin = len(pairs) * cols
    used = begin + extra.shape[1]
    for peer in range(group):
        whole[peer, begin:used, :] = extra[peer]
        if used < rows * ranks:
            whole[peer, used:, :] = jnp.zeros((rows * ranks - used, extra.shape[2]), bfloat)
    copies = []
    for step in range(ranks):
        parts = bits_of(step // 2, count)[::-1]
        place = pl.multiple_of(rank_of(step, parts) * rows, 16)
        for peer in range(group):
            source = whole.at[peer_of(peer, step % 2 == 1), pl.ds(place, rows)]
            target = (keep, send)[step % 2].at[step // 2, peer]
            copies.append(pltpu.make_async_copy(source, target, sems.at[len(copies)]))
    for copy in copies:
        copy.start()
    for copy in copies:
        copy.wait()


def grads_call(arrays, pairs, extra, rows, cols):
    ranks, group = lax.axis_size("dp"), lax.axis_size("tensor")
    features = extra.shape[-1]
    height = arrays[0].shape[0]
    inside = pl.BlockSpec(memory_space=pltpu.VMEM)
    anywhere = pl.BlockSpec(memory_space=pl.ANY)
    out = jax.ShapeDtypeStruct((ranks // 2, group, rows, features), bfloat)
    return list(pl.pallas_call(
        functools.partial(grads_kernel, ranks, group, rows, cols, pairs),
        in_specs=[inside] * (len(arrays) + 1),
        out_specs=[anywhere] * 2,
        out_shape=[out, out],
        scratch_shapes=[
            pltpu.VMEM((group, rows * ranks, features), bfloat),
            pltpu.VMEM((cols, features), single),
            pltpu.SemaphoreType.DMA((ranks * group,)),
        ],
        compiler_params=pltpu.CompilerParams(vmem_limit_bytes=VMEM_BYTES),
        cost_estimate=pl.CostEstimate(
            flops=height * features * features,
            bytes_accessed=group * rows * ranks * features // 2,
            transcendentals=0,
        ),
    )(*arrays, extra))


def core_terms(keep, send):
    shape = (2,) * (len(upper_bits()) + 2) + keep.shape[2:]
    return [keep.reshape(shape), swap(send, "dp", 1).reshape(shape)]


def flip_z(values, place):
    for number, bit in enumerate((2, 1)):
        values = jnp.where(
            bit_set("tensor", bit) == 1, jnp.flip(values, place + number), values
        )
    return values


def share_turn(piece, number):
    other = swap_path(piece, number)
    high = jnp.bitwise_and(lax.axis_index("dp"), turn_bit(number)) != 0
    return jnp.stack([jnp.where(high, other, piece), jnp.where(high, piece, other)])


def share_core(piece):
    count = len(upper_bits())
    other = turn_axes(swap(piece, "dp", 1), 0)
    high = lax.axis_index("dp") % 2 == 1
    piece = jnp.stack([jnp.where(high, other, piece), jnp.where(high, piece, other)], axis=count)
    return own_turns(piece, 0).reshape((lax.axis_size("dp"),) + piece.shape[count + 1 :])


def flip_dp(values, place):
    ranks = lax.axis_size("dp")
    shape = values.shape
    bits = upper_bits() + [1]
    bits.sort(reverse=True)
    values = values.reshape(shape[:place] + (2,) * len(bits) + shape[place + 1 :])
    for number, bit in enumerate(bits):
        values = jnp.where(
            bit_set("dp", bit) == 1, jnp.flip(values, place + number), values
        )
    return values.reshape(shape[:place] + (ranks,) + shape[place + 1 :])


def grid_table(bucket):
    grid_height = jnp.where(
        bucket == 0, SIDE, jnp.where(bucket == 1, 3 * SIDE // 4, 3 * SIDE // 2)
    ).astype(jnp.int32)
    grid_width = jnp.where(
        bucket == 0, SIDE, jnp.where(bucket == 1, 5 * SIDE // 4, 5 * SIDE // 8)
    ).astype(jnp.int32)
    return (grid_height, grid_width)


def inside_tap(inner_pos, grid_height, grid_width, row_step, col_step):
    grid_row = inner_pos // grid_width
    grid_col = inner_pos % grid_width
    return (
        (inner_pos < grid_height * grid_width)
        & (grid_row + row_step >= 0)
        & (grid_row + row_step < grid_height)
        & (grid_col + col_step >= 0)
        & (grid_col + col_step < grid_width)
    )


def look_up(table, item):
    known = item[:, None] == jnp.arange(table.shape[0], dtype=jnp.int32)[None, :]
    return jnp.sum(jnp.where(known, table[None, :], 0), axis=1)


def shift_blocks(slots, total, item_bucket, sign, limit):
    item = slots // ITEM_SLOTS
    inner = slots % ITEM_SLOTS
    height, width = grid_table(look_up(item_bucket, item))
    index = jnp.arange(slots.shape[0], dtype=jnp.int32)
    known = (slots >= 0) & (slots < total) & (index < limit)
    columns = jnp.arange(BLOCK + 2 * REACH, dtype=jnp.int32)
    taps = []
    for row_step in (-1, 0, 1):
        for col_step in (-1, 0, 1):
            down, right = sign * row_step, sign * col_step
            inside = known & inside_tap(inner, height, width, down, right)
            target = index % BLOCK + REACH + down * width + right
            taps.append(
                (columns[None, :] == target[:, None]) & inside[:, None]
            )
    return jnp.stack(taps, axis=0).astype(bfloat)


def fetch_weights(core, begin, steps, sources, held, sems):
    own, *others = sources
    rows = held.shape[-2]
    chunks = []
    for step in range(steps):
        first, second = (begin + step) // 2, (begin + step) % 2
        slot = step % 2
        rank = rank_of(core, (first, second))
        place = pl.multiple_of(rank * rows, 16)
        copies = []
        for kind in range(3):
            target = held.at[slot, kind]
            copies.append((own.at[kind, pl.ds(place, rows)], target.at[0]))
            copies.append(
                (others[second].at[first, :, kind * rows : (kind + 1) * rows], target.at[1:4])
            )
        chunks.append(
            [
                pltpu.make_async_copy(source, target, sems.at[slot, number])
                for number, (source, target) in enumerate(copies)
            ]
        )
    for step in range(steps):

        @pl.when(pl.program_id(0) == step)
        def _():
            if step == 0:
                for copy in chunks[0]:
                    copy.start()
            if step + 1 < steps:
                for copy in chunks[step + 1]:
                    copy.start()
            for copy in chunks[step]:
                copy.wait()


def ffn_kernel(
    core,
    begin,
    steps,
    adds,
    own_rows,
    own_pad,
    normed_ref,
    grad_ref,
    reach_ref,
    back_ref,
    last_ref,
    small_ref,
    *refs,
):
    count = 3 if core is not None else 1
    sources = refs[:count]
    added = None
    if adds:
        added = refs[count]
        count += 1
    ffn_ref, dnormed_ref, dweight_ref, dsmall_ref = refs[count : count + 4]
    active, slope, dconv, glu, dexpand, *buffers = refs[count + 4 :]

    def store_grad(kind, grad):
        if added is not None:
            grad = grad + added[0, kind].astype(single)
        dweight_ref[0, kind] = grad.astype(bfloat)

    if core is None:
        weight = lambda kind: sources[0][0, kind]
    else:
        held, sems = buffers
        fetch_weights(core, begin, steps, sources, held, sems)
        slot = lax.rem(pl.program_id(0), 2)
        weight = lambda kind: held[slot, kind].reshape(-1, held.shape[-1])
    @pl.when(pl.program_id(0) == 0)
    def _():
        ffn_ref[...] = jnp.zeros_like(ffn_ref)
        dnormed_ref[...] = jnp.zeros_like(dnormed_ref)

    normed = normed_ref[...]
    channels = small_ref.shape[2]
    for half in range(2):
        expand = dot_nt(normed, weight(half)) + small_ref[half, 10:11, :]
        sig = jax.nn.sigmoid(expand)
        active[half] = (expand * sig).astype(bfloat)
        mid, sig_mid = expand[2 * REACH : 2 * REACH + own_pad], sig[2 * REACH : 2 * REACH + own_pad]
        slope[half] = sig_mid * (1.0 + mid * (1.0 - sig_mid))
    dglu = dot_nt(grad_ref[...], weight(2))
    blocks = grad_ref.shape[0] // BLOCK
    for block in range(blocks):
        begin = block * BLOCK
        convs = []
        for half in range(2):
            moved = dot_nn(
                reach_ref[block], active[half, begin : begin + BLOCK + 2 * REACH, :]
            )
            total = small_ref[half, 9:10, :]
            for tap in range(9):
                total = total + moved[tap * BLOCK : (tap + 1) * BLOCK] * small_ref[half, tap : tap + 1, :]
            convs.append(total)
        value, gate = convs
        sig = jax.nn.sigmoid(gate)
        act = gate * sig
        grad = dglu[begin : begin + BLOCK]
        glu[begin : begin + BLOCK, :] = (value * act).astype(bfloat)
        dconv[0, begin : begin + BLOCK, :] = (grad * act).astype(bfloat)
        dconv[1, begin : begin + BLOCK, :] = (
            grad * value * (sig * (1.0 + gate * (1.0 - sig)))
        ).astype(bfloat)

    glu_own = glu[REACH : REACH + own_pad, :]
    if own_rows != own_pad:
        here = lax.broadcasted_iota(jnp.int32, (own_pad, channels), 0) < own_rows
        glu_own = jnp.where(here, glu_own.astype(single), 0.0).astype(bfloat)
    grad_own = grad_ref[REACH : REACH + own_pad, :]
    ffn_ref[...] += dot_nn(glu_own, weight(2))
    store_grad(2, dot_tn(glu_own, grad_own))
    normed_own = normed_ref[2 * REACH : 2 * REACH + own_pad, :]
    for half in range(2):
        dconv_own = dconv[half, REACH : REACH + own_pad, :].astype(single)
        if own_rows != own_pad:
            dconv_own = jnp.where(here, dconv_own, 0.0)
        dsmall_ref[half, 9:10, :] = jnp.sum(dconv_own, axis=0, keepdims=True)
        sums = [jnp.zeros((8, channels), single) for _ in range(9)]
        dbias = jnp.zeros((8, channels), single)
        for block in range(pl.cdiv(own_pad, BLOCK)):
            begin = block * BLOCK
            height = min(BLOCK, own_pad - begin)
            picks = back_ref[block] if height == BLOCK else last_ref[...]
            moved = dot_nn(picks, dconv[half, begin : begin + height + 2 * REACH, :])
            here_active = active[half, 2 * REACH + begin : 2 * REACH + begin + height, :].astype(single)
            total = jnp.zeros((height, channels), single)
            for tap in range(9):
                part = moved[tap * height : (tap + 1) * height]
                total = total + part * small_ref[half, tap : tap + 1, :]
                sums[tap] = sums[tap] + jnp.sum(
                    (part * here_active).reshape(height // 8, 8, channels), axis=0
                )
            grad = total * slope[half, begin : begin + height, :]
            dbias = dbias + jnp.sum(grad.reshape(height // 8, 8, channels), axis=0)
            dexpand[half, begin : begin + height, :] = grad.astype(bfloat)
        for tap in range(9):
            dsmall_ref[half, tap : tap + 1, :] = jnp.sum(sums[tap], axis=0, keepdims=True)
        dsmall_ref[half, 10:11, :] = jnp.sum(dbias, axis=0, keepdims=True)
        dsmall_ref[half, 11:16, :] = jnp.zeros((5, channels), single)
    for half in range(2):
        grad = dexpand[half]
        dnormed_ref[...] += dot_nn(grad, weight(half))
        store_grad(half, dot_tn(grad, normed_own))


def ffn_call(core, begin, steps, added, own_rows, own_pad, normed, grad, reach, back, last, weights, small):
    wide, features = normed.shape
    tall = grad.shape[0]
    channels = small.shape[2] // 4
    count = channels * steps
    direct = len(weights) > 1
    whole = lambda array: pl.BlockSpec(array.shape, lambda i: (0,) * array.ndim)
    rows = lambda base: pl.BlockSpec((1, 3, channels, features), lambda i: (i + base, 0, 0, 0))
    tiny = lambda base: pl.BlockSpec((2, 16, channels), lambda i: (0, 0, i + base))
    held = pl.BlockSpec((own_pad, features), lambda i: (0, 0))
    flops = 2 * count * features * (2 * wide + tall + 6 * own_pad) + 2 * count * 9 * 256 * 2 * (
        tall + own_pad
    )
    scratch = [
        pltpu.VMEM((2, wide, channels), bfloat),
        pltpu.VMEM((2, own_pad, channels), single),
        pltpu.VMEM((2, tall, channels), bfloat),
        pltpu.VMEM((tall, channels), bfloat),
        pltpu.VMEM((2, own_pad, channels), bfloat),
    ]
    if direct:
        group = weights[1].shape[1] + 1
        piece = weights[1].shape[2] // 3
        scratch += [
            pltpu.VMEM((2, 3, group, piece, features), bfloat),
            pltpu.SemaphoreType.DMA((2, 6)),
        ]
    return pl.pallas_call(
        functools.partial(
            ffn_kernel, core if direct else None, begin, steps, len(added) > 0, own_rows, own_pad
        ),
        grid=(steps,),
        in_specs=[whole(normed), whole(grad), whole(reach), whole(back), whole(last), tiny(begin)]
        + ([pl.BlockSpec(memory_space=pl.ANY)] * 3 if direct else [rows(begin)])
        + [rows(0)] * len(added),
        out_specs=[held, held, rows(0), tiny(0)],
        out_shape=[
            jax.ShapeDtypeStruct((own_pad, features), single),
            jax.ShapeDtypeStruct((own_pad, features), single),
            jax.ShapeDtypeStruct((steps, 3, channels, features), bfloat),
            jax.ShapeDtypeStruct((2, 16, count), single),
        ],
        scratch_shapes=scratch,
        compiler_params=pltpu.CompilerParams(vmem_limit_bytes=VMEM_BYTES),
        cost_estimate=pl.CostEstimate(
            flops=flops // 8, bytes_accessed=2 * count * features, transcendentals=count * tall // 4
        ),
    )(normed, grad, reach, back, last, small, *weights, *added)


def same_head():
    row = lax.broadcasted_iota(jnp.int32, (LANES, LANES), 0) // HEAD
    column = lax.broadcasted_iota(jnp.int32, (LANES, LANES), 1) // HEAD
    return row == column


def head_sums(left, right, extra):
    full = jnp.where(same_head(), dot_tn(left, right), 0.0)
    block = jnp.sum(full.reshape(LANES // HEAD, HEAD, LANES), axis=0)
    rest = jnp.zeros((TABLE - HEAD - 1, LANES), single)
    return jnp.concatenate([block, extra, rest], axis=0)


def head_blocks(table):
    tall = jnp.concatenate([table[:HEAD]] * (LANES // HEAD), axis=0)
    return jnp.where(same_head(), tall, 0.0).astype(bfloat)


def masked(values, column):
    return (values.astype(single) * column).astype(bfloat)


def softplus(values):
    return jnp.maximum(values, 0.0) + jnp.log1p(jnp.exp(-jnp.abs(values)))


def project_kernel(
    normed, wq, wk, wv, first, second, pre_q, pre_k, query, keys, values, table_1, table_2
):
    rows = normed[...]
    pre_q[...] = dot_nt(rows, wq[...])
    query[...] = softplus(pre_q[...]).astype(bfloat)
    pre_k[...] = dot_nt(rows, wk[...])
    key = softplus(pre_k[...]).astype(bfloat)
    keys[...] = key
    value = dot_nt(rows, wv[...]).astype(bfloat)
    values[...] = value
    for column, table in ((first, table_1), (second, table_2)):
        chosen = masked(key, column[...])
        table[...] = head_sums(
            chosen, value, jnp.sum(chosen.astype(single), axis=0, keepdims=True)
        )


def attend_kernel(query, state_1, state_2, first, second, wo, ratio, den, attn, out):
    @pl.when(pl.program_id(0) == 0)
    def _():
        out[...] = jnp.zeros_like(out)

    rows = query[...]
    parts = ((first[...], state_1[...]), (second[...], state_2[...]))
    numerator, weights = 0.0, 0.0
    for column, state in parts:
        numerator = numerator + dot_nn(masked(rows, column), head_blocks(state))
        weights = weights + column * state[HEAD : HEAD + 1]
    ones = same_head().astype(single).astype(bfloat)
    den[...] = dot_nn((rows.astype(single) * weights).astype(bfloat), ones)
    ratio[...] = numerator / den[...]
    attn[...] = ratio[...].astype(bfloat)
    out[...] += dot_nn(attn[...], wo[...])


def attend_back_kernel(
    grad, wo, ratio, den, query, pre_q, state_1, state_2, first, second, dquery, table_1, table_2
):
    dratio = dot_nt(grad[...], wo[...])
    ones = same_head().astype(single).astype(bfloat)
    dnumer = dratio / den[...]
    dden = -dot_nn((dratio * ratio[...]).astype(bfloat), ones) / den[...]
    rows = query[...]
    total_grad, weights = 0.0, 0.0
    for column, state, table in (
        (first[...], state_1[...], table_1),
        (second[...], state_2[...], table_2),
    ):
        chosen = (dnumer * column).astype(bfloat)
        total_grad = total_grad + dot_nt(chosen, head_blocks(state))
        weights = weights + column * state[HEAD : HEAD + 1]
        extra = jnp.sum(rows.astype(single) * dden * column, axis=0, keepdims=True)
        table[...] = head_sums(rows, chosen, extra)
    total_grad = total_grad + weights * dden
    dquery[...] = (total_grad * jax.nn.sigmoid(pre_q[...])).astype(bfloat)


def project_back_kernel(
    dquery, keys, values, pre_k, state_1, state_2, first, second, wq, wk, wv, dkeys, dvalues, dnormed
):
    @pl.when(pl.program_id(0) == 0)
    def _():
        dnormed[...] = jnp.zeros_like(dnormed)

    key_grad, value_grad = 0.0, 0.0
    for column, state in ((first[...], state_1[...]), (second[...], state_2[...])):
        block = head_blocks(state)
        key_grad = key_grad + dot_nt(masked(values[...], column), block)
        key_grad = key_grad + column * state[HEAD : HEAD + 1]
        value_grad = value_grad + dot_nn(masked(keys[...], column), block)
    dkeys[...] = (key_grad * jax.nn.sigmoid(pre_k[...])).astype(bfloat)
    dvalues[...] = value_grad.astype(bfloat)
    dnormed[...] += (
        dot_nn(dquery[...], wq[...]) + dot_nn(dkeys[...], wk[...]) + dot_nn(dvalues[...], wv[...])
    )


def lane_call(kernel, kinds, arrays, outs, rows, features):
    specs = {
        "l": pl.BlockSpec((rows, LANES), lambda g: (0, g)),
        "w": pl.BlockSpec((LANES, features), lambda g: (g, 0)),
        "t": pl.BlockSpec((TABLE, LANES), lambda g: (0, g)),
        "c": pl.BlockSpec((rows, 1), lambda g: (0, 0)),
        "a": pl.BlockSpec((rows, features), lambda g: (0, 0)),
    }
    shape = {"l": (rows, features), "t": (TABLE, features), "a": (rows, features)}
    return pl.pallas_call(
        kernel,
        grid=(features // LANES,),
        in_specs=[specs[kind] for kind in kinds],
        out_specs=[specs[kind] for kind, _ in outs],
        out_shape=[jax.ShapeDtypeStruct(shape[kind], dtype) for kind, dtype in outs],
        compiler_params=pltpu.CompilerParams(vmem_limit_bytes=VMEM_BYTES),
        cost_estimate=pl.CostEstimate(
            flops=rows * features * features, bytes_accessed=rows * features, transcendentals=0
        ),
    )(*arrays)


def head_probs(query, keys, lengths):
    scores = dot_nt(query, keys) * (XHEAD ** (-0.5))
    place = lax.broadcasted_iota(jnp.int32, scores.shape, 1)
    live = place < lengths
    scores = jnp.where(live, scores, -1e30)
    top = jnp.max(scores, axis=-1, keepdims=True)
    powers = jnp.exp(scores - top)
    return powers / jnp.sum(powers, axis=-1, keepdims=True)


def cross_kernel(query_ref, keys_ref, vals_ref, length_ref, mix_ref):
    probs = head_probs(query_ref[...], keys_ref[0], length_ref[...])
    mix_ref[...] = dot_nn(probs.astype(bfloat), vals_ref[0]).astype(bfloat)


def cross_back_kernel(
    query_ref, keys_ref, vals_ref, length_ref, dmix_ref, dquery_ref, dkeys_ref, dvals_ref, dbias_ref
):
    query, keys, dmix = query_ref[...], keys_ref[0], dmix_ref[...]
    probs = head_probs(query, keys, length_ref[...])
    dprobs = dot_nt(dmix, vals_ref[0])
    dvals_ref[0] = dot_tn(dmix, probs.astype(bfloat))[:XHEAD].astype(bfloat)
    row_dot = jnp.sum(probs * dprobs, axis=-1, keepdims=True)
    dscores = (probs * (dprobs - row_dot) * (XHEAD ** (-0.5))).astype(bfloat)
    dquery = dot_nn(dscores, keys)
    dbias_ref[...] = jnp.sum(dquery, axis=0, keepdims=True)
    dquery_ref[...] = dquery.astype(bfloat)
    dkeys_ref[0] = dot_tn(query, dscores)[:XHEAD].astype(bfloat)


def cross_specs(rows):
    lane = pl.BlockSpec((rows, XLANE), lambda h: (0, h))
    text = pl.BlockSpec((1, TXT_PAD, XLANE), lambda h: (h, 0, 0))
    length = pl.BlockSpec((rows, 1), lambda h: (0, 0))
    return lane, text, length


def cross_call(query, keys, vals, lengths):
    rows, heads = query.shape[0], keys.shape[0]
    lane, text, length = cross_specs(rows)
    return pl.pallas_call(
        cross_kernel,
        grid=(heads,),
        in_specs=[lane, text, text, length],
        out_specs=lane,
        out_shape=jax.ShapeDtypeStruct((rows, heads * XLANE), bfloat),
        compiler_params=pltpu.CompilerParams(vmem_limit_bytes=VMEM_BYTES),
        cost_estimate=pl.CostEstimate(
            flops=heads * rows * TXT_PAD * XLANE,
            bytes_accessed=2 * rows * heads * XLANE,
            transcendentals=heads * rows * TXT_PAD // 8,
        ),
    )(query, keys, vals, lengths)


def cross_back_call(query, keys, vals, lengths, dmix):
    rows, heads = query.shape[0], keys.shape[0]
    lane, text, length = cross_specs(rows)
    return pl.pallas_call(
        cross_back_kernel,
        grid=(heads,),
        in_specs=[lane, text, text, length, lane],
        out_specs=[
            lane,
            pl.BlockSpec((1, XHEAD, TXT_PAD), lambda h: (h, 0, 0)),
            pl.BlockSpec((1, XHEAD, TXT_PAD), lambda h: (h, 0, 0)),
            pl.BlockSpec((1, XLANE), lambda h: (0, h)),
        ],
        out_shape=[
            jax.ShapeDtypeStruct((rows, heads * XLANE), bfloat),
            jax.ShapeDtypeStruct((heads, XHEAD, TXT_PAD), bfloat),
            jax.ShapeDtypeStruct((heads, XHEAD, TXT_PAD), bfloat),
            jax.ShapeDtypeStruct((1, heads * XLANE), single),
        ],
        compiler_params=pltpu.CompilerParams(vmem_limit_bytes=VMEM_BYTES),
        cost_estimate=pl.CostEstimate(
            flops=heads * rows * TXT_PAD * XLANE,
            bytes_accessed=2 * rows * heads * XLANE,
            transcendentals=heads * rows * TXT_PAD // 8,
        ),
    )(query, keys, vals, lengths, dmix)


def norm_parts(values):
    centred = values - jnp.mean(values, axis=-1, keepdims=True)
    inv_std = lax.rsqrt(jnp.mean(centred * centred, axis=-1, keepdims=True) + norm_eps)
    return (centred * inv_std, inv_std)


def norm_back(grad_in, normal, inv_std, scale):
    scaled = grad_in * (1.0 + scale)
    return (
        scaled
        - jnp.mean(scaled, axis=-1, keepdims=True)
        - normal * jnp.mean(scaled * normal, axis=-1, keepdims=True)
    ) * inv_std


def pad_rows(values, rows):
    return jnp.pad(values, ((0, rows - values.shape[0]),) + ((0, 0),) * (values.ndim - 1))


def pad_heads(rows, heads):
    features = rows.shape[1]
    shaped = rows.reshape(heads, XHEAD, features)
    return jnp.pad(shaped, ((0, 0), (0, XLANE - XHEAD), (0, 0))).reshape(heads * XLANE, features)


def local(
    tokens,
    cotangent,
    item_bucket,
    text_len,
    t_mod,
    text_tokens,
    shift_table,
    w_qkv,
    w_out,
    out_bias,
    w_xq,
    xq_bias,
    w_xkv,
    xv_bias,
    w_xo,
    xo_bias,
    w_in,
    in_bias,
    dw_weight,
    dw_bias,
    w_pt,
):
    group = lax.axis_size("tensor")
    ranks = lax.axis_size("dp")
    me_z = lax.axis_index("tensor")
    me_d = lax.axis_index("dp")
    own_rows, width = tokens.shape
    own_pad = -(-own_rows // 32) * 32
    tall = -(-(own_rows + 2 * REACH) // BLOCK) * BLOCK
    wide = tall + 2 * REACH
    total_rows = own_rows * group * ranks
    item_count = t_mod.shape[0]
    heads = width // HEAD
    xheads = width // XHEAD
    cols = w_xq.shape[1]
    channels = w_in.shape[2]
    padded_channels = -(-channels // 384) * 384
    own_start = (me_d * group + me_z) * own_rows
    first_item = own_start // ITEM_SLOTS
    last_item = (own_start + own_rows - 1) // ITEM_SLOTS
    two_items = last_item != first_item

    bits = upper_bits()
    att_piece = attention_rows(cols)
    att_pad = att_piece * ranks
    att_rows = 3 * cols
    rows_qkv = pad_rows(w_qkv.transpose(1, 2, 0).reshape(att_rows, width), att_pad)
    rows_mix = pad_rows(jnp.concatenate([w_out, w_xq.T, w_xo], axis=0), att_pad)
    ffn_piece = padded_channels // ranks
    half_count = padded_channels * group // 2
    rows_ffn = jnp.stack(
        [pad_rows(rows, padded_channels) for rows in (w_in[:, 0].T, w_in[:, 1].T, w_pt)]
    )
    own_qkv = rows_qkv.reshape(ranks, att_piece, width)
    own_mix = rows_mix.reshape(ranks, att_piece, width)
    piece_1 = lax.dynamic_index_in_dim(own_qkv, me_d, 0, keepdims=False)
    piece_2 = lax.dynamic_index_in_dim(own_mix, me_d, 0, keepdims=False)

    def near_z(piece, far):
        near = swap_z(jnp.stack([piece, far]), 1)
        return jnp.stack([near[0], far, near[1]])

    def turn(values, number):
        return jnp.stack([values, swap_path(values, number)])

    def mid_turns(values):
        for number in range(1, len(bits) - 1):
            values = turn(values, number)
        return values.reshape((-1,) + values.shape[-3:])

    def last_turn(values):
        return swap_path(values, len(bits) - 1)

    own_slots = own_start + jnp.arange(own_rows, dtype=jnp.int32)
    item = own_slots // ITEM_SLOTS
    in_first = (item == first_item)[:, None]
    in_second = jnp.logical_not(in_first)
    mod_first = shift_table + lax.dynamic_index_in_dim(t_mod, first_item, 0, keepdims=False)
    mod_second = shift_table + lax.dynamic_index_in_dim(t_mod, last_item, 0, keepdims=False)
    row_mod = lambda number: jnp.where(in_first, mod_first[number][None], mod_second[number][None])
    shift_a, scale_a, gate_a, shift_f, scale_f, gate_f = [row_mod(number) for number in range(6)]
    tokens_f = tokens.astype(single)
    grad_out = cotangent.astype(single)
    normal_a, inv_std_a = norm_parts(tokens_f)
    normed = (normal_a * (1.0 + scale_a) + shift_a).astype(bfloat)

    far_1 = swap_z(piece_1, 0)
    far_1, normed = tie(far_1, normed)
    wave_1 = near_z(piece_1, far_1)
    wave_1, rows_ffn, item_bucket, piece_2 = tie(wave_1, rows_ffn, item_bucket, piece_2)
    far_2 = swap_z(piece_2, 0)
    wave_1 = turn(wave_1, 0)
    inner = own_slots % ITEM_SLOTS
    grid_h, grid_w = grid_table(look_up(item_bucket, item))
    valid = inner < grid_h * grid_w
    live = valid.astype(single)[:, None]
    tall_slots = own_start - REACH + jnp.arange(tall, dtype=jnp.int32)
    reach = shift_blocks(tall_slots, total_rows, item_bucket, 1, tall)
    reach = reach.reshape(9, tall // BLOCK, BLOCK, -1).transpose(1, 0, 2, 3)
    reach = reach.reshape(tall // BLOCK, 9 * BLOCK, -1)
    far_2, wave_1, reach, text_tokens = tie(far_2, wave_1, reach, text_tokens)
    wave_1 = mid_turns(wave_1)
    last_1 = last_turn(wave_1)
    core_1 = swap(wave_1, "dp", 1)
    wave_2 = near_z(piece_2, far_2)
    text_rows_here = text_tokens.shape[0]
    text_half = pad_rows(text_tokens, -(-text_rows_here // 16) * 16)
    text_half = lax.dynamic_index_in_dim(
        text_half.reshape(2, -1, width), me_d % 2, 0, keepdims=False
    )
    text_far = swap(text_half, "tensor", 2)
    pad_slots = own_start + jnp.arange(own_pad, dtype=jnp.int32)
    back = shift_blocks(pad_slots, total_rows, item_bucket, -1, own_rows)
    full_blocks = own_pad // BLOCK
    rest = own_pad - full_blocks * BLOCK
    back_full = back[:, : full_blocks * BLOCK].reshape(9, full_blocks, BLOCK, -1).transpose(1, 0, 2, 3)
    back_full = back_full.reshape(full_blocks, 9 * BLOCK, -1)
    rest = max(rest, 32)
    back_last = back[:, own_pad - rest :, : rest + 2 * REACH].reshape(9 * rest, -1)
    d_ffn = (grad_out * live * gate_f).astype(bfloat)
    wave_1, last_1, core_1, wave_2, back_full, back_last, d_ffn, text_far = tie(
        wave_1, last_1, core_1, wave_2, back_full, back_last, d_ffn, text_far
    )
    core_last_1 = swap(last_1, "dp", 1)
    piece_3 = lax.dynamic_slice_in_dim(rows_ffn, me_d * ffn_piece, ffn_piece, 1)
    piece_3 = piece_3.reshape(3 * ffn_piece, width)
    core_last_1, wave_2, piece_3 = tie(core_last_1, wave_2, piece_3)
    wave_2 = turn(wave_2, 0)
    far_3 = swap_z(piece_3, 0)
    text_near = swap(jnp.stack([text_half, text_far]), "tensor", 1)
    wq, wk, wv = [
        part.reshape(width, width) for part in assemble(own_qkv, (wave_1, last_1, core_1, core_last_1), cols)
    ]
    wq, wk, wv, wave_2, text_near = tie(wq, wk, wv, wave_2, text_near)
    wave_2 = mid_turns(wave_2)
    last_2 = last_turn(wave_2)
    core_2 = swap(wave_2, "dp", 1)
    in_order = lambda rel: [
        lax.dynamic_index_in_dim(rel, me_z ^ peer, 0, keepdims=False) for peer in range(group)
    ]
    by_core = lambda one, two: jnp.stack(
        [jnp.where(me_d % 2 == 0, one, two), jnp.where(me_d % 2 == 0, two, one)]
    )
    text_rel = jnp.stack([text_half, text_near[0], text_far, text_near[1]])
    text_other = swap(text_rel, "dp", 1)

    first_live = (in_first & valid[:, None]).astype(single)
    second_live = (in_second & valid[:, None]).astype(single)
    first_all, second_all = in_first.astype(single), in_second.astype(single)
    over_lanes = functools.partial(lane_call, rows=own_rows, features=width)
    pre_q, pre_k, query, keys, values, table_1, table_2 = over_lanes(
        project_kernel,
        "awwwcc",
        (normed, wq, wk, wv, first_live, second_live),
        (("l", single), ("l", single), ("l", bfloat), ("l", bfloat), ("l", bfloat), ("t", single), ("t", single)),
    )

    span_rows = own_rows * group
    span_start = me_d * span_rows
    span_first = span_start // ITEM_SLOTS
    span_last = (span_start + span_rows - 1) // ITEM_SLOTS
    span_items = (span_rows - 2) // ITEM_SLOTS + 2

    def item_table(first_part, second_part):
        parts = []
        for number in range(span_items):
            chosen = jnp.where(first_item - span_first == number, first_part, 0.0)
            also = two_items & (last_item - span_first == number)
            parts.append(chosen + jnp.where(also, second_part, 0.0))
        return jnp.stack(parts).astype(bfloat)

    def item_sums(table):
        count = ranks - 1
        tail_part = lax.dynamic_index_in_dim(table, span_last - span_first, 0, keepdims=False)
        below = lax.ppermute(tail_part, "dp", [(i, i + 1) for i in range(count)])
        above = lax.ppermute(table[0], "dp", [(i + 1, i) for i in range(count)])
        below_same = (span_start - 1) // ITEM_SLOTS == span_first
        above_same = (span_start + span_rows) // ITEM_SLOTS == span_last
        sums = []
        for number in (first_item, last_item):
            part = lax.dynamic_index_in_dim(table, number - span_first, 0, keepdims=False)
            part = part.astype(single)
            part = part + jnp.where(below_same & (number == span_first), below.astype(single), 0.0)
            part = part + jnp.where(above_same & (number == span_last), above.astype(single), 0.0)
            sums.append(part)
        return sums

    small_rel = jnp.concatenate([dw_weight, dw_bias[None], in_bias[None]], axis=0)
    small_rel = jnp.pad(small_rel, ((0, 5), (0, 0), (0, padded_channels - channels)))
    sizes = small_rel.size
    small_rel = jnp.concatenate([small_rel.reshape(-1), xq_bias]).astype(bfloat)
    small_tall = -(-small_rel.size // (32 * cols)) * 16
    small_rel = jnp.pad(small_rel, (0, 2 * small_tall * cols - small_rel.size))
    small_half = lax.dynamic_index_in_dim(
        small_rel.reshape(2, small_tall, cols), me_d % 2, 0, keepdims=False
    )
    down = tuple(range(2, 2 + len(bits)))

    table = item_table(table_1, table_2)
    table, text_other, far_3 = tie(table, text_other, far_3)
    table = total([table, swap(table, "tensor", 1)])
    text_rel = by_core(text_rel, text_other).swapaxes(0, 1).reshape(group, -1, width)
    text_all = jnp.concatenate(in_order(text_rel[:, :text_rows_here]))
    text_kv = jnp.einsum("td,dke->tke", text_all, w_xkv, preferred_element_type=single)
    xkv_own = jnp.stack([text_kv[:, 0], text_kv[:, 1] + xv_bias], axis=0).astype(bfloat)
    both_half = jnp.concatenate(
        [lax.dynamic_index_in_dim(xkv_own, me_d % 2, 0, keepdims=False), small_half], axis=0
    )
    table, both_half, last_2, core_2 = tie(table, both_half, last_2, core_2)
    table = total([table, swap(table, "tensor", 2)])
    both_far = swap(both_half, "tensor", 2)
    core_last_2 = swap(last_2, "dp", 1)
    table, both_far, core_last_2, far_3 = tie(table, both_far, core_last_2, far_3)
    state_1, state_2 = item_sums(table)
    wave_3 = near_z(piece_3, far_3)
    both_near = swap(jnp.stack([both_half, both_far]), "tensor", 1)
    wo, wxq, wxo = [
        part.reshape(width, width) for part in assemble(own_mix, (wave_2, last_2, core_2, core_last_2), cols)
    ]
    wxq_pad = pad_heads(wxq, xheads)
    wxo_pad = pad_heads(wxo, xheads)
    state_1, state_2, wo, wxq_pad, wxo_pad, both_near = tie(
        state_1, state_2, wo, wxq_pad, wxo_pad, both_near
    )
    both_rel = jnp.stack([both_half, both_near[0], both_far, both_near[1]])
    both_other = swap(both_rel, "dp", 1)
    attn_ratio, denominator, attn, attn_sum = over_lanes(
        attend_kernel,
        "lttccw",
        (query, state_1, state_2, first_all, second_all, wo),
        (("l", single), ("l", single), ("l", bfloat), ("a", single)),
    )
    attn_out = attn_sum + out_bias
    after_attn = tokens_f + live * gate_a * attn_out

    after_attn, wave_3, both_other = tie(after_attn, wave_3, both_other)
    wave_3 = turn(wave_3, 0)
    cross_in = after_attn.astype(bfloat)
    xq_product = dot_nt(cross_in, wxq_pad)
    both = by_core(both_rel, both_other)
    xkv_all = both[:, :, :TXT].swapaxes(0, 1)
    xkv_all = jnp.stack(in_order(xkv_all)).reshape(group, 2, TXT, cols // XHEAD, XHEAD)
    xkv_all = xkv_all.transpose(1, 0, 3, 2, 4).reshape(2, xheads, TXT, XHEAD)
    xkv_all = jnp.pad(xkv_all, ((0, 0), (0, 0), (0, TXT_PAD - TXT), (0, XLANE - XHEAD)))
    xkeys, xvals = xkv_all[0], xkv_all[1]
    small = both[:, :, TXT:].swapaxes(0, 1).reshape(group, -1).astype(single)
    xq_rel = small[:, sizes : sizes + cols]
    small = flip_dp(small[:, :sizes].reshape(group, 16, 2, ranks, ffn_piece), 3)
    small = small.reshape((group, 16, 2) + (2,) * (len(bits) + 1) + (ffn_piece,))
    small = jnp.moveaxis(small, 0, len(bits) + 3)
    small = small.transpose((len(bits) + 2, 1, 0) + down[::-1] + (len(bits) + 3, len(bits) + 4))
    small = small.reshape(small.shape[:-2] + (2, 2, ffn_piece))
    small = [
        turn_z(own_turns(small[core], 2, core == 1), 2 + len(bits), core == 1).reshape(
            2, 16, half_count
        )
        for core in (0, 1)
    ]
    xq_bias_all = jnp.stack(in_order(xq_rel)).reshape(xheads, XHEAD)
    xq_bias_all = jnp.pad(xq_bias_all, ((0, 0), (0, XLANE - XHEAD))).reshape(xheads * XLANE)
    lengths = look_up(text_len, item)[:, None]
    xquery = (xq_product + xq_bias_all).astype(bfloat)
    xquery, wave_3 = tie(xquery, wave_3)
    wave_3 = mid_turns(wave_3)
    last_3 = last_turn(wave_3)
    core_3 = swap(wave_3, "dp", 1)
    cross_mix = cross_call(xquery, xkeys, xvals, lengths)
    cross_out = dot_nn(cross_mix, wxo_pad) + xo_bias
    after_cross = after_attn + live * cross_out

    normal_f, inv_std_f = norm_parts(after_cross)
    normed_ffn = (normal_f * (1.0 + scale_f) + shift_f).astype(bfloat)
    normed_ffn, wave_3, last_3, core_3, *small = tie(normed_ffn, wave_3, last_3, core_3, *small)
    core_last_3 = swap(last_3, "dp", 1)
    def ffn_half(core):
        count = len(bits)
        own = flip_dp(rows_ffn.reshape(3, ranks, ffn_piece, width), 1)
        own = own.reshape((3,) + (2,) * (count + 1) + (ffn_piece, width))
        own = jnp.moveaxis(lax.index_in_dim(own, core, count + 1, keepdims=False), 0, count)
        own = own_turns(own.transpose(tuple(range(count))[::-1] + (count, count + 1, count + 2)), 0, core == 1)
        others = jnp.concatenate(((wave_3, last_3), (core_3, core_last_3))[core])
        others = others.reshape((2,) * count + (group - 1, 3, ffn_piece, width))
        others = others.transpose(tuple(range(count))[::-1] + tuple(range(count, count + 4)))
        joined = jnp.concatenate([jnp.expand_dims(own, count), others], axis=count)
        joined = jnp.moveaxis(joined, count + 1, 2)
        return joined.reshape(4, 3, half_count // 4, width)

    direct = ffn_piece % 16 == 0 and len(bits) == 2
    weights_ffn = [
        [rows_ffn, *((wave_3, last_3), (core_3, core_last_3))[core]] if direct else [ffn_half(core)]
        for core in (0, 1)
    ]

    above = shift_devices(
        jnp.concatenate([normed_ffn[own_rows - 2 * REACH :], d_ffn[own_rows - REACH :]], axis=0), 1
    )
    below = shift_devices(jnp.concatenate([normed_ffn[: 2 * REACH], d_ffn[:REACH]], axis=0), -1)
    normed_ext = pad_rows(
        jnp.concatenate([above[: 2 * REACH], normed_ffn, below[: 2 * REACH]], axis=0), wide
    )
    d_ffn_ext = pad_rows(
        jnp.concatenate([above[2 * REACH :], d_ffn, below[2 * REACH :]], axis=0), tall
    )
    tables = (reach, back_full, back_last)
    def ffn_part(core, begin, *added):
        return ffn_call(
            core, begin, 2, added, own_rows, own_pad, normed_ext, d_ffn_ext, *tables, weights_ffn[core], small[core]
        )

    part_3 = ffn_part(1, 2)
    normed_ext, *part_3 = tie(normed_ext, *part_3)
    other_3 = swap(part_3[2], "dp", 1)
    part_2 = ffn_part(1, 0)
    normed_ext, other_3, *part_2 = tie(normed_ext, other_3, *part_2)
    other_2 = swap(part_2[2], "dp", 1)
    part_1 = ffn_part(0, 2, other_3)
    normed_ext, other_2, *part_1 = tie(normed_ext, other_2, *part_1)
    turn_shape = (2, 3) + (2,) * len(bits) + (ffn_piece, width)
    ffn_got = swap_path(part_1[2], 0).reshape(turn_shape)
    part_0 = ffn_part(0, 0, other_2)
    parts = (part_0, part_1, part_2, part_3)
    ffn_out = sum(part[0] for part in parts)[:own_rows]
    d_normed_ffn = sum(part[1] for part in parts)[:own_rows]
    ffn_terms = [part_0[2].reshape(turn_shape), ffn_got]
    d_small_half = [
        jnp.concatenate([low[3], high[3]], axis=2) for low, high in ((part_0, part_1), (part_2, part_3))
    ]

    d_small = jnp.stack(
        [
            turn_z(
                own_turns(
                    part.astype(bfloat).reshape((2, 16) + (2,) * (len(bits) + 2) + (ffn_piece,)),
                    2,
                    core == 1,
                ),
                2 + len(bits),
                core == 1,
            )
            for core, part in enumerate(d_small_half)
        ],
        axis=len(bits) + 2,
    )
    order = (len(bits) + 3, len(bits) + 4, 0, 1) + down[::-1] + (len(bits) + 2, len(bits) + 5)
    d_small = flip_z(d_small.transpose(order), 0)
    d_small = d_small.reshape(group, 2, 16, ranks, ffn_piece)[:, :, :11]
    d_small = flip_dp(d_small, 3).reshape(group, -1)
    small_rows = -(-d_small.shape[1] // (16 * width)) * 16
    d_small = jnp.pad(d_small, ((0, 0), (0, small_rows * width - d_small.shape[1])))
    d_small = d_small.reshape(group, small_rows, width)

    out_tokens = (after_cross + live * gate_f * ffn_out).astype(bfloat)
    d_gate_f = grad_out * live * ffn_out
    grad_cross = grad_out + norm_back(d_normed_ffn, normal_f, inv_std_f, scale_f)

    d_cross = grad_cross * live
    d_xo_bias = jnp.sum(d_cross, axis=0)
    d_cross_low = d_cross.astype(bfloat)
    d_cross_low, ffn_terms[-1] = tie(d_cross_low, ffn_terms[-1])
    for stage in range(1, len(bits)):
        ffn_terms = halve_path(ffn_terms, stage, 0 if stage == 1 else 1)
    d_mix = dot_nt(d_cross_low, wxo_pad).astype(bfloat)
    d_query_low, d_keys, d_vals, d_xq_part = cross_back_call(xquery, xkeys, xvals, lengths, d_mix)
    d_query_low, ffn_terms[-1] = tie(d_query_low, ffn_terms[-1])
    ffn_terms = halve_z_once(ffn_terms, 1, 1)
    grad_attn = grad_cross + dot_nn(d_query_low, wxq_pad)

    d_attn_out = grad_attn * live * gate_a
    d_gate_a = grad_attn * live * attn_out
    d_out_bias = jnp.sum(d_attn_out, axis=0)
    d_attn_low = d_attn_out.astype(bfloat)

    text_rows = 2 * cols * TXT_PAD // width
    mix_rows = -(-(att_rows + text_rows + small_rows) // (16 * ranks)) * 16
    lanes = width // TXT_PAD
    d_kv = jnp.concatenate(
        [d_keys.reshape(group, cols, TXT_PAD), d_vals.reshape(group, cols, TXT_PAD)], axis=1
    )
    d_kv = jnp.concatenate(
        [d_kv[:, number * text_rows : (number + 1) * text_rows] for number in range(lanes)], axis=2
    )
    mix_arrays = [
        attn,
        d_attn_low,
        d_query_low,
        cross_in,
        cross_mix,
        d_cross_low,
    ]
    mix_extra = jnp.concatenate([d_kv, d_small], axis=1)
    d_query_in, table_1, table_2 = over_lanes(
        attend_back_kernel,
        "awllllttcc",
        (d_attn_low, wo, attn_ratio, denominator, query, pre_q, state_1, state_2, first_all, second_all),
        (("l", bfloat), ("t", single), ("t", single)),
    )
    d_table = item_table(table_1, table_2)
    def mod_sum(rows):
        return jnp.stack(
            [
                jnp.sum(jnp.where(in_first, rows, 0.0), axis=0),
                jnp.sum(jnp.where(in_second, rows, 0.0), axis=0),
            ]
        )

    d_table, mix_extra, ffn_terms[-1] = tie(d_table, mix_extra, ffn_terms[-1])
    d_table = total([d_table, swap(d_table, "tensor", 1)])
    mod_sums = [
        mod_sum(rows) for rows in (d_gate_a, d_normed_ffn, d_normed_ffn * normal_f, d_gate_f)
    ]
    d_table, d_out_bias, d_xo_bias, *mod_sums = tie(d_table, d_out_bias, d_xo_bias, *mod_sums)
    d_table = total([d_table, swap(d_table, "tensor", 2)])
    mix_grads = grads_call(mix_arrays, ((0, 1), (2, 3), (4, 5)), mix_extra, mix_rows, cols)
    d_table, mix_grads[1] = tie(d_table, mix_grads[1])
    mix_terms = core_terms(*mix_grads)
    d_state_1, d_state_2 = item_sums(d_table)
    d_state_1, d_state_2, mix_terms[1] = tie(d_state_1, d_state_2, mix_terms[1])
    mix_terms = halve_path(mix_terms, 0, 0)
    ffn_terms = halve_z_once(ffn_terms, 2, 1)
    d_keys_in, d_values_low, d_normed = over_lanes(
        project_back_kernel,
        "llllttccwww",
        (d_query_in, keys, values, pre_k, d_state_1, d_state_2, first_live, second_live, wq, wk, wv),
        (("l", bfloat), ("l", bfloat), ("a", single)),
    )
    d_tokens = grad_attn + norm_back(d_normed, normal_a, inv_std_a, scale_a)

    sums = jnp.stack([mod_sum(d_normed), mod_sum(d_normed * normal_a)] + mod_sums, axis=1)
    items = jnp.arange(item_count, dtype=jnp.int32)[:, None, None]
    mod_table = jnp.where(items == first_item, sums[0][None], 0.0) + jnp.where(
        (items == first_item + 1), sums[1][None], 0.0
    )
    xq_row = d_xq_part.reshape(xheads, XLANE)[:, :XHEAD].reshape(width)
    rows_all = jnp.concatenate(
        [mod_table.reshape(-1, width), jnp.stack([d_out_bias, d_xo_bias, xq_row], axis=0)], axis=0
    )
    rows_count = rows_all.shape[0]
    last_rows = -(-(att_rows + rows_count) // (16 * ranks)) * 16
    spare = -(-rows_count // 16) * 16
    rows_all = pad_rows(rows_all.astype(bfloat), spare)
    rows_all = jnp.broadcast_to(rows_all[None], (group, spare, width))

    qkv_grads = grads_call(
        [d_query_in, d_keys_in, d_values_low, normed],
        ((0, 3), (1, 3), (2, 3)),
        rows_all,
        last_rows,
        cols,
    )
    qkv_grads[1], mix_terms[-1], ffn_terms[-1] = tie(qkv_grads[1], mix_terms[-1], ffn_terms[-1])
    qkv_terms = core_terms(*qkv_grads)
    for stage in range(1, len(bits)):
        mix_terms = halve_path(mix_terms, stage, 0)
    qkv_terms[1], mix_terms[-1] = tie(qkv_terms[1], mix_terms[-1])
    qkv_terms = halve_path(qkv_terms, 0, 0)
    mix_terms = halve_z_once(mix_terms, 1, 0)
    qkv_terms[-1], mix_terms[-1] = tie(qkv_terms[-1], mix_terms[-1])
    for stage in range(1, len(bits)):
        qkv_terms = halve_path(qkv_terms, stage, 0)
    mix_terms = halve_z_once(mix_terms, 2, 0)
    qkv_terms[-1], mix_terms[-1], *ffn_terms = tie(qkv_terms[-1], mix_terms[-1], *ffn_terms)
    qkv_terms = halve_z_once(qkv_terms, 1, 0)
    d_mix_all = share_turn(total(mix_terms), 0)
    d_ffn_all = share_turn(total(ffn_terms), 0)
    qkv_terms[-1], d_mix_all, d_ffn_all = tie(qkv_terms[-1], d_mix_all, d_ffn_all)
    qkv_terms = halve_z_once(qkv_terms, 2, 0)
    for stage in range(1, len(bits)):
        d_mix_all = share_turn(d_mix_all, stage)
    qkv_terms[-1], d_mix_all = tie(qkv_terms[-1], d_mix_all)
    d_qkv_all = share_turn(total(qkv_terms), 0)
    d_mix_all = share_core(d_mix_all)
    for stage in range(1, len(bits)):
        d_ffn_all = share_turn(d_ffn_all, stage)
    d_qkv_all, d_mix_all, d_ffn_all = tie(d_qkv_all, d_mix_all, d_ffn_all)
    for stage in range(1, len(bits)):
        d_qkv_all = share_turn(d_qkv_all, stage)
    d_ffn_all = share_core(d_ffn_all)
    d_qkv_all, d_ffn_all = tie(d_qkv_all, d_ffn_all)
    d_qkv_all = share_core(d_qkv_all)
    d_ffn_all = d_ffn_all.transpose(1, 0, 2, 3)
    d_ffn_all = d_ffn_all.reshape(3, padded_channels, width)[:, :channels]
    d_w_in = jnp.stack([d_ffn_all[0].T, d_ffn_all[1].T], axis=1).astype(single)
    d_w_pt = d_ffn_all[2].astype(single)

    d_mix_all = d_mix_all.reshape(-1, width)
    d_w_out = d_mix_all[:cols].astype(single)
    d_w_xq = d_mix_all[cols : 2 * cols].T.astype(single)
    d_w_xo = d_mix_all[2 * cols : 3 * cols].astype(single)
    d_kv = d_mix_all[att_rows : att_rows + text_rows]
    d_kv = jnp.concatenate(
        [d_kv[:, number * TXT_PAD : (number + 1) * TXT_PAD] for number in range(lanes)], axis=0
    )
    d_kv = d_kv.reshape(2, cols, TXT_PAD)[:, :, :TXT]
    d_xv_bias = jnp.sum(d_kv[1].astype(single), axis=1)
    d_w_xkv = jnp.einsum("td,ket->dke", text_all, d_kv, preferred_element_type=single)
    d_text = jnp.einsum("ket,dke->td", d_kv, w_xkv, preferred_element_type=single)
    d_text = reduce_z(d_text.astype(bfloat).reshape(2, 2, TXT // group, width)).astype(single)
    d_small = d_mix_all[att_rows + text_rows : att_rows + text_rows + small_rows].reshape(-1)
    d_small = d_small[: 22 * padded_channels].reshape(2, 11, padded_channels)[:, :, :channels]
    d_small = d_small.swapaxes(0, 1).astype(single)
    d_dw_weight, d_dw_bias, d_in_bias = d_small[:9], d_small[9], d_small[10]

    d_qkv_all = d_qkv_all.reshape(-1, width)
    d_w_qkv = d_qkv_all[:att_rows].reshape(3, cols, width).transpose(2, 0, 1).astype(single)
    rows_all = d_qkv_all[att_rows : att_rows + rows_count].astype(single)
    d_t_mod = rows_all[:-3].reshape(mod_table.shape)
    d_out_bias, d_xo_bias = rows_all[-3], rows_all[-2]
    d_xq_bias = lax.dynamic_slice_in_dim(rows_all[-1], me_z * cols, cols, 0)
    d_shift_table = jnp.sum(d_t_mod, axis=0)
    return (
        out_tokens,
        d_tokens,
        d_t_mod,
        d_text,
        d_shift_table,
        d_w_qkv,
        d_w_out,
        d_out_bias,
        d_w_xq,
        d_xq_bias,
        d_w_xkv,
        d_xv_bias,
        d_w_xo,
        d_xo_bias,
        d_w_in,
        d_in_bias,
        d_dw_weight,
        d_dw_bias,
        d_w_pt,
    )


def solution(mesh):
    rows = P(("dp", "tensor"), None)
    placed = (
        rows,
        rows,
        P(),
        P(),
        P(),
        P("tensor", None),
        P(),
        P(None, None, "tensor"),
        P("tensor", None),
        P(),
        P(None, "tensor"),
        P("tensor"),
        P(None, None, "tensor"),
        P("tensor"),
        P("tensor", None),
        P(),
        P(None, None, "tensor"),
        P(None, "tensor"),
        P(None, None, "tensor"),
        P(None, "tensor"),
        P("tensor", None),
    )
    return jax.shard_map(
        local,
        mesh=mesh,
        in_specs=placed,
        out_specs=(
            rows,
            rows,
            P(),
            P("tensor", None),
            P(),
            P(None, None, "tensor"),
            P("tensor", None),
            P(),
            P(None, "tensor"),
            P("tensor"),
            P(None, None, "tensor"),
            P("tensor"),
            P("tensor", None),
            P(),
            P(None, None, "tensor"),
            P(None, "tensor"),
            P(None, None, "tensor"),
            P(None, "tensor"),
            P("tensor", None),
        ),
        check_vma=False,
    )
```

```python
import functools

import jax
import jax.numpy as jnp
from jax import lax
from jax.experimental import pallas as pl
from jax.experimental.pallas import tpu as pltpu
from jax.sharding import PartitionSpec as P

HEAD = 32
XHEAD = 72
XLANE = 128
TXT = 300
TXT_PAD = 384
SIDE = 32
ITEM_SLOTS = 1024
REACH = 48
BLOCK = 128
LANES = 384
TABLE = 40

norm_eps = 1e-06
bfloat = jnp.bfloat16
single = jnp.float32
VMEM_BYTES = 60 * 1024 * 1024


def dot_nn(a, b):
    return lax.dot_general(a, b, (((1,), (0,)), ((), ())), preferred_element_type=single)


def dot_nt(a, b):
    return lax.dot_general(a, b, (((1,), (1,)), ((), ())), preferred_element_type=single)


def dot_tn(a, b):
    return lax.dot_general(a, b, (((0,), (0,)), ((), ())), preferred_element_type=single)


def swap(values, axis, bit):
    count = lax.axis_size(axis)
    return lax.ppermute(values, axis, [(i, i ^ bit) for i in range(count)])


def shift_devices(values, step):
    count = lax.axis_size("dp") * lax.axis_size("tensor")
    pairs = [(i, i + step) for i in range(count) if 0 <= i + step < count]
    return lax.ppermute(values, ("dp", "tensor"), pairs)


def bit_set(axis, bit):
    return (lax.axis_index(axis) // bit) % 2


def upper_bits():
    count = lax.axis_size("dp")
    bits = []
    bit = 2
    while bit < count:
        bits.append(bit)
        bit *= 2
    return bits


def turns(core):
    bits = upper_bits()
    cut = len(bits) // 2
    return bits[cut:] + bits[:cut] if core else bits


def turn_bit(number, sibling=False):
    core = lax.axis_index("dp") % 2
    first, second = turns(0)[number], turns(1)[number]
    return jnp.where(core == (1 if sibling else 0), first, second)


def swap_path(values, number):
    count = lax.axis_size("dp")
    return lax.ppermute(
        values, "dp", [(i, i ^ turns(i % 2)[number]) for i in range(count)]
    )


def swap_z(values, number):
    ranks, group = lax.axis_size("dp"), lax.axis_size("tensor")
    pairs = []
    for rank in range(ranks):
        bit = (2, 1)[(rank + number) % 2]
        pairs += [(rank * group + peer, rank * group + (peer ^ bit)) for peer in range(group)]
    return lax.ppermute(values, ("dp", "tensor"), pairs)


def peer_of(place, sibling=False):
    core = lax.axis_index("dp") % 2
    if place in (1, 2):
        place = jnp.where(core == (1 if sibling else 0), place, 3 - place)
    return jnp.bitwise_xor(lax.axis_index("tensor"), place)


def turn_z(values, place, sibling=False):
    core = lax.axis_index("dp") % 2
    return jnp.where(
        core == (1 if sibling else 0), values, jnp.swapaxes(values, place, place + 1)
    )


def turn_axes(values, place):
    count = len(upper_bits())
    axes = list(range(values.ndim))
    axes[place : place + count] = [place + turns(1).index(bit) for bit in turns(0)]
    return values.transpose(axes)


def own_turns(values, place, sibling=False):
    core = lax.axis_index("dp") % 2
    return jnp.where(core == (1 if sibling else 0), values, turn_axes(values, place))


def rank_of(step, parts):
    core = step % 2
    rank = jnp.bitwise_xor(lax.axis_index("dp"), core)
    for number in range(len(upper_bits())):
        if parts[number]:
            rank = jnp.bitwise_xor(rank, turn_bit(number, core == 1))
    return rank


def tie(*arrays):
    return lax.optimization_barrier(arrays)


def grow(values, axis, bit, place, absolute):
    other = swap(values, axis, bit)
    if absolute:
        high = bit_set(axis, bit) == 1
        return jnp.stack(
            [jnp.where(high, other, values), jnp.where(high, values, other)], axis=place
        )
    return jnp.stack([values, other], axis=place)


def grow_bits(values, axis, bits, absolute):
    have = []
    for bit in bits:
        values = grow(values, axis, bit, sum(h > bit for h in have), absolute)
        have.append(bit)
    return values


def total(terms):
    summed = terms[0].astype(single)
    for term in terms[1:]:
        summed = summed + term.astype(single)
    return summed.astype(bfloat)


def pick_at(terms, place, number):
    return [lax.index_in_dim(term, number, place, keepdims=False) for term in terms]


def gather_z(piece, absolute):
    return grow_bits(piece, "tensor", [2, 1], absolute)


def grow_path(values):
    for number in range(len(upper_bits())):
        values = jnp.stack([values, swap_path(values, number)])
    return values


def reduce_z(values, bit, place):
    own = bit_set("tensor", bit)
    keep = lax.dynamic_index_in_dim(values, own, place, keepdims=False)
    send = lax.dynamic_index_in_dim(values, 1 - own, place, keepdims=False)
    return total([keep, swap(send, "tensor", bit)])


def halve_path(terms, number, place):
    other = swap_path(total(pick_at(terms, place, 1)), number)
    return pick_at(terms, place, 0) + [other]


def halve_z_once(terms, bit, place):
    place = place + 1 if bit == 1 else place
    other = swap_z(total(pick_at(terms, place, 1)), 1 if bit == 1 else 0)
    return pick_at(terms, place, 0) + [other]


def attention_rows(cols):
    rows = -(-3 * cols // lax.axis_size("dp"))
    return -(-rows // 16) * 16


def bits_of(number, count):
    return [(number >> place) % 2 for place in range(count)]


def row_cuts(rows, cols):
    return sorted({0, rows} | {end % rows for end in (cols, 2 * cols, 3 * cols)})


def assemble_kernel(ranks, group, rows, cols, own, *refs):
    sources, refs = refs[:4], refs[4:]
    *outs, out, sems, out_sems = refs
    me_z = lax.axis_index("tensor")
    cuts = row_cuts(rows, cols)
    count = len(upper_bits())
    copies = []

    def put(source, rank, peer, low, high):
        place = rank * rows + low
        if isinstance(place, int) and place >= 3 * cols:
            return
        kind = place // cols
        target = out.at[kind, peer, pl.ds(pl.multiple_of(place - kind * cols, 16), high - low)]
        copy = pltpu.make_async_copy(source, target, sems.at[len(copies)])
        copies.append((place < 3 * cols, copy))

    for low, high in zip(cuts[:-1], cuts[1:]):
        for rank in range(ranks):
            put(own.at[rank, low:high], rank, me_z, low, high)
        for step in range(ranks):
            place, upper = step // 2 // (ranks // 4), step // 2 % (ranks // 4)
            source = sources[2 * (step % 2) + place]
            rank = rank_of(step, bits_of(step // 2, count))
            for peer in range(1, group):
                put(
                    source.at[upper, peer - 1, low:high],
                    rank,
                    peer_of(peer, step % 2 == 1),
                    low,
                    high,
                )
    for move in ("start", "wait"):
        for live, copy in copies:

            @pl.when(live)
            def _():
                getattr(copy, move)()

    stores = [
        pltpu.make_async_copy(out.at[kind], outs[kind], out_sems.at[kind]) for kind in range(3)
    ]
    for copy in stores:
        copy.start()
    for copy in stores:
        copy.wait()


def assemble(own, parts, cols):
    ranks, rows, features = own.shape
    group = parts[0].shape[1] + 1
    count = (len(row_cuts(rows, cols)) - 1) * ranks * group
    anywhere = pl.BlockSpec(memory_space=pl.ANY)
    return pl.pallas_call(
        functools.partial(assemble_kernel, ranks, group, rows, cols),
        in_specs=[anywhere] * 5,
        out_specs=[anywhere] * 3,
        out_shape=[jax.ShapeDtypeStruct((group, cols, features), own.dtype)] * 3,
        scratch_shapes=[
            pltpu.VMEM((3, group, cols, features), own.dtype),
            pltpu.SemaphoreType.DMA((count,)),
            pltpu.SemaphoreType.DMA((3,)),
        ],
        compiler_params=pltpu.CompilerParams(vmem_limit_bytes=VMEM_BYTES),
        cost_estimate=pl.CostEstimate(
            flops=0, bytes_accessed=ranks * rows * group * features, transcendentals=0
        ),
    )(own, *parts)


def grads_kernel(ranks, group, rows, cols, pairs, *refs):
    inputs, (extra, keep, send, whole, block, sems) = refs[:-6], refs[-6:]
    count = len(upper_bits())
    for kind, (left, right) in enumerate(pairs):
        grad = dot_tn(inputs[left][...], inputs[right][...])
        each = cols // XHEAD
        for peer in range(group):
            if grad.shape[0] == group * cols:
                rows_here = grad[peer * cols : (peer + 1) * cols]
            else:
                for head in range(each):
                    place = (peer * each + head) * XLANE
                    block[head * XHEAD : (head + 1) * XHEAD, :] = grad[place : place + XHEAD]
                rows_here = block[...]
            whole[peer, kind * cols : (kind + 1) * cols, :] = rows_here.astype(bfloat)
    begin = len(pairs) * cols
    used = begin + extra.shape[1]
    for peer in range(group):
        whole[peer, begin:used, :] = extra[peer]
        if used < rows * ranks:
            whole[peer, used:, :] = jnp.zeros((rows * ranks - used, extra.shape[2]), bfloat)
    copies = []
    for step in range(ranks):
        parts = bits_of(step // 2, count)[::-1]
        place = pl.multiple_of(rank_of(step, parts) * rows, 16)
        for peer in range(group):
            source = whole.at[peer_of(peer, step % 2 == 1), pl.ds(place, rows)]
            target = (keep, send)[step % 2].at[step // 2, peer]
            copies.append(pltpu.make_async_copy(source, target, sems.at[len(copies)]))
    for copy in copies:
        copy.start()
    for copy in copies:
        copy.wait()


def grads_call(arrays, pairs, extra, rows, cols):
    ranks, group = lax.axis_size("dp"), lax.axis_size("tensor")
    features = extra.shape[-1]
    height = arrays[0].shape[0]
    inside = pl.BlockSpec(memory_space=pltpu.VMEM)
    anywhere = pl.BlockSpec(memory_space=pl.ANY)
    out = jax.ShapeDtypeStruct((ranks // 2, group, rows, features), bfloat)
    return list(pl.pallas_call(
        functools.partial(grads_kernel, ranks, group, rows, cols, pairs),
        in_specs=[inside] * (len(arrays) + 1),
        out_specs=[anywhere] * 2,
        out_shape=[out, out],
        scratch_shapes=[
            pltpu.VMEM((group, rows * ranks, features), bfloat),
            pltpu.VMEM((cols, features), single),
            pltpu.SemaphoreType.DMA((ranks * group,)),
        ],
        compiler_params=pltpu.CompilerParams(vmem_limit_bytes=VMEM_BYTES),
        cost_estimate=pl.CostEstimate(
            flops=height * features * features,
            bytes_accessed=group * rows * ranks * features // 2,
            transcendentals=0,
        ),
    )(*arrays, extra))


def core_terms(keep, send):
    shape = (2,) * (len(upper_bits()) + 2) + keep.shape[2:]
    return [keep.reshape(shape), swap(send, "dp", 1).reshape(shape)]


def flip_z(values, place):
    for number, bit in enumerate((2, 1)):
        values = jnp.where(
            bit_set("tensor", bit) == 1, jnp.flip(values, place + number), values
        )
    return values


def share_turn(piece, number):
    other = swap_path(piece, number)
    high = jnp.bitwise_and(lax.axis_index("dp"), turn_bit(number)) != 0
    return jnp.stack([jnp.where(high, other, piece), jnp.where(high, piece, other)])


def share_core(piece):
    count = len(upper_bits())
    other = turn_axes(swap(piece, "dp", 1), 0)
    high = lax.axis_index("dp") % 2 == 1
    piece = jnp.stack([jnp.where(high, other, piece), jnp.where(high, piece, other)], axis=count)
    return own_turns(piece, 0).reshape((lax.axis_size("dp"),) + piece.shape[count + 1 :])


def flip_dp(values, place):
    ranks = lax.axis_size("dp")
    shape = values.shape
    bits = upper_bits() + [1]
    bits.sort(reverse=True)
    values = values.reshape(shape[:place] + (2,) * len(bits) + shape[place + 1 :])
    for number, bit in enumerate(bits):
        values = jnp.where(
            bit_set("dp", bit) == 1, jnp.flip(values, place + number), values
        )
    return values.reshape(shape[:place] + (ranks,) + shape[place + 1 :])


def grid_table(bucket):
    grid_height = jnp.where(
        bucket == 0, SIDE, jnp.where(bucket == 1, 3 * SIDE // 4, 3 * SIDE // 2)
    ).astype(jnp.int32)
    grid_width = jnp.where(
        bucket == 0, SIDE, jnp.where(bucket == 1, 5 * SIDE // 4, 5 * SIDE // 8)
    ).astype(jnp.int32)
    return (grid_height, grid_width)


def inside_tap(inner_pos, grid_height, grid_width, row_step, col_step):
    grid_row = inner_pos // grid_width
    grid_col = inner_pos % grid_width
    return (
        (inner_pos < grid_height * grid_width)
        & (grid_row + row_step >= 0)
        & (grid_row + row_step < grid_height)
        & (grid_col + col_step >= 0)
        & (grid_col + col_step < grid_width)
    )


def look_up(table, item):
    known = item[:, None] == jnp.arange(table.shape[0], dtype=jnp.int32)[None, :]
    return jnp.sum(jnp.where(known, table[None, :], 0), axis=1)


def shift_blocks(slots, total, item_bucket, sign, limit):
    item = slots // ITEM_SLOTS
    inner = slots % ITEM_SLOTS
    height, width = grid_table(look_up(item_bucket, item))
    index = jnp.arange(slots.shape[0], dtype=jnp.int32)
    known = (slots >= 0) & (slots < total) & (index < limit)
    columns = jnp.arange(BLOCK + 2 * REACH, dtype=jnp.int32)
    taps = []
    for row_step in (-1, 0, 1):
        for col_step in (-1, 0, 1):
            down, right = sign * row_step, sign * col_step
            inside = known & inside_tap(inner, height, width, down, right)
            target = index % BLOCK + REACH + down * width + right
            taps.append(
                (columns[None, :] == target[:, None]) & inside[:, None]
            )
    return jnp.stack(taps, axis=0).astype(bfloat)


def fetch_weights(core, begin, steps, sources, held, sems):
    own, *others = sources
    rows = held.shape[-2]
    chunks = []
    for step in range(steps):
        first, second = (begin + step) // 2, (begin + step) % 2
        slot = step % 2
        rank = rank_of(core, (first, second))
        place = pl.multiple_of(rank * rows, 16)
        copies = []
        for kind in range(3):
            target = held.at[slot, kind]
            copies.append((own.at[kind, pl.ds(place, rows)], target.at[0]))
            copies.append(
                (others[second].at[first, :, kind * rows : (kind + 1) * rows], target.at[1:4])
            )
        chunks.append(
            [
                pltpu.make_async_copy(source, target, sems.at[slot, number])
                for number, (source, target) in enumerate(copies)
            ]
        )
    for step in range(steps):

        @pl.when(pl.program_id(0) == step)
        def _():
            if step == 0:
                for copy in chunks[0]:
                    copy.start()
            if step + 1 < steps:
                for copy in chunks[step + 1]:
                    copy.start()
            for copy in chunks[step]:
                copy.wait()


def ffn_kernel(
    core,
    begin,
    steps,
    adds,
    own_rows,
    own_pad,
    normed_ref,
    grad_ref,
    reach_ref,
    back_ref,
    last_ref,
    small_ref,
    *refs,
):
    count = 3 if core is not None else 1
    sources = refs[:count]
    added = None
    if adds:
        added = refs[count]
        count += 1
    ffn_ref, dnormed_ref, dweight_ref, dsmall_ref = refs[count : count + 4]
    active, slope, dconv, glu, dexpand, *buffers = refs[count + 4 :]

    def store_grad(kind, grad):
        if added is not None:
            grad = grad + added[0, kind].astype(single)
        dweight_ref[0, kind] = grad.astype(bfloat)

    if core is None:
        weight = lambda kind: sources[0][0, kind]
    else:
        held, sems = buffers
        fetch_weights(core, begin, steps, sources, held, sems)
        slot = lax.rem(pl.program_id(0), 2)
        weight = lambda kind: held[slot, kind].reshape(-1, held.shape[-1])
    @pl.when(pl.program_id(0) == 0)
    def _():
        ffn_ref[...] = jnp.zeros_like(ffn_ref)
        dnormed_ref[...] = jnp.zeros_like(dnormed_ref)

    normed = normed_ref[...]
    channels = small_ref.shape[2]
    for half in range(2):
        expand = dot_nt(normed, weight(half)) + small_ref[half, 10:11, :]
        sig = jax.nn.sigmoid(expand)
        active[half] = (expand * sig).astype(bfloat)
        mid, sig_mid = expand[2 * REACH : 2 * REACH + own_pad], sig[2 * REACH : 2 * REACH + own_pad]
        slope[half] = sig_mid * (1.0 + mid * (1.0 - sig_mid))
    dglu = dot_nt(grad_ref[...], weight(2))
    blocks = grad_ref.shape[0] // BLOCK
    for block in range(blocks):
        begin = block * BLOCK
        convs = []
        for half in range(2):
            moved = dot_nn(
                reach_ref[block], active[half, begin : begin + BLOCK + 2 * REACH, :]
            )
            total = small_ref[half, 9:10, :]
            for tap in range(9):
                total = total + moved[tap * BLOCK : (tap + 1) * BLOCK] * small_ref[half, tap : tap + 1, :]
            convs.append(total)
        value, gate = convs
        sig = jax.nn.sigmoid(gate)
        act = gate * sig
        grad = dglu[begin : begin + BLOCK]
        glu[begin : begin + BLOCK, :] = (value * act).astype(bfloat)
        dconv[0, begin : begin + BLOCK, :] = (grad * act).astype(bfloat)
        dconv[1, begin : begin + BLOCK, :] = (
            grad * value * (sig * (1.0 + gate * (1.0 - sig)))
        ).astype(bfloat)

    glu_own = glu[REACH : REACH + own_pad, :]
    if own_rows != own_pad:
        here = lax.broadcasted_iota(jnp.int32, (own_pad, channels), 0) < own_rows
        glu_own = jnp.where(here, glu_own.astype(single), 0.0).astype(bfloat)
    grad_own = grad_ref[REACH : REACH + own_pad, :]
    ffn_ref[...] += dot_nn(glu_own, weight(2))
    store_grad(2, dot_tn(glu_own, grad_own))
    normed_own = normed_ref[2 * REACH : 2 * REACH + own_pad, :]
    for half in range(2):
        dconv_own = dconv[half, REACH : REACH + own_pad, :].astype(single)
        if own_rows != own_pad:
            dconv_own = jnp.where(here, dconv_own, 0.0)
        dsmall_ref[half, 9:10, :] = jnp.sum(dconv_own, axis=0, keepdims=True)
        sums = [jnp.zeros((8, channels), single) for _ in range(9)]
        dbias = jnp.zeros((8, channels), single)
        for block in range(pl.cdiv(own_pad, BLOCK)):
            begin = block * BLOCK
            height = min(BLOCK, own_pad - begin)
            picks = back_ref[block] if height == BLOCK else last_ref[...]
            moved = dot_nn(picks, dconv[half, begin : begin + height + 2 * REACH, :])
            here_active = active[half, 2 * REACH + begin : 2 * REACH + begin + height, :].astype(single)
            total = jnp.zeros((height, channels), single)
            for tap in range(9):
                part = moved[tap * height : (tap + 1) * height]
                total = total + part * small_ref[half, tap : tap + 1, :]
                sums[tap] = sums[tap] + jnp.sum(
                    (part * here_active).reshape(height // 8, 8, channels), axis=0
                )
            grad = total * slope[half, begin : begin + height, :]
            dbias = dbias + jnp.sum(grad.reshape(height // 8, 8, channels), axis=0)
            dexpand[half, begin : begin + height, :] = grad.astype(bfloat)
        for tap in range(9):
            dsmall_ref[half, tap : tap + 1, :] = jnp.sum(sums[tap], axis=0, keepdims=True)
        dsmall_ref[half, 10:11, :] = jnp.sum(dbias, axis=0, keepdims=True)
        dsmall_ref[half, 11:16, :] = jnp.zeros((5, channels), single)
    for half in range(2):
        grad = dexpand[half]
        dnormed_ref[...] += dot_nn(grad, weight(half))
        store_grad(half, dot_tn(grad, normed_own))


def ffn_call(core, begin, steps, added, own_rows, own_pad, normed, grad, reach, back, last, weights, small):
    wide, features = normed.shape
    tall = grad.shape[0]
    channels = small.shape[2] // 4
    count = channels * steps
    direct = len(weights) > 1
    whole = lambda array: pl.BlockSpec(array.shape, lambda i: (0,) * array.ndim)
    rows = lambda base: pl.BlockSpec((1, 3, channels, features), lambda i: (i + base, 0, 0, 0))
    tiny = lambda base: pl.BlockSpec((2, 16, channels), lambda i: (0, 0, i + base))
    held = pl.BlockSpec((own_pad, features), lambda i: (0, 0))
    flops = 2 * count * features * (2 * wide + tall + 6 * own_pad) + 2 * count * 9 * 256 * 2 * (
        tall + own_pad
    )
    scratch = [
        pltpu.VMEM((2, wide, channels), bfloat),
        pltpu.VMEM((2, own_pad, channels), single),
        pltpu.VMEM((2, tall, channels), bfloat),
        pltpu.VMEM((tall, channels), bfloat),
        pltpu.VMEM((2, own_pad, channels), bfloat),
    ]
    if direct:
        group = weights[1].shape[1] + 1
        piece = weights[1].shape[2] // 3
        scratch += [
            pltpu.VMEM((2, 3, group, piece, features), bfloat),
            pltpu.SemaphoreType.DMA((2, 6)),
        ]
    return pl.pallas_call(
        functools.partial(
            ffn_kernel, core if direct else None, begin, steps, len(added) > 0, own_rows, own_pad
        ),
        grid=(steps,),
        in_specs=[whole(normed), whole(grad), whole(reach), whole(back), whole(last), tiny(begin)]
        + ([pl.BlockSpec(memory_space=pl.ANY)] * 3 if direct else [rows(begin)])
        + [rows(0)] * len(added),
        out_specs=[held, held, rows(0), tiny(0)],
        out_shape=[
            jax.ShapeDtypeStruct((own_pad, features), single),
            jax.ShapeDtypeStruct((own_pad, features), single),
            jax.ShapeDtypeStruct((steps, 3, channels, features), bfloat),
            jax.ShapeDtypeStruct((2, 16, count), single),
        ],
        scratch_shapes=scratch,
        compiler_params=pltpu.CompilerParams(vmem_limit_bytes=VMEM_BYTES),
        cost_estimate=pl.CostEstimate(
            flops=flops // 8, bytes_accessed=2 * count * features, transcendentals=count * tall // 4
        ),
    )(normed, grad, reach, back, last, small, *weights, *added)


def same_head():
    row = lax.broadcasted_iota(jnp.int32, (LANES, LANES), 0) // HEAD
    column = lax.broadcasted_iota(jnp.int32, (LANES, LANES), 1) // HEAD
    return row == column


def head_sums(left, right, extra):
    full = jnp.where(same_head(), dot_tn(left, right), 0.0)
    block = jnp.sum(full.reshape(LANES // HEAD, HEAD, LANES), axis=0)
    rest = jnp.zeros((TABLE - HEAD - 1, LANES), single)
    return jnp.concatenate([block, extra, rest], axis=0)


def head_blocks(table):
    tall = jnp.concatenate([table[:HEAD]] * (LANES // HEAD), axis=0)
    return jnp.where(same_head(), tall, 0.0).astype(bfloat)


def masked(values, column):
    return (values.astype(single) * column).astype(bfloat)


def softplus(values):
    return jnp.maximum(values, 0.0) + jnp.log1p(jnp.exp(-jnp.abs(values)))


def project_kernel(
    normed, wq, wk, wv, first, second, pre_q, pre_k, query, keys, values, table_1, table_2
):
    rows = normed[...]
    pre_q[...] = dot_nt(rows, wq[...])
    query[...] = softplus(pre_q[...]).astype(bfloat)
    pre_k[...] = dot_nt(rows, wk[...])
    key = softplus(pre_k[...]).astype(bfloat)
    keys[...] = key
    value = dot_nt(rows, wv[...]).astype(bfloat)
    values[...] = value
    for column, table in ((first, table_1), (second, table_2)):
        chosen = masked(key, column[...])
        table[...] = head_sums(
            chosen, value, jnp.sum(chosen.astype(single), axis=0, keepdims=True)
        )


def attend_kernel(query, state_1, state_2, first, second, wo, ratio, den, attn, out):
    @pl.when(pl.program_id(0) == 0)
    def _():
        out[...] = jnp.zeros_like(out)

    rows = query[...]
    parts = ((first[...], state_1[...]), (second[...], state_2[...]))
    numerator, weights = 0.0, 0.0
    for column, state in parts:
        numerator = numerator + dot_nn(masked(rows, column), head_blocks(state))
        weights = weights + column * state[HEAD : HEAD + 1]
    ones = same_head().astype(single).astype(bfloat)
    den[...] = dot_nn((rows.astype(single) * weights).astype(bfloat), ones)
    ratio[...] = numerator / den[...]
    attn[...] = ratio[...].astype(bfloat)
    out[...] += dot_nn(attn[...], wo[...])


def attend_back_kernel(
    grad, wo, ratio, den, query, pre_q, state_1, state_2, first, second, dquery, table_1, table_2
):
    dratio = dot_nt(grad[...], wo[...])
    ones = same_head().astype(single).astype(bfloat)
    dnumer = dratio / den[...]
    dden = -dot_nn((dratio * ratio[...]).astype(bfloat), ones) / den[...]
    rows = query[...]
    total_grad, weights = 0.0, 0.0
    for column, state, table in (
        (first[...], state_1[...], table_1),
        (second[...], state_2[...], table_2),
    ):
        chosen = (dnumer * column).astype(bfloat)
        total_grad = total_grad + dot_nt(chosen, head_blocks(state))
        weights = weights + column * state[HEAD : HEAD + 1]
        extra = jnp.sum(rows.astype(single) * dden * column, axis=0, keepdims=True)
        table[...] = head_sums(rows, chosen, extra)
    total_grad = total_grad + weights * dden
    dquery[...] = (total_grad * jax.nn.sigmoid(pre_q[...])).astype(bfloat)


def project_back_kernel(
    dquery, keys, values, pre_k, state_1, state_2, first, second, wq, wk, wv, dkeys, dvalues, dnormed
):
    @pl.when(pl.program_id(0) == 0)
    def _():
        dnormed[...] = jnp.zeros_like(dnormed)

    key_grad, value_grad = 0.0, 0.0
    for column, state in ((first[...], state_1[...]), (second[...], state_2[...])):
        block = head_blocks(state)
        key_grad = key_grad + dot_nt(masked(values[...], column), block)
        key_grad = key_grad + column * state[HEAD : HEAD + 1]
        value_grad = value_grad + dot_nn(masked(keys[...], column), block)
    dkeys[...] = (key_grad * jax.nn.sigmoid(pre_k[...])).astype(bfloat)
    dvalues[...] = value_grad.astype(bfloat)
    dnormed[...] += (
        dot_nn(dquery[...], wq[...]) + dot_nn(dkeys[...], wk[...]) + dot_nn(dvalues[...], wv[...])
    )


def lane_call(kernel, kinds, arrays, outs, rows, features):
    specs = {
        "l": pl.BlockSpec((rows, LANES), lambda g: (0, g)),
        "w": pl.BlockSpec((LANES, features), lambda g: (g, 0)),
        "t": pl.BlockSpec((TABLE, LANES), lambda g: (0, g)),
        "c": pl.BlockSpec((rows, 1), lambda g: (0, 0)),
        "a": pl.BlockSpec((rows, features), lambda g: (0, 0)),
    }
    shape = {"l": (rows, features), "t": (TABLE, features), "a": (rows, features)}
    return pl.pallas_call(
        kernel,
        grid=(features // LANES,),
        in_specs=[specs[kind] for kind in kinds],
        out_specs=[specs[kind] for kind, _ in outs],
        out_shape=[jax.ShapeDtypeStruct(shape[kind], dtype) for kind, dtype in outs],
        compiler_params=pltpu.CompilerParams(vmem_limit_bytes=VMEM_BYTES),
        cost_estimate=pl.CostEstimate(
            flops=rows * features * features, bytes_accessed=rows * features, transcendentals=0
        ),
    )(*arrays)


def head_probs(query, keys, lengths):
    scores = dot_nt(query, keys) * (XHEAD ** (-0.5))
    place = lax.broadcasted_iota(jnp.int32, scores.shape, 1)
    live = place < lengths
    scores = jnp.where(live, scores, -1e30)
    top = jnp.max(scores, axis=-1, keepdims=True)
    powers = jnp.exp(scores - top)
    return powers / jnp.sum(powers, axis=-1, keepdims=True)


def cross_kernel(query_ref, keys_ref, vals_ref, length_ref, mix_ref):
    probs = head_probs(query_ref[...], keys_ref[0], length_ref[...])
    mix_ref[...] = dot_nn(probs.astype(bfloat), vals_ref[0]).astype(bfloat)


def cross_back_kernel(
    query_ref, keys_ref, vals_ref, length_ref, dmix_ref, dquery_ref, dkeys_ref, dvals_ref, dbias_ref
):
    query, keys, dmix = query_ref[...], keys_ref[0], dmix_ref[...]
    probs = head_probs(query, keys, length_ref[...])
    dprobs = dot_nt(dmix, vals_ref[0])
    dvals_ref[0] = dot_tn(dmix, probs.astype(bfloat))[:XHEAD].astype(bfloat)
    row_dot = jnp.sum(probs * dprobs, axis=-1, keepdims=True)
    dscores = (probs * (dprobs - row_dot) * (XHEAD ** (-0.5))).astype(bfloat)
    dquery = dot_nn(dscores, keys)
    dbias_ref[...] = jnp.sum(dquery, axis=0, keepdims=True)
    dquery_ref[...] = dquery.astype(bfloat)
    dkeys_ref[0] = dot_tn(query, dscores)[:XHEAD].astype(bfloat)


def cross_specs(rows):
    lane = pl.BlockSpec((rows, XLANE), lambda h: (0, h))
    text = pl.BlockSpec((1, TXT_PAD, XLANE), lambda h: (h, 0, 0))
    length = pl.BlockSpec((rows, 1), lambda h: (0, 0))
    return lane, text, length


def cross_call(query, keys, vals, lengths):
    rows, heads = query.shape[0], keys.shape[0]
    lane, text, length = cross_specs(rows)
    return pl.pallas_call(
        cross_kernel,
        grid=(heads,),
        in_specs=[lane, text, text, length],
        out_specs=lane,
        out_shape=jax.ShapeDtypeStruct((rows, heads * XLANE), bfloat),
        compiler_params=pltpu.CompilerParams(vmem_limit_bytes=VMEM_BYTES),
        cost_estimate=pl.CostEstimate(
            flops=heads * rows * TXT_PAD * XLANE,
            bytes_accessed=2 * rows * heads * XLANE,
            transcendentals=heads * rows * TXT_PAD // 8,
        ),
    )(query, keys, vals, lengths)


def cross_back_call(query, keys, vals, lengths, dmix):
    rows, heads = query.shape[0], keys.shape[0]
    lane, text, length = cross_specs(rows)
    return pl.pallas_call(
        cross_back_kernel,
        grid=(heads,),
        in_specs=[lane, text, text, length, lane],
        out_specs=[
            lane,
            pl.BlockSpec((1, XHEAD, TXT_PAD), lambda h: (h, 0, 0)),
            pl.BlockSpec((1, XHEAD, TXT_PAD), lambda h: (h, 0, 0)),
            pl.BlockSpec((1, XLANE), lambda h: (0, h)),
        ],
        out_shape=[
            jax.ShapeDtypeStruct((rows, heads * XLANE), bfloat),
            jax.ShapeDtypeStruct((heads, XHEAD, TXT_PAD), bfloat),
            jax.ShapeDtypeStruct((heads, XHEAD, TXT_PAD), bfloat),
            jax.ShapeDtypeStruct((1, heads * XLANE), single),
        ],
        compiler_params=pltpu.CompilerParams(vmem_limit_bytes=VMEM_BYTES),
        cost_estimate=pl.CostEstimate(
            flops=heads * rows * TXT_PAD * XLANE,
            bytes_accessed=2 * rows * heads * XLANE,
            transcendentals=heads * rows * TXT_PAD // 8,
        ),
    )(query, keys, vals, lengths, dmix)


def norm_parts(values):
    centred = values - jnp.mean(values, axis=-1, keepdims=True)
    inv_std = lax.rsqrt(jnp.mean(centred * centred, axis=-1, keepdims=True) + norm_eps)
    return (centred * inv_std, inv_std)


def norm_back(grad_in, normal, inv_std, scale):
    scaled = grad_in * (1.0 + scale)
    return (
        scaled
        - jnp.mean(scaled, axis=-1, keepdims=True)
        - normal * jnp.mean(scaled * normal, axis=-1, keepdims=True)
    ) * inv_std


def pad_rows(values, rows):
    return jnp.pad(values, ((0, rows - values.shape[0]),) + ((0, 0),) * (values.ndim - 1))


def pad_heads(rows, heads):
    features = rows.shape[1]
    shaped = rows.reshape(heads, XHEAD, features)
    return jnp.pad(shaped, ((0, 0), (0, XLANE - XHEAD), (0, 0))).reshape(heads * XLANE, features)


def local(
    tokens,
    cotangent,
    item_bucket,
    text_len,
    t_mod,
    text_tokens,
    shift_table,
    w_qkv,
    w_out,
    out_bias,
    w_xq,
    xq_bias,
    w_xkv,
    xv_bias,
    w_xo,
    xo_bias,
    w_in,
    in_bias,
    dw_weight,
    dw_bias,
    w_pt,
):
    group = lax.axis_size("tensor")
    ranks = lax.axis_size("dp")
    me_z = lax.axis_index("tensor")
    me_d = lax.axis_index("dp")
    own_rows, width = tokens.shape
    own_pad = -(-own_rows // 32) * 32
    tall = -(-(own_rows + 2 * REACH) // BLOCK) * BLOCK
    wide = tall + 2 * REACH
    total_rows = own_rows * group * ranks
    item_count = t_mod.shape[0]
    heads = width // HEAD
    xheads = width // XHEAD
    cols = w_xq.shape[1]
    channels = w_in.shape[2]
    padded_channels = -(-channels // 384) * 384
    own_start = (me_d * group + me_z) * own_rows
    first_item = own_start // ITEM_SLOTS
    last_item = (own_start + own_rows - 1) // ITEM_SLOTS
    two_items = last_item != first_item

    bits = upper_bits()
    att_piece = attention_rows(cols)
    att_pad = att_piece * ranks
    att_rows = 3 * cols
    rows_qkv = pad_rows(w_qkv.transpose(1, 2, 0).reshape(att_rows, width), att_pad)
    rows_mix = pad_rows(jnp.concatenate([w_out, w_xq.T, w_xo], axis=0), att_pad)
    ffn_piece = padded_channels // ranks
    half_count = padded_channels * group // 2
    rows_ffn = jnp.stack(
        [pad_rows(rows, padded_channels) for rows in (w_in[:, 0].T, w_in[:, 1].T, w_pt)]
    )
    own_qkv = rows_qkv.reshape(ranks, att_piece, width)
    own_mix = rows_mix.reshape(ranks, att_piece, width)
    piece_1 = lax.dynamic_index_in_dim(own_qkv, me_d, 0, keepdims=False)
    piece_2 = lax.dynamic_index_in_dim(own_mix, me_d, 0, keepdims=False)

    def near_z(piece, far):
        near = swap_z(jnp.stack([piece, far]), 1)
        return jnp.stack([near[0], far, near[1]])

    def turn(values, number):
        return jnp.stack([values, swap_path(values, number)])

    def mid_turns(values):
        for number in range(1, len(bits) - 1):
            values = turn(values, number)
        return values.reshape((-1,) + values.shape[-3:])

    def last_turn(values):
        return swap_path(values, len(bits) - 1)

    own_slots = own_start + jnp.arange(own_rows, dtype=jnp.int32)
    item = own_slots // ITEM_SLOTS
    in_first = (item == first_item)[:, None]
    in_second = jnp.logical_not(in_first)
    mod_first = shift_table + lax.dynamic_index_in_dim(t_mod, first_item, 0, keepdims=False)
    mod_second = shift_table + lax.dynamic_index_in_dim(t_mod, last_item, 0, keepdims=False)
    row_mod = lambda number: jnp.where(in_first, mod_first[number][None], mod_second[number][None])
    shift_a, scale_a, gate_a, shift_f, scale_f, gate_f = [row_mod(number) for number in range(6)]
    tokens_f = tokens.astype(single)
    grad_out = cotangent.astype(single)
    normal_a, inv_std_a = norm_parts(tokens_f)
    normed = (normal_a * (1.0 + scale_a) + shift_a).astype(bfloat)

    far_1 = swap_z(piece_1, 0)
    far_1, normed = tie(far_1, normed)
    wave_1 = near_z(piece_1, far_1)
    wave_1, item_bucket, piece_2 = tie(wave_1, item_bucket, piece_2)
    far_2 = swap_z(piece_2, 0)
    wave_1 = turn(wave_1, 0)
    inner = own_slots % ITEM_SLOTS
    grid_h, grid_w = grid_table(look_up(item_bucket, item))
    valid = inner < grid_h * grid_w
    live = valid.astype(single)[:, None]
    tall_slots = own_start - REACH + jnp.arange(tall, dtype=jnp.int32)
    reach = shift_blocks(tall_slots, total_rows, item_bucket, 1, tall)
    reach = reach.reshape(9, tall // BLOCK, BLOCK, -1).transpose(1, 0, 2, 3)
    reach = reach.reshape(tall // BLOCK, 9 * BLOCK, -1)
    wave_1, reach, text_tokens = tie(wave_1, reach, text_tokens)
    wave_1 = mid_turns(wave_1)
    last_1 = last_turn(wave_1)
    core_1 = swap(wave_1, "dp", 1)
    wave_2 = near_z(piece_2, far_2)
    text_rows_here = text_tokens.shape[0]
    text_half = pad_rows(text_tokens, -(-text_rows_here // 16) * 16)
    text_half = lax.dynamic_index_in_dim(
        text_half.reshape(2, -1, width), me_d % 2, 0, keepdims=False
    )
    text_far = swap(text_half, "tensor", 2)
    pad_slots = own_start + jnp.arange(own_pad, dtype=jnp.int32)
    back = shift_blocks(pad_slots, total_rows, item_bucket, -1, own_rows)
    full_blocks = own_pad // BLOCK
    rest = own_pad - full_blocks * BLOCK
    back_full = back[:, : full_blocks * BLOCK].reshape(9, full_blocks, BLOCK, -1).transpose(1, 0, 2, 3)
    back_full = back_full.reshape(full_blocks, 9 * BLOCK, -1)
    rest = max(rest, 32)
    back_last = back[:, own_pad - rest :, : rest + 2 * REACH].reshape(9 * rest, -1)
    d_ffn = (grad_out * live * gate_f).astype(bfloat)
    wave_1, last_1, core_1, wave_2, back_full, back_last, d_ffn, text_far, rows_ffn = tie(
        wave_1, last_1, core_1, wave_2, back_full, back_last, d_ffn, text_far, rows_ffn
    )
    core_last_1 = swap(last_1, "dp", 1)
    piece_3 = lax.dynamic_slice_in_dim(rows_ffn, me_d * ffn_piece, ffn_piece, 1)
    piece_3 = piece_3.reshape(3 * ffn_piece, width)
    core_last_1, wave_2, piece_3 = tie(core_last_1, wave_2, piece_3)
    wave_2 = turn(wave_2, 0)
    far_3 = swap_z(piece_3, 0)
    text_near = swap(jnp.stack([text_half, text_far]), "tensor", 1)
    wq, wk, wv = [
        part.reshape(width, width) for part in assemble(own_qkv, (wave_1, last_1, core_1, core_last_1), cols)
    ]
    wq, wk, wv, wave_2, text_near = tie(wq, wk, wv, wave_2, text_near)
    wave_2 = mid_turns(wave_2)
    last_2 = last_turn(wave_2)
    core_2 = swap(wave_2, "dp", 1)
    in_order = lambda rel: [
        lax.dynamic_index_in_dim(rel, me_z ^ peer, 0, keepdims=False) for peer in range(group)
    ]
    by_core = lambda one, two: jnp.stack(
        [jnp.where(me_d % 2 == 0, one, two), jnp.where(me_d % 2 == 0, two, one)]
    )
    text_rel = jnp.stack([text_half, text_near[0], text_far, text_near[1]])
    text_other = swap(text_rel, "dp", 1)

    first_live = (in_first & valid[:, None]).astype(single)
    second_live = (in_second & valid[:, None]).astype(single)
    first_all, second_all = in_first.astype(single), in_second.astype(single)
    over_lanes = functools.partial(lane_call, rows=own_rows, features=width)
    pre_q, pre_k, query, keys, values, table_1, table_2 = over_lanes(
        project_kernel,
        "awwwcc",
        (normed, wq, wk, wv, first_live, second_live),
        (("l", single), ("l", single), ("l", bfloat), ("l", bfloat), ("l", bfloat), ("t", single), ("t", single)),
    )

    span_rows = own_rows * group
    span_start = me_d * span_rows
    span_first = span_start // ITEM_SLOTS
    span_last = (span_start + span_rows - 1) // ITEM_SLOTS
    span_items = (span_rows - 2) // ITEM_SLOTS + 2

    def item_table(first_part, second_part):
        parts = []
        for number in range(span_items):
            chosen = jnp.where(first_item - span_first == number, first_part, 0.0)
            also = two_items & (last_item - span_first == number)
            parts.append(chosen + jnp.where(also, second_part, 0.0))
        return jnp.stack(parts).astype(bfloat)

    def item_sums(table):
        count = ranks - 1
        tail_part = lax.dynamic_index_in_dim(table, span_last - span_first, 0, keepdims=False)
        below = lax.ppermute(tail_part, "dp", [(i, i + 1) for i in range(count)])
        above = lax.ppermute(table[0], "dp", [(i + 1, i) for i in range(count)])
        below_same = (span_start - 1) // ITEM_SLOTS == span_first
        above_same = (span_start + span_rows) // ITEM_SLOTS == span_last
        sums = []
        for number in (first_item, last_item):
            part = lax.dynamic_index_in_dim(table, number - span_first, 0, keepdims=False)
            part = part.astype(single)
            part = part + jnp.where(below_same & (number == span_first), below.astype(single), 0.0)
            part = part + jnp.where(above_same & (number == span_last), above.astype(single), 0.0)
            sums.append(part)
        return sums

    small_rel = jnp.concatenate([dw_weight, dw_bias[None], in_bias[None]], axis=0)
    small_rel = jnp.pad(small_rel, ((0, 5), (0, 0), (0, padded_channels - channels)))
    sizes = small_rel.size
    small_rel = jnp.concatenate([small_rel.reshape(-1), xq_bias]).astype(bfloat)
    small_tall = -(-small_rel.size // (32 * cols)) * 16
    small_rel = jnp.pad(small_rel, (0, 2 * small_tall * cols - small_rel.size))
    small_half = lax.dynamic_index_in_dim(
        small_rel.reshape(2, small_tall, cols), me_d % 2, 0, keepdims=False
    )
    down = tuple(range(2, 2 + len(bits)))

    table = item_table(table_1, table_2)
    table, text_other, far_3 = tie(table, text_other, far_3)
    table = total([table, swap_z(table, 0)])
    text_rel = by_core(text_rel, text_other).swapaxes(0, 1).reshape(group, -1, width)
    text_all = jnp.concatenate(in_order(text_rel[:, :text_rows_here]))
    text_kv = jnp.einsum("td,dke->tke", text_all, w_xkv, preferred_element_type=single)
    xkv_own = jnp.stack([text_kv[:, 0], text_kv[:, 1] + xv_bias], axis=0).astype(bfloat)
    both_half = jnp.concatenate(
        [lax.dynamic_index_in_dim(xkv_own, me_d % 2, 0, keepdims=False), small_half], axis=0
    )
    table, both_half, last_2, core_2 = tie(table, both_half, last_2, core_2)
    table = total([table, swap_z(table, 1)])
    both_far = swap(both_half, "tensor", 2)
    core_last_2 = swap(last_2, "dp", 1)
    table, both_far, core_last_2, far_3 = tie(table, both_far, core_last_2, far_3)
    state_1, state_2 = item_sums(table)
    wave_3 = near_z(piece_3, far_3)
    both_near = swap(jnp.stack([both_half, both_far]), "tensor", 1)
    wo, wxq, wxo = [
        part.reshape(width, width) for part in assemble(own_mix, (wave_2, last_2, core_2, core_last_2), cols)
    ]
    wxq_pad = pad_heads(wxq, xheads)
    wxo_pad = pad_heads(wxo, xheads)
    state_1, state_2, wo, wxq_pad, wxo_pad, both_near = tie(
        state_1, state_2, wo, wxq_pad, wxo_pad, both_near
    )
    both_rel = jnp.stack([both_half, both_near[0], both_far, both_near[1]])
    both_other = swap(both_rel, "dp", 1)
    attn_ratio, denominator, attn, attn_sum = over_lanes(
        attend_kernel,
        "lttccw",
        (query, state_1, state_2, first_all, second_all, wo),
        (("l", single), ("l", single), ("l", bfloat), ("a", single)),
    )
    attn_out = attn_sum + out_bias
    after_attn = tokens_f + live * gate_a * attn_out

    after_attn, wave_3, both_other = tie(after_attn, wave_3, both_other)
    wave_3 = turn(wave_3, 0)
    cross_in = after_attn.astype(bfloat)
    xq_product = dot_nt(cross_in, wxq_pad)
    both = by_core(both_rel, both_other)
    xkv_all = both[:, :, :TXT].swapaxes(0, 1)
    xkv_all = jnp.stack(in_order(xkv_all)).reshape(group, 2, TXT, cols // XHEAD, XHEAD)
    xkv_all = xkv_all.transpose(1, 0, 3, 2, 4).reshape(2, xheads, TXT, XHEAD)
    xkv_all = jnp.pad(xkv_all, ((0, 0), (0, 0), (0, TXT_PAD - TXT), (0, XLANE - XHEAD)))
    xkeys, xvals = xkv_all[0], xkv_all[1]
    small = both[:, :, TXT:].swapaxes(0, 1).reshape(group, -1).astype(single)
    xq_rel = small[:, sizes : sizes + cols]
    small = flip_dp(small[:, :sizes].reshape(group, 16, 2, ranks, ffn_piece), 3)
    small = small.reshape((group, 16, 2) + (2,) * (len(bits) + 1) + (ffn_piece,))
    small = jnp.moveaxis(small, 0, len(bits) + 3)
    small = small.transpose((len(bits) + 2, 1, 0) + down[::-1] + (len(bits) + 3, len(bits) + 4))
    small = small.reshape(small.shape[:-2] + (2, 2, ffn_piece))
    small = [
        turn_z(own_turns(small[core], 2, core == 1), 2 + len(bits), core == 1).reshape(
            2, 16, half_count
        )
        for core in (0, 1)
    ]
    xq_bias_all = jnp.stack(in_order(xq_rel)).reshape(xheads, XHEAD)
    xq_bias_all = jnp.pad(xq_bias_all, ((0, 0), (0, XLANE - XHEAD))).reshape(xheads * XLANE)
    lengths = look_up(text_len, item)[:, None]
    xquery = (xq_product + xq_bias_all).astype(bfloat)
    xquery, wave_3 = tie(xquery, wave_3)
    wave_3 = mid_turns(wave_3)
    last_3 = last_turn(wave_3)
    core_3 = swap(wave_3, "dp", 1)
    cross_mix = cross_call(xquery, xkeys, xvals, lengths)
    cross_out = dot_nn(cross_mix, wxo_pad) + xo_bias
    after_cross = after_attn + live * cross_out

    normal_f, inv_std_f = norm_parts(after_cross)
    normed_ffn = (normal_f * (1.0 + scale_f) + shift_f).astype(bfloat)
    normed_ffn, wave_3, last_3, core_3, *small = tie(normed_ffn, wave_3, last_3, core_3, *small)
    core_last_3 = swap(last_3, "dp", 1)
    def ffn_half(core):
        count = len(bits)
        own = flip_dp(rows_ffn.reshape(3, ranks, ffn_piece, width), 1)
        own = own.reshape((3,) + (2,) * (count + 1) + (ffn_piece, width))
        own = jnp.moveaxis(lax.index_in_dim(own, core, count + 1, keepdims=False), 0, count)
        own = own_turns(own.transpose(tuple(range(count))[::-1] + (count, count + 1, count + 2)), 0, core == 1)
        others = jnp.concatenate(((wave_3, last_3), (core_3, core_last_3))[core])
        others = others.reshape((2,) * count + (group - 1, 3, ffn_piece, width))
        others = others.transpose(tuple(range(count))[::-1] + tuple(range(count, count + 4)))
        joined = jnp.concatenate([jnp.expand_dims(own, count), others], axis=count)
        joined = jnp.moveaxis(joined, count + 1, 2)
        return joined.reshape(4, 3, half_count // 4, width)

    direct = ffn_piece % 16 == 0 and len(bits) == 2
    weights_ffn = [
        [rows_ffn, *((wave_3, last_3), (core_3, core_last_3))[core]] if direct else [ffn_half(core)]
        for core in (0, 1)
    ]

    above = shift_devices(
        jnp.concatenate([normed_ffn[own_rows - 2 * REACH :], d_ffn[own_rows - REACH :]], axis=0), 1
    )
    below = shift_devices(jnp.concatenate([normed_ffn[: 2 * REACH], d_ffn[:REACH]], axis=0), -1)
    normed_ext = pad_rows(
        jnp.concatenate([above[: 2 * REACH], normed_ffn, below[: 2 * REACH]], axis=0), wide
    )
    d_ffn_ext = pad_rows(
        jnp.concatenate([above[2 * REACH :], d_ffn, below[2 * REACH :]], axis=0), tall
    )
    tables = (reach, back_full, back_last)
    def ffn_part(core, begin, *added):
        return ffn_call(
            core, begin, 2, added, own_rows, own_pad, normed_ext, d_ffn_ext, *tables, weights_ffn[core], small[core]
        )

    part_3 = ffn_part(1, 2)
    normed_ext, *part_3 = tie(normed_ext, *part_3)
    other_3 = swap(part_3[2], "dp", 1)
    part_2 = ffn_part(1, 0)
    normed_ext, other_3, *part_2 = tie(normed_ext, other_3, *part_2)
    other_2 = swap(part_2[2], "dp", 1)
    part_1 = ffn_part(0, 2, other_3)
    normed_ext, other_2, *part_1 = tie(normed_ext, other_2, *part_1)
    turn_shape = (2, 3) + (2,) * len(bits) + (ffn_piece, width)
    ffn_got = swap_path(part_1[2], 0).reshape(turn_shape)
    part_0 = ffn_part(0, 0, other_2)
    parts = (part_0, part_1, part_2, part_3)
    ffn_out = sum(part[0] for part in parts)[:own_rows]
    d_normed_ffn = sum(part[1] for part in parts)[:own_rows]
    ffn_terms = [part_0[2].reshape(turn_shape), ffn_got]
    d_small_half = [
        jnp.concatenate([low[3], high[3]], axis=2) for low, high in ((part_0, part_1), (part_2, part_3))
    ]

    d_small = jnp.stack(
        [
            turn_z(
                own_turns(
                    part.astype(bfloat).reshape((2, 16) + (2,) * (len(bits) + 2) + (ffn_piece,)),
                    2,
                    core == 1,
                ),
                2 + len(bits),
                core == 1,
            )
            for core, part in enumerate(d_small_half)
        ],
        axis=len(bits) + 2,
    )
    order = (len(bits) + 3, len(bits) + 4, 0, 1) + down[::-1] + (len(bits) + 2, len(bits) + 5)
    d_small = flip_z(d_small.transpose(order), 0)
    d_small = d_small.reshape(group, 2, 16, ranks, ffn_piece)[:, :, :11]
    d_small = flip_dp(d_small, 3).reshape(group, -1)
    small_rows = -(-d_small.shape[1] // (16 * width)) * 16
    d_small = jnp.pad(d_small, ((0, 0), (0, small_rows * width - d_small.shape[1])))
    d_small = d_small.reshape(group, small_rows, width)

    out_tokens = (after_cross + live * gate_f * ffn_out).astype(bfloat)
    d_gate_f = grad_out * live * ffn_out
    grad_cross = grad_out + norm_back(d_normed_ffn, normal_f, inv_std_f, scale_f)

    d_cross = grad_cross * live
    d_xo_bias = jnp.sum(d_cross, axis=0)
    d_cross_low = d_cross.astype(bfloat)
    d_cross_low, ffn_terms[-1] = tie(d_cross_low, ffn_terms[-1])
    for stage in range(1, len(bits)):
        ffn_terms = halve_path(ffn_terms, stage, 0 if stage == 1 else 1)
    d_mix = dot_nt(d_cross_low, wxo_pad).astype(bfloat)
    d_query_low, d_keys, d_vals, d_xq_part = cross_back_call(xquery, xkeys, xvals, lengths, d_mix)
    d_query_low, ffn_terms[-1] = tie(d_query_low, ffn_terms[-1])
    ffn_terms = halve_z_once(ffn_terms, 1, 1)
    grad_attn = grad_cross + dot_nn(d_query_low, wxq_pad)

    d_attn_out = grad_attn * live * gate_a
    d_gate_a = grad_attn * live * attn_out
    d_out_bias = jnp.sum(d_attn_out, axis=0)
    d_attn_low = d_attn_out.astype(bfloat)

    text_rows = 2 * cols * TXT_PAD // width
    mix_rows = -(-(att_rows + text_rows + small_rows) // (16 * ranks)) * 16
    lanes = width // TXT_PAD
    d_kv = jnp.concatenate(
        [d_keys.reshape(group, cols, TXT_PAD), d_vals.reshape(group, cols, TXT_PAD)], axis=1
    )
    d_kv = jnp.concatenate(
        [d_kv[:, number * text_rows : (number + 1) * text_rows] for number in range(lanes)], axis=2
    )
    mix_arrays = [
        attn,
        d_attn_low,
        d_query_low,
        cross_in,
        cross_mix,
        d_cross_low,
    ]
    mix_extra = jnp.concatenate([d_kv, d_small], axis=1)
    d_query_in, table_1, table_2 = over_lanes(
        attend_back_kernel,
        "awllllttcc",
        (d_attn_low, wo, attn_ratio, denominator, query, pre_q, state_1, state_2, first_all, second_all),
        (("l", bfloat), ("t", single), ("t", single)),
    )
    d_table = item_table(table_1, table_2)
    def mod_sum(rows):
        return jnp.stack(
            [
                jnp.sum(jnp.where(in_first, rows, 0.0), axis=0),
                jnp.sum(jnp.where(in_second, rows, 0.0), axis=0),
            ]
        )

    d_table, mix_extra, ffn_terms[-1] = tie(d_table, mix_extra, ffn_terms[-1])
    d_table = total([d_table, swap_z(d_table, 0)])
    mod_sums = [
        mod_sum(rows) for rows in (d_gate_a, d_normed_ffn, d_normed_ffn * normal_f, d_gate_f)
    ]
    d_table, d_out_bias, d_xo_bias, *mod_sums = tie(d_table, d_out_bias, d_xo_bias, *mod_sums)
    d_table = total([d_table, swap_z(d_table, 1)])
    mix_grads = grads_call(mix_arrays, ((0, 1), (2, 3), (4, 5)), mix_extra, mix_rows, cols)
    d_table, mix_grads[1] = tie(d_table, mix_grads[1])
    mix_terms = core_terms(*mix_grads)
    d_state_1, d_state_2 = item_sums(d_table)
    d_state_1, d_state_2, mix_terms[1] = tie(d_state_1, d_state_2, mix_terms[1])
    mix_terms = halve_path(mix_terms, 0, 0)
    ffn_terms = halve_z_once(ffn_terms, 2, 1)
    d_keys_in, d_values_low, d_normed = over_lanes(
        project_back_kernel,
        "llllttccwww",
        (d_query_in, keys, values, pre_k, d_state_1, d_state_2, first_live, second_live, wq, wk, wv),
        (("l", bfloat), ("l", bfloat), ("a", single)),
    )
    d_tokens = grad_attn + norm_back(d_normed, normal_a, inv_std_a, scale_a)

    sums = jnp.stack([mod_sum(d_normed), mod_sum(d_normed * normal_a)] + mod_sums, axis=1)
    items = jnp.arange(item_count, dtype=jnp.int32)[:, None, None]
    mod_table = jnp.where(items == first_item, sums[0][None], 0.0) + jnp.where(
        (items == first_item + 1), sums[1][None], 0.0
    )
    xq_row = d_xq_part.reshape(xheads, XLANE)[:, :XHEAD].reshape(width)
    rows_all = jnp.concatenate(
        [mod_table.reshape(-1, width), jnp.stack([d_out_bias, d_xo_bias, xq_row], axis=0)], axis=0
    )
    rows_count = rows_all.shape[0]
    last_rows = -(-(att_rows + rows_count) // (16 * ranks)) * 16
    spare = -(-rows_count // 16) * 16
    rows_all = pad_rows(rows_all.astype(bfloat), spare)
    rows_all = jnp.broadcast_to(rows_all[None], (group, spare, width))

    rows_all, mix_terms[-1] = tie(rows_all, mix_terms[-1])
    for stage in range(1, len(bits)):
        mix_terms = halve_path(mix_terms, stage, 0)
    qkv_grads = grads_call(
        [d_query_in, d_keys_in, d_values_low, normed],
        ((0, 3), (1, 3), (2, 3)),
        rows_all,
        last_rows,
        cols,
    )
    qkv_grads[1], ffn_terms[-1], mix_terms[-1] = tie(qkv_grads[1], ffn_terms[-1], mix_terms[-1])
    qkv_terms = core_terms(*qkv_grads)
    qkv_terms[1], mix_terms[-1] = tie(qkv_terms[1], mix_terms[-1])
    qkv_terms = halve_path(qkv_terms, 0, 0)
    mix_terms = halve_z_once(mix_terms, 1, 0)
    qkv_terms[-1], mix_terms[-1] = tie(qkv_terms[-1], mix_terms[-1])
    for stage in range(1, len(bits)):
        qkv_terms = halve_path(qkv_terms, stage, 0)
    mix_terms = halve_z_once(mix_terms, 2, 0)
    qkv_terms[-1], mix_terms[-1], *ffn_terms = tie(qkv_terms[-1], mix_terms[-1], *ffn_terms)
    qkv_terms = halve_z_once(qkv_terms, 1, 0)
    d_mix_all = share_turn(total(mix_terms), 0)
    d_ffn_all = share_turn(total(ffn_terms), 0)
    qkv_terms[-1], d_mix_all, d_ffn_all = tie(qkv_terms[-1], d_mix_all, d_ffn_all)
    qkv_terms = halve_z_once(qkv_terms, 2, 0)
    for stage in range(1, len(bits)):
        d_mix_all = share_turn(d_mix_all, stage)
    qkv_terms[-1], d_mix_all = tie(qkv_terms[-1], d_mix_all)
    d_qkv_all = share_turn(total(qkv_terms), 0)
    d_mix_all = share_core(d_mix_all)
    for stage in range(1, len(bits)):
        d_ffn_all = share_turn(d_ffn_all, stage)
    d_qkv_all, d_mix_all, d_ffn_all = tie(d_qkv_all, d_mix_all, d_ffn_all)
    for stage in range(1, len(bits)):
        d_qkv_all = share_turn(d_qkv_all, stage)
    d_ffn_all = share_core(d_ffn_all)
    d_mix_all = d_mix_all.reshape(-1, width)
    d_kv = d_mix_all[att_rows : att_rows + text_rows]
    d_kv = jnp.concatenate(
        [d_kv[:, number * TXT_PAD : (number + 1) * TXT_PAD] for number in range(lanes)], axis=0
    )
    d_kv = d_kv.reshape(2, cols, TXT_PAD)[:, :, :TXT]
    d_xv_bias = jnp.sum(d_kv[1].astype(single), axis=1)
    d_w_xkv = jnp.einsum("td,ket->dke", text_all, d_kv, preferred_element_type=single)
    d_text = jnp.einsum("ket,dke->td", d_kv, w_xkv, preferred_element_type=single)
    d_text = reduce_z(d_text.astype(bfloat).reshape(2, 2, TXT // group, width), 1, 1)
    d_qkv_all, d_ffn_all, d_text = tie(d_qkv_all, d_ffn_all, d_text)
    d_qkv_all = share_core(d_qkv_all)
    d_text = reduce_z(d_text, 2, 0).astype(single)
    d_ffn_all = d_ffn_all.transpose(1, 0, 2, 3)
    d_ffn_all = d_ffn_all.reshape(3, padded_channels, width)[:, :channels]
    d_w_in = jnp.stack([d_ffn_all[0].T, d_ffn_all[1].T], axis=1).astype(single)
    d_w_pt = d_ffn_all[2].astype(single)

    d_w_out = d_mix_all[:cols].astype(single)
    d_w_xq = d_mix_all[cols : 2 * cols].T.astype(single)
    d_w_xo = d_mix_all[2 * cols : 3 * cols].astype(single)
    d_small = d_mix_all[att_rows + text_rows : att_rows + text_rows + small_rows].reshape(-1)
    d_small = d_small[: 22 * padded_channels].reshape(2, 11, padded_channels)[:, :, :channels]
    d_small = d_small.swapaxes(0, 1).astype(single)
    d_dw_weight, d_dw_bias, d_in_bias = d_small[:9], d_small[9], d_small[10]

    d_qkv_all = d_qkv_all.reshape(-1, width)
    d_w_qkv = d_qkv_all[:att_rows].reshape(3, cols, width).transpose(2, 0, 1).astype(single)
    rows_all = d_qkv_all[att_rows : att_rows + rows_count].astype(single)
    d_t_mod = rows_all[:-3].reshape(mod_table.shape)
    d_out_bias, d_xo_bias = rows_all[-3], rows_all[-2]
    d_xq_bias = lax.dynamic_slice_in_dim(rows_all[-1], me_z * cols, cols, 0)
    d_shift_table = jnp.sum(d_t_mod, axis=0)
    return (
        out_tokens,
        d_tokens,
        d_t_mod,
        d_text,
        d_shift_table,
        d_w_qkv,
        d_w_out,
        d_out_bias,
        d_w_xq,
        d_xq_bias,
        d_w_xkv,
        d_xv_bias,
        d_w_xo,
        d_xo_bias,
        d_w_in,
        d_in_bias,
        d_dw_weight,
        d_dw_bias,
        d_w_pt,
    )


def solution(mesh):
    rows = P(("dp", "tensor"), None)
    placed = (
        rows,
        rows,
        P(),
        P(),
        P(),
        P("tensor", None),
        P(),
        P(None, None, "tensor"),
        P("tensor", None),
        P(),
        P(None, "tensor"),
        P("tensor"),
        P(None, None, "tensor"),
        P("tensor"),
        P("tensor", None),
        P(),
        P(None, None, "tensor"),
        P(None, "tensor"),
        P(None, None, "tensor"),
        P(None, "tensor"),
        P("tensor", None),
    )
    return jax.shard_map(
        local,
        mesh=mesh,
        in_specs=placed,
        out_specs=(
            rows,
            rows,
            P(),
            P("tensor", None),
            P(),
            P(None, None, "tensor"),
            P("tensor", None),
            P(),
            P(None, "tensor"),
            P("tensor"),
            P(None, None, "tensor"),
            P("tensor"),
            P("tensor", None),
            P(),
            P(None, None, "tensor"),
            P(None, "tensor"),
            P(None, None, "tensor"),
            P(None, "tensor"),
            P("tensor", None),
        ),
        check_vma=False,
    )
```

```python
import functools

import jax
import jax.numpy as jnp
from jax import lax
from jax.experimental import pallas as pl
from jax.experimental.pallas import tpu as pltpu
from jax.sharding import PartitionSpec as P

HEAD = 32
XHEAD = 72
XLANE = 128
TXT = 300
TXT_PAD = 384
SIDE = 32
ITEM_SLOTS = 1024
REACH = 48
BLOCK = 128
LANES = 384
TABLE = 40

norm_eps = 1e-06
bfloat = jnp.bfloat16
single = jnp.float32
VMEM_BYTES = 60 * 1024 * 1024


def dot_nn(a, b):
    return lax.dot_general(a, b, (((1,), (0,)), ((), ())), preferred_element_type=single)


def dot_nt(a, b):
    return lax.dot_general(a, b, (((1,), (1,)), ((), ())), preferred_element_type=single)


def dot_tn(a, b):
    return lax.dot_general(a, b, (((0,), (0,)), ((), ())), preferred_element_type=single)


def swap(values, axis, bit):
    count = lax.axis_size(axis)
    return lax.ppermute(values, axis, [(i, i ^ bit) for i in range(count)])


def shift_devices(values, step):
    count = lax.axis_size("dp") * lax.axis_size("tensor")
    pairs = [(i, i + step) for i in range(count) if 0 <= i + step < count]
    return lax.ppermute(values, ("dp", "tensor"), pairs)


def bit_set(axis, bit):
    return (lax.axis_index(axis) // bit) % 2


def upper_bits():
    count = lax.axis_size("dp")
    bits = []
    bit = 2
    while bit < count:
        bits.append(bit)
        bit *= 2
    return bits


def turns(core):
    bits = upper_bits()
    cut = len(bits) // 2
    return bits[cut:] + bits[:cut] if core else bits


def turn_bit(number, sibling=False):
    core = lax.axis_index("dp") % 2
    first, second = turns(0)[number], turns(1)[number]
    return jnp.where(core == (1 if sibling else 0), first, second)


def swap_path(values, number):
    count = lax.axis_size("dp")
    return lax.ppermute(
        values, "dp", [(i, i ^ turns(i % 2)[number]) for i in range(count)]
    )


def swap_z(values, number):
    ranks, group = lax.axis_size("dp"), lax.axis_size("tensor")
    pairs = []
    for rank in range(ranks):
        bit = (2, 1)[(rank + number) % 2]
        pairs += [(rank * group + peer, rank * group + (peer ^ bit)) for peer in range(group)]
    return lax.ppermute(values, ("dp", "tensor"), pairs)


def peer_of(place, sibling=False):
    core = lax.axis_index("dp") % 2
    if place in (1, 2):
        place = jnp.where(core == (1 if sibling else 0), place, 3 - place)
    return jnp.bitwise_xor(lax.axis_index("tensor"), place)


def turn_z(values, place, sibling=False):
    core = lax.axis_index("dp") % 2
    return jnp.where(
        core == (1 if sibling else 0), values, jnp.swapaxes(values, place, place + 1)
    )


def turn_axes(values, place):
    count = len(upper_bits())
    axes = list(range(values.ndim))
    axes[place : place + count] = [place + turns(1).index(bit) for bit in turns(0)]
    return values.transpose(axes)


def own_turns(values, place, sibling=False):
    core = lax.axis_index("dp") % 2
    return jnp.where(core == (1 if sibling else 0), values, turn_axes(values, place))


def rank_of(step, parts):
    core = step % 2
    rank = jnp.bitwise_xor(lax.axis_index("dp"), core)
    for number in range(len(upper_bits())):
        if parts[number]:
            rank = jnp.bitwise_xor(rank, turn_bit(number, core == 1))
    return rank


def tie(*arrays):
    return lax.optimization_barrier(arrays)


def grow(values, axis, bit, place, absolute):
    other = swap(values, axis, bit)
    if absolute:
        high = bit_set(axis, bit) == 1
        return jnp.stack(
            [jnp.where(high, other, values), jnp.where(high, values, other)], axis=place
        )
    return jnp.stack([values, other], axis=place)


def grow_bits(values, axis, bits, absolute):
    have = []
    for bit in bits:
        values = grow(values, axis, bit, sum(h > bit for h in have), absolute)
        have.append(bit)
    return values


def total(terms):
    summed = terms[0].astype(single)
    for term in terms[1:]:
        summed = summed + term.astype(single)
    return summed.astype(bfloat)


def pick_at(terms, place, number):
    return [lax.index_in_dim(term, number, place, keepdims=False) for term in terms]


def gather_z(piece, absolute):
    return grow_bits(piece, "tensor", [2, 1], absolute)


def grow_path(values):
    for number in range(len(upper_bits())):
        values = jnp.stack([values, swap_path(values, number)])
    return values


def reduce_z(values, bit, place):
    own = bit_set("tensor", bit)
    keep = lax.dynamic_index_in_dim(values, own, place, keepdims=False)
    send = lax.dynamic_index_in_dim(values, 1 - own, place, keepdims=False)
    return total([keep, swap(send, "tensor", bit)])


def halve_path(terms, number, place):
    other = swap_path(total(pick_at(terms, place, 1)), number)
    return pick_at(terms, place, 0) + [other]


def halve_z_once(terms, bit, place):
    place = place + 1 if bit == 1 else place
    other = swap_z(total(pick_at(terms, place, 1)), 1 if bit == 1 else 0)
    return pick_at(terms, place, 0) + [other]


def attention_rows(cols):
    rows = -(-3 * cols // lax.axis_size("dp"))
    return -(-rows // 16) * 16


def bits_of(number, count):
    return [(number >> place) % 2 for place in range(count)]


def row_cuts(rows, cols):
    return sorted({0, rows} | {end % rows for end in (cols, 2 * cols, 3 * cols)})


def assemble_kernel(ranks, group, rows, cols, own, *refs):
    sources, refs = refs[:4], refs[4:]
    *outs, out, sems, out_sems = refs
    me_z = lax.axis_index("tensor")
    cuts = row_cuts(rows, cols)
    count = len(upper_bits())
    copies = []

    def put(source, rank, peer, low, high):
        place = rank * rows + low
        if isinstance(place, int) and place >= 3 * cols:
            return
        kind = place // cols
        target = out.at[kind, peer, pl.ds(pl.multiple_of(place - kind * cols, 16), high - low)]
        copy = pltpu.make_async_copy(source, target, sems.at[len(copies)])
        copies.append((place < 3 * cols, copy))

    for low, high in zip(cuts[:-1], cuts[1:]):
        for rank in range(ranks):
            put(own.at[rank, low:high], rank, me_z, low, high)
        for step in range(ranks):
            place, upper = step // 2 // (ranks // 4), step // 2 % (ranks // 4)
            source = sources[2 * (step % 2) + place]
            rank = rank_of(step, bits_of(step // 2, count))
            for peer in range(1, group):
                put(
                    source.at[upper, peer - 1, low:high],
                    rank,
                    peer_of(peer, step % 2 == 1),
                    low,
                    high,
                )
    for move in ("start", "wait"):
        for live, copy in copies:

            @pl.when(live)
            def _():
                getattr(copy, move)()

    stores = [
        pltpu.make_async_copy(out.at[kind], outs[kind], out_sems.at[kind]) for kind in range(3)
    ]
    for copy in stores:
        copy.start()
    for copy in stores:
        copy.wait()


def assemble(own, parts, cols):
    ranks, rows, features = own.shape
    group = parts[0].shape[1] + 1
    count = (len(row_cuts(rows, cols)) - 1) * ranks * group
    anywhere = pl.BlockSpec(memory_space=pl.ANY)
    return pl.pallas_call(
        functools.partial(assemble_kernel, ranks, group, rows, cols),
        in_specs=[anywhere] * 5,
        out_specs=[anywhere] * 3,
        out_shape=[jax.ShapeDtypeStruct((group, cols, features), own.dtype)] * 3,
        scratch_shapes=[
            pltpu.VMEM((3, group, cols, features), own.dtype),
            pltpu.SemaphoreType.DMA((count,)),
            pltpu.SemaphoreType.DMA((3,)),
        ],
        compiler_params=pltpu.CompilerParams(vmem_limit_bytes=VMEM_BYTES),
        cost_estimate=pl.CostEstimate(
            flops=0, bytes_accessed=ranks * rows * group * features, transcendentals=0
        ),
    )(own, *parts)


def grads_kernel(ranks, group, rows, cols, pairs, *refs):
    inputs, (extra, keep, send, whole, block, sems) = refs[:-6], refs[-6:]
    count = len(upper_bits())
    for kind, (left, right) in enumerate(pairs):
        grad = dot_tn(inputs[left][...], inputs[right][...])
        each = cols // XHEAD
        for peer in range(group):
            if grad.shape[0] == group * cols:
                rows_here = grad[peer * cols : (peer + 1) * cols]
            else:
                for head in range(each):
                    place = (peer * each + head) * XLANE
                    block[head * XHEAD : (head + 1) * XHEAD, :] = grad[place : place + XHEAD]
                rows_here = block[...]
            whole[peer, kind * cols : (kind + 1) * cols, :] = rows_here.astype(bfloat)
    begin = len(pairs) * cols
    used = begin + extra.shape[1]
    for peer in range(group):
        whole[peer, begin:used, :] = extra[peer]
        if used < rows * ranks:
            whole[peer, used:, :] = jnp.zeros((rows * ranks - used, extra.shape[2]), bfloat)
    copies = []
    for step in range(ranks):
        parts = bits_of(step // 2, count)[::-1]
        place = pl.multiple_of(rank_of(step, parts) * rows, 16)
        for peer in range(group):
            source = whole.at[peer_of(peer, step % 2 == 1), pl.ds(place, rows)]
            target = (keep, send)[step % 2].at[step // 2, peer]
            copies.append(pltpu.make_async_copy(source, target, sems.at[len(copies)]))
    for copy in copies:
        copy.start()
    for copy in copies:
        copy.wait()


def grads_call(arrays, pairs, extra, rows, cols):
    ranks, group = lax.axis_size("dp"), lax.axis_size("tensor")
    features = extra.shape[-1]
    height = arrays[0].shape[0]
    inside = pl.BlockSpec(memory_space=pltpu.VMEM)
    anywhere = pl.BlockSpec(memory_space=pl.ANY)
    out = jax.ShapeDtypeStruct((ranks // 2, group, rows, features), bfloat)
    return list(pl.pallas_call(
        functools.partial(grads_kernel, ranks, group, rows, cols, pairs),
        in_specs=[inside] * (len(arrays) + 1),
        out_specs=[anywhere] * 2,
        out_shape=[out, out],
        scratch_shapes=[
            pltpu.VMEM((group, rows * ranks, features), bfloat),
            pltpu.VMEM((cols, features), single),
            pltpu.SemaphoreType.DMA((ranks * group,)),
        ],
        compiler_params=pltpu.CompilerParams(vmem_limit_bytes=VMEM_BYTES),
        cost_estimate=pl.CostEstimate(
            flops=height * features * features,
            bytes_accessed=group * rows * ranks * features // 2,
            transcendentals=0,
        ),
    )(*arrays, extra))


def core_terms(keep, send):
    shape = (2,) * (len(upper_bits()) + 2) + keep.shape[2:]
    return [keep.reshape(shape), swap(send, "dp", 1).reshape(shape)]


def flip_z(values, place):
    for number, bit in enumerate((2, 1)):
        values = jnp.where(
            bit_set("tensor", bit) == 1, jnp.flip(values, place + number), values
        )
    return values


def share_turn(piece, number):
    other = swap_path(piece, number)
    high = jnp.bitwise_and(lax.axis_index("dp"), turn_bit(number)) != 0
    return jnp.stack([jnp.where(high, other, piece), jnp.where(high, piece, other)])


def share_core(piece):
    count = len(upper_bits())
    other = turn_axes(swap(piece, "dp", 1), 0)
    high = lax.axis_index("dp") % 2 == 1
    piece = jnp.stack([jnp.where(high, other, piece), jnp.where(high, piece, other)], axis=count)
    return own_turns(piece, 0).reshape((lax.axis_size("dp"),) + piece.shape[count + 1 :])


def flip_dp(values, place):
    ranks = lax.axis_size("dp")
    shape = values.shape
    bits = upper_bits() + [1]
    bits.sort(reverse=True)
    values = values.reshape(shape[:place] + (2,) * len(bits) + shape[place + 1 :])
    for number, bit in enumerate(bits):
        values = jnp.where(
            bit_set("dp", bit) == 1, jnp.flip(values, place + number), values
        )
    return values.reshape(shape[:place] + (ranks,) + shape[place + 1 :])


def grid_table(bucket):
    grid_height = jnp.where(
        bucket == 0, SIDE, jnp.where(bucket == 1, 3 * SIDE // 4, 3 * SIDE // 2)
    ).astype(jnp.int32)
    grid_width = jnp.where(
        bucket == 0, SIDE, jnp.where(bucket == 1, 5 * SIDE // 4, 5 * SIDE // 8)
    ).astype(jnp.int32)
    return (grid_height, grid_width)


def inside_tap(inner_pos, grid_height, grid_width, row_step, col_step):
    grid_row = inner_pos // grid_width
    grid_col = inner_pos % grid_width
    return (
        (inner_pos < grid_height * grid_width)
        & (grid_row + row_step >= 0)
        & (grid_row + row_step < grid_height)
        & (grid_col + col_step >= 0)
        & (grid_col + col_step < grid_width)
    )


def look_up(table, item):
    known = item[:, None] == jnp.arange(table.shape[0], dtype=jnp.int32)[None, :]
    return jnp.sum(jnp.where(known, table[None, :], 0), axis=1)


def shift_blocks(slots, total, item_bucket, sign, limit):
    item = slots // ITEM_SLOTS
    inner = slots % ITEM_SLOTS
    height, width = grid_table(look_up(item_bucket, item))
    index = jnp.arange(slots.shape[0], dtype=jnp.int32)
    known = (slots >= 0) & (slots < total) & (index < limit)
    columns = jnp.arange(BLOCK + 2 * REACH, dtype=jnp.int32)
    taps = []
    for row_step in (-1, 0, 1):
        for col_step in (-1, 0, 1):
            down, right = sign * row_step, sign * col_step
            inside = known & inside_tap(inner, height, width, down, right)
            target = index % BLOCK + REACH + down * width + right
            taps.append(
                (columns[None, :] == target[:, None]) & inside[:, None]
            )
    return jnp.stack(taps, axis=0).astype(bfloat)


def fetch_weights(core, begin, steps, sources, held, sems):
    own, *others = sources
    rows = held.shape[-2]
    chunks = []
    for step in range(steps):
        first, second = (begin + step) // 2, (begin + step) % 2
        slot = step % 2
        rank = rank_of(core, (first, second))
        place = pl.multiple_of(rank * rows, 16)
        copies = []
        for kind in range(3):
            target = held.at[slot, kind]
            copies.append((own.at[kind, pl.ds(place, rows)], target.at[0]))
            copies.append(
                (others[second].at[first, :, kind * rows : (kind + 1) * rows], target.at[1:4])
            )
        chunks.append(
            [
                pltpu.make_async_copy(source, target, sems.at[slot, number])
                for number, (source, target) in enumerate(copies)
            ]
        )
    for step in range(steps):

        @pl.when(pl.program_id(0) == step)
        def _():
            if step == 0:
                for copy in chunks[0]:
                    copy.start()
            if step + 1 < steps:
                for copy in chunks[step + 1]:
                    copy.start()
            for copy in chunks[step]:
                copy.wait()


def ffn_kernel(
    core,
    begin,
    steps,
    adds,
    own_rows,
    own_pad,
    normed_ref,
    grad_ref,
    reach_ref,
    back_ref,
    last_ref,
    small_ref,
    *refs,
):
    count = 3 if core is not None else 1
    sources = refs[:count]
    added = None
    if adds:
        added = refs[count]
        count += 1
    ffn_ref, dnormed_ref, dweight_ref, dsmall_ref = refs[count : count + 4]
    active, slope, dconv, glu, dexpand, *buffers = refs[count + 4 :]

    def store_grad(kind, grad):
        if added is not None:
            grad = grad + added[0, kind].astype(single)
        dweight_ref[0, kind] = grad.astype(bfloat)

    if core is None:
        weight = lambda kind: sources[0][0, kind]
    else:
        held, sems = buffers
        fetch_weights(core, begin, steps, sources, held, sems)
        slot = lax.rem(pl.program_id(0), 2)
        weight = lambda kind: held[slot, kind].reshape(-1, held.shape[-1])
    @pl.when(pl.program_id(0) == 0)
    def _():
        ffn_ref[...] = jnp.zeros_like(ffn_ref)
        dnormed_ref[...] = jnp.zeros_like(dnormed_ref)

    normed = normed_ref[...]
    channels = small_ref.shape[2]
    for half in range(2):
        expand = dot_nt(normed, weight(half)) + small_ref[half, 10:11, :]
        sig = jax.nn.sigmoid(expand)
        active[half] = (expand * sig).astype(bfloat)
        mid, sig_mid = expand[2 * REACH : 2 * REACH + own_pad], sig[2 * REACH : 2 * REACH + own_pad]
        slope[half] = sig_mid * (1.0 + mid * (1.0 - sig_mid))
    dglu = dot_nt(grad_ref[...], weight(2))
    blocks = grad_ref.shape[0] // BLOCK
    for block in range(blocks):
        begin = block * BLOCK
        convs = []
        for half in range(2):
            moved = dot_nn(
                reach_ref[block], active[half, begin : begin + BLOCK + 2 * REACH, :]
            )
            total = small_ref[half, 9:10, :]
            for tap in range(9):
                total = total + moved[tap * BLOCK : (tap + 1) * BLOCK] * small_ref[half, tap : tap + 1, :]
            convs.append(total)
        value, gate = convs
        sig = jax.nn.sigmoid(gate)
        act = gate * sig
        grad = dglu[begin : begin + BLOCK]
        glu[begin : begin + BLOCK, :] = (value * act).astype(bfloat)
        dconv[0, begin : begin + BLOCK, :] = (grad * act).astype(bfloat)
        dconv[1, begin : begin + BLOCK, :] = (
            grad * value * (sig * (1.0 + gate * (1.0 - sig)))
        ).astype(bfloat)

    glu_own = glu[REACH : REACH + own_pad, :]
    if own_rows != own_pad:
        here = lax.broadcasted_iota(jnp.int32, (own_pad, channels), 0) < own_rows
        glu_own = jnp.where(here, glu_own.astype(single), 0.0).astype(bfloat)
    grad_own = grad_ref[REACH : REACH + own_pad, :]
    ffn_ref[...] += dot_nn(glu_own, weight(2))
    store_grad(2, dot_tn(glu_own, grad_own))
    normed_own = normed_ref[2 * REACH : 2 * REACH + own_pad, :]
    for half in range(2):
        dconv_own = dconv[half, REACH : REACH + own_pad, :].astype(single)
        if own_rows != own_pad:
            dconv_own = jnp.where(here, dconv_own, 0.0)
        dsmall_ref[half, 9:10, :] = jnp.sum(dconv_own, axis=0, keepdims=True)
        sums = [jnp.zeros((8, channels), single) for _ in range(9)]
        dbias = jnp.zeros((8, channels), single)
        for block in range(pl.cdiv(own_pad, BLOCK)):
            begin = block * BLOCK
            height = min(BLOCK, own_pad - begin)
            picks = back_ref[block] if height == BLOCK else last_ref[...]
            moved = dot_nn(picks, dconv[half, begin : begin + height + 2 * REACH, :])
            here_active = active[half, 2 * REACH + begin : 2 * REACH + begin + height, :].astype(single)
            total = jnp.zeros((height, channels), single)
            for tap in range(9):
                part = moved[tap * height : (tap + 1) * height]
                total = total + part * small_ref[half, tap : tap + 1, :]
                sums[tap] = sums[tap] + jnp.sum(
                    (part * here_active).reshape(height // 8, 8, channels), axis=0
                )
            grad = total * slope[half, begin : begin + height, :]
            dbias = dbias + jnp.sum(grad.reshape(height // 8, 8, channels), axis=0)
            dexpand[half, begin : begin + height, :] = grad.astype(bfloat)
        for tap in range(9):
            dsmall_ref[half, tap : tap + 1, :] = jnp.sum(sums[tap], axis=0, keepdims=True)
        dsmall_ref[half, 10:11, :] = jnp.sum(dbias, axis=0, keepdims=True)
        dsmall_ref[half, 11:16, :] = jnp.zeros((5, channels), single)
    for half in range(2):
        grad = dexpand[half]
        dnormed_ref[...] += dot_nn(grad, weight(half))
        store_grad(half, dot_tn(grad, normed_own))


def ffn_call(core, begin, steps, added, own_rows, own_pad, normed, grad, reach, back, last, weights, small):
    wide, features = normed.shape
    tall = grad.shape[0]
    channels = small.shape[2] // 4
    count = channels * steps
    direct = len(weights) > 1
    whole = lambda array: pl.BlockSpec(array.shape, lambda i: (0,) * array.ndim)
    rows = lambda base: pl.BlockSpec((1, 3, channels, features), lambda i: (i + base, 0, 0, 0))
    tiny = lambda base: pl.BlockSpec((2, 16, channels), lambda i: (0, 0, i + base))
    held = pl.BlockSpec((own_pad, features), lambda i: (0, 0))
    flops = 2 * count * features * (2 * wide + tall + 6 * own_pad) + 2 * count * 9 * 256 * 2 * (
        tall + own_pad
    )
    scratch = [
        pltpu.VMEM((2, wide, channels), bfloat),
        pltpu.VMEM((2, own_pad, channels), single),
        pltpu.VMEM((2, tall, channels), bfloat),
        pltpu.VMEM((tall, channels), bfloat),
        pltpu.VMEM((2, own_pad, channels), bfloat),
    ]
    if direct:
        group = weights[1].shape[1] + 1
        piece = weights[1].shape[2] // 3
        scratch += [
            pltpu.VMEM((2, 3, group, piece, features), bfloat),
            pltpu.SemaphoreType.DMA((2, 6)),
        ]
    return pl.pallas_call(
        functools.partial(
            ffn_kernel, core if direct else None, begin, steps, len(added) > 0, own_rows, own_pad
        ),
        grid=(steps,),
        in_specs=[whole(normed), whole(grad), whole(reach), whole(back), whole(last), tiny(begin)]
        + ([pl.BlockSpec(memory_space=pl.ANY)] * 3 if direct else [rows(begin)])
        + [rows(0)] * len(added),
        out_specs=[held, held, rows(0), tiny(0)],
        out_shape=[
            jax.ShapeDtypeStruct((own_pad, features), single),
            jax.ShapeDtypeStruct((own_pad, features), single),
            jax.ShapeDtypeStruct((steps, 3, channels, features), bfloat),
            jax.ShapeDtypeStruct((2, 16, count), single),
        ],
        scratch_shapes=scratch,
        compiler_params=pltpu.CompilerParams(vmem_limit_bytes=VMEM_BYTES),
        cost_estimate=pl.CostEstimate(
            flops=flops // 8, bytes_accessed=2 * count * features, transcendentals=count * tall // 4
        ),
    )(normed, grad, reach, back, last, small, *weights, *added)


def same_head():
    row = lax.broadcasted_iota(jnp.int32, (LANES, LANES), 0) // HEAD
    column = lax.broadcasted_iota(jnp.int32, (LANES, LANES), 1) // HEAD
    return row == column


def head_sums(left, right, extra):
    full = jnp.where(same_head(), dot_tn(left, right), 0.0)
    block = jnp.sum(full.reshape(LANES // HEAD, HEAD, LANES), axis=0)
    rest = jnp.zeros((TABLE - HEAD - 1, LANES), single)
    return jnp.concatenate([block, extra, rest], axis=0)


def head_blocks(table):
    tall = jnp.concatenate([table[:HEAD]] * (LANES // HEAD), axis=0)
    return jnp.where(same_head(), tall, 0.0).astype(bfloat)


def masked(values, column):
    return (values.astype(single) * column).astype(bfloat)


def softplus(values):
    return jnp.maximum(values, 0.0) + jnp.log1p(jnp.exp(-jnp.abs(values)))


def project_kernel(
    normed, wq, wk, wv, first, second, pre_q, pre_k, query, keys, values, table_1, table_2
):
    rows = normed[...]
    pre_q[...] = dot_nt(rows, wq[...])
    query[...] = softplus(pre_q[...]).astype(bfloat)
    pre_k[...] = dot_nt(rows, wk[...])
    key = softplus(pre_k[...]).astype(bfloat)
    keys[...] = key
    value = dot_nt(rows, wv[...]).astype(bfloat)
    values[...] = value
    for column, table in ((first, table_1), (second, table_2)):
        chosen = masked(key, column[...])
        table[...] = head_sums(
            chosen, value, jnp.sum(chosen.astype(single), axis=0, keepdims=True)
        )


def attend_kernel(query, state_1, state_2, first, second, wo, ratio, den, attn, out):
    @pl.when(pl.program_id(0) == 0)
    def _():
        out[...] = jnp.zeros_like(out)

    rows = query[...]
    parts = ((first[...], state_1[...]), (second[...], state_2[...]))
    numerator, weights = 0.0, 0.0
    for column, state in parts:
        numerator = numerator + dot_nn(masked(rows, column), head_blocks(state))
        weights = weights + column * state[HEAD : HEAD + 1]
    ones = same_head().astype(single).astype(bfloat)
    den[...] = dot_nn((rows.astype(single) * weights).astype(bfloat), ones)
    ratio[...] = numerator / den[...]
    attn[...] = ratio[...].astype(bfloat)
    out[...] += dot_nn(attn[...], wo[...])


def attend_back_kernel(
    grad, wo, ratio, den, query, pre_q, state_1, state_2, first, second, dquery, table_1, table_2
):
    dratio = dot_nt(grad[...], wo[...])
    ones = same_head().astype(single).astype(bfloat)
    dnumer = dratio / den[...]
    dden = -dot_nn((dratio * ratio[...]).astype(bfloat), ones) / den[...]
    rows = query[...]
    total_grad, weights = 0.0, 0.0
    for column, state, table in (
        (first[...], state_1[...], table_1),
        (second[...], state_2[...], table_2),
    ):
        chosen = (dnumer * column).astype(bfloat)
        total_grad = total_grad + dot_nt(chosen, head_blocks(state))
        weights = weights + column * state[HEAD : HEAD + 1]
        extra = jnp.sum(rows.astype(single) * dden * column, axis=0, keepdims=True)
        table[...] = head_sums(rows, chosen, extra)
    total_grad = total_grad + weights * dden
    dquery[...] = (total_grad * jax.nn.sigmoid(pre_q[...])).astype(bfloat)


def project_back_kernel(
    dquery, keys, values, pre_k, state_1, state_2, first, second, wq, wk, wv, dkeys, dvalues, dnormed
):
    @pl.when(pl.program_id(0) == 0)
    def _():
        dnormed[...] = jnp.zeros_like(dnormed)

    key_grad, value_grad = 0.0, 0.0
    for column, state in ((first[...], state_1[...]), (second[...], state_2[...])):
        block = head_blocks(state)
        key_grad = key_grad + dot_nt(masked(values[...], column), block)
        key_grad = key_grad + column * state[HEAD : HEAD + 1]
        value_grad = value_grad + dot_nn(masked(keys[...], column), block)
    dkeys[...] = (key_grad * jax.nn.sigmoid(pre_k[...])).astype(bfloat)
    dvalues[...] = value_grad.astype(bfloat)
    dnormed[...] += (
        dot_nn(dquery[...], wq[...]) + dot_nn(dkeys[...], wk[...]) + dot_nn(dvalues[...], wv[...])
    )


def lane_call(kernel, kinds, arrays, outs, rows, features):
    specs = {
        "l": pl.BlockSpec((rows, LANES), lambda g: (0, g)),
        "w": pl.BlockSpec((LANES, features), lambda g: (g, 0)),
        "t": pl.BlockSpec((TABLE, LANES), lambda g: (0, g)),
        "c": pl.BlockSpec((rows, 1), lambda g: (0, 0)),
        "a": pl.BlockSpec((rows, features), lambda g: (0, 0)),
    }
    shape = {"l": (rows, features), "t": (TABLE, features), "a": (rows, features)}
    return pl.pallas_call(
        kernel,
        grid=(features // LANES,),
        in_specs=[specs[kind] for kind in kinds],
        out_specs=[specs[kind] for kind, _ in outs],
        out_shape=[jax.ShapeDtypeStruct(shape[kind], dtype) for kind, dtype in outs],
        compiler_params=pltpu.CompilerParams(vmem_limit_bytes=VMEM_BYTES),
        cost_estimate=pl.CostEstimate(
            flops=rows * features * features, bytes_accessed=rows * features, transcendentals=0
        ),
    )(*arrays)


def head_probs(query, keys, lengths):
    scores = dot_nt(query, keys) * (XHEAD ** (-0.5))
    place = lax.broadcasted_iota(jnp.int32, scores.shape, 1)
    live = place < lengths
    scores = jnp.where(live, scores, -1e30)
    top = jnp.max(scores, axis=-1, keepdims=True)
    powers = jnp.exp(scores - top)
    return powers / jnp.sum(powers, axis=-1, keepdims=True)


def cross_kernel(query_ref, keys_ref, vals_ref, length_ref, mix_ref):
    probs = head_probs(query_ref[...], keys_ref[0], length_ref[...])
    mix_ref[...] = dot_nn(probs.astype(bfloat), vals_ref[0]).astype(bfloat)


def cross_back_kernel(
    query_ref, keys_ref, vals_ref, length_ref, dmix_ref, dquery_ref, dkeys_ref, dvals_ref, dbias_ref
):
    query, keys, dmix = query_ref[...], keys_ref[0], dmix_ref[...]
    probs = head_probs(query, keys, length_ref[...])
    dprobs = dot_nt(dmix, vals_ref[0])
    dvals_ref[0] = dot_tn(dmix, probs.astype(bfloat))[:XHEAD].astype(bfloat)
    row_dot = jnp.sum(probs * dprobs, axis=-1, keepdims=True)
    dscores = (probs * (dprobs - row_dot) * (XHEAD ** (-0.5))).astype(bfloat)
    dquery = dot_nn(dscores, keys)
    dbias_ref[...] = jnp.sum(dquery, axis=0, keepdims=True)
    dquery_ref[...] = dquery.astype(bfloat)
    dkeys_ref[0] = dot_tn(query, dscores)[:XHEAD].astype(bfloat)


def cross_specs(rows):
    lane = pl.BlockSpec((rows, XLANE), lambda h: (0, h))
    text = pl.BlockSpec((1, TXT_PAD, XLANE), lambda h: (h, 0, 0))
    length = pl.BlockSpec((rows, 1), lambda h: (0, 0))
    return lane, text, length


def cross_call(query, keys, vals, lengths):
    rows, heads = query.shape[0], keys.shape[0]
    lane, text, length = cross_specs(rows)
    return pl.pallas_call(
        cross_kernel,
        grid=(heads,),
        in_specs=[lane, text, text, length],
        out_specs=lane,
        out_shape=jax.ShapeDtypeStruct((rows, heads * XLANE), bfloat),
        compiler_params=pltpu.CompilerParams(vmem_limit_bytes=VMEM_BYTES),
        cost_estimate=pl.CostEstimate(
            flops=heads * rows * TXT_PAD * XLANE,
            bytes_accessed=2 * rows * heads * XLANE,
            transcendentals=heads * rows * TXT_PAD // 8,
        ),
    )(query, keys, vals, lengths)


def cross_back_call(query, keys, vals, lengths, dmix):
    rows, heads = query.shape[0], keys.shape[0]
    lane, text, length = cross_specs(rows)
    return pl.pallas_call(
        cross_back_kernel,
        grid=(heads,),
        in_specs=[lane, text, text, length, lane],
        out_specs=[
            lane,
            pl.BlockSpec((1, XHEAD, TXT_PAD), lambda h: (h, 0, 0)),
            pl.BlockSpec((1, XHEAD, TXT_PAD), lambda h: (h, 0, 0)),
            pl.BlockSpec((1, XLANE), lambda h: (0, h)),
        ],
        out_shape=[
            jax.ShapeDtypeStruct((rows, heads * XLANE), bfloat),
            jax.ShapeDtypeStruct((heads, XHEAD, TXT_PAD), bfloat),
            jax.ShapeDtypeStruct((heads, XHEAD, TXT_PAD), bfloat),
            jax.ShapeDtypeStruct((1, heads * XLANE), single),
        ],
        compiler_params=pltpu.CompilerParams(vmem_limit_bytes=VMEM_BYTES),
        cost_estimate=pl.CostEstimate(
            flops=heads * rows * TXT_PAD * XLANE,
            bytes_accessed=2 * rows * heads * XLANE,
            transcendentals=heads * rows * TXT_PAD // 8,
        ),
    )(query, keys, vals, lengths, dmix)


def norm_parts(values):
    centred = values - jnp.mean(values, axis=-1, keepdims=True)
    inv_std = lax.rsqrt(jnp.mean(centred * centred, axis=-1, keepdims=True) + norm_eps)
    return (centred * inv_std, inv_std)


def norm_back(grad_in, normal, inv_std, scale):
    scaled = grad_in * (1.0 + scale)
    return (
        scaled
        - jnp.mean(scaled, axis=-1, keepdims=True)
        - normal * jnp.mean(scaled * normal, axis=-1, keepdims=True)
    ) * inv_std


def pad_rows(values, rows):
    return jnp.pad(values, ((0, rows - values.shape[0]),) + ((0, 0),) * (values.ndim - 1))


def pad_heads(rows, heads):
    features = rows.shape[1]
    shaped = rows.reshape(heads, XHEAD, features)
    return jnp.pad(shaped, ((0, 0), (0, XLANE - XHEAD), (0, 0))).reshape(heads * XLANE, features)


def local(
    tokens,
    cotangent,
    item_bucket,
    text_len,
    t_mod,
    text_tokens,
    shift_table,
    w_qkv,
    w_out,
    out_bias,
    w_xq,
    xq_bias,
    w_xkv,
    xv_bias,
    w_xo,
    xo_bias,
    w_in,
    in_bias,
    dw_weight,
    dw_bias,
    w_pt,
):
    group = lax.axis_size("tensor")
    ranks = lax.axis_size("dp")
    me_z = lax.axis_index("tensor")
    me_d = lax.axis_index("dp")
    own_rows, width = tokens.shape
    own_pad = -(-own_rows // 32) * 32
    tall = -(-(own_rows + 2 * REACH) // BLOCK) * BLOCK
    wide = tall + 2 * REACH
    total_rows = own_rows * group * ranks
    item_count = t_mod.shape[0]
    heads = width // HEAD
    xheads = width // XHEAD
    cols = w_xq.shape[1]
    channels = w_in.shape[2]
    padded_channels = -(-channels // 384) * 384
    own_start = (me_d * group + me_z) * own_rows
    first_item = own_start // ITEM_SLOTS
    last_item = (own_start + own_rows - 1) // ITEM_SLOTS
    two_items = last_item != first_item

    bits = upper_bits()
    att_piece = attention_rows(cols)
    att_pad = att_piece * ranks
    att_rows = 3 * cols
    rows_qkv = pad_rows(w_qkv.transpose(1, 2, 0).reshape(att_rows, width), att_pad)
    rows_mix = pad_rows(jnp.concatenate([w_out, w_xq.T, w_xo], axis=0), att_pad)
    ffn_piece = padded_channels // ranks
    half_count = padded_channels * group // 2
    rows_ffn = jnp.stack(
        [pad_rows(rows, padded_channels) for rows in (w_in[:, 0].T, w_in[:, 1].T, w_pt)]
    )
    own_qkv = rows_qkv.reshape(ranks, att_piece, width)
    own_mix = rows_mix.reshape(ranks, att_piece, width)
    piece_1 = lax.dynamic_index_in_dim(own_qkv, me_d, 0, keepdims=False)
    piece_2 = lax.dynamic_index_in_dim(own_mix, me_d, 0, keepdims=False)

    def near_z(piece, far):
        near = swap_z(jnp.stack([piece, far]), 1)
        return jnp.stack([near[0], far, near[1]])

    def turn(values, number):
        return jnp.stack([values, swap_path(values, number)])

    def mid_turns(values):
        for number in range(1, len(bits) - 1):
            values = turn(values, number)
        return values.reshape((-1,) + values.shape[-3:])

    def last_turn(values):
        return swap_path(values, len(bits) - 1)

    own_slots = own_start + jnp.arange(own_rows, dtype=jnp.int32)
    item = own_slots // ITEM_SLOTS
    in_first = (item == first_item)[:, None]
    in_second = jnp.logical_not(in_first)
    mod_first = shift_table + lax.dynamic_index_in_dim(t_mod, first_item, 0, keepdims=False)
    mod_second = shift_table + lax.dynamic_index_in_dim(t_mod, last_item, 0, keepdims=False)
    row_mod = lambda number: jnp.where(in_first, mod_first[number][None], mod_second[number][None])
    shift_a, scale_a, gate_a, shift_f, scale_f, gate_f = [row_mod(number) for number in range(6)]
    tokens_f = tokens.astype(single)
    grad_out = cotangent.astype(single)
    normal_a, inv_std_a = norm_parts(tokens_f)
    normed = (normal_a * (1.0 + scale_a) + shift_a).astype(bfloat)

    far_1 = swap_z(piece_1, 0)
    far_1, normed = tie(far_1, normed)
    wave_1 = near_z(piece_1, far_1)
    wave_1, item_bucket, piece_2 = tie(wave_1, item_bucket, piece_2)
    far_2 = swap_z(piece_2, 0)
    wave_1 = turn(wave_1, 0)
    inner = own_slots % ITEM_SLOTS
    grid_h, grid_w = grid_table(look_up(item_bucket, item))
    valid = inner < grid_h * grid_w
    live = valid.astype(single)[:, None]
    tall_slots = own_start - REACH + jnp.arange(tall, dtype=jnp.int32)
    reach = shift_blocks(tall_slots, total_rows, item_bucket, 1, tall)
    reach = reach.reshape(9, tall // BLOCK, BLOCK, -1).transpose(1, 0, 2, 3)
    reach = reach.reshape(tall // BLOCK, 9 * BLOCK, -1)
    wave_1, reach, text_tokens = tie(wave_1, reach, text_tokens)
    wave_1 = mid_turns(wave_1)
    last_1 = last_turn(wave_1)
    core_1 = swap(wave_1, "dp", 1)
    wave_2 = near_z(piece_2, far_2)
    text_rows_here = text_tokens.shape[0]
    text_half = pad_rows(text_tokens, -(-text_rows_here // 16) * 16)
    text_half = lax.dynamic_index_in_dim(
        text_half.reshape(2, -1, width), me_d % 2, 0, keepdims=False
    )
    text_far = swap(text_half, "tensor", 2)
    pad_slots = own_start + jnp.arange(own_pad, dtype=jnp.int32)
    back = shift_blocks(pad_slots, total_rows, item_bucket, -1, own_rows)
    full_blocks = own_pad // BLOCK
    rest = own_pad - full_blocks * BLOCK
    back_full = back[:, : full_blocks * BLOCK].reshape(9, full_blocks, BLOCK, -1).transpose(1, 0, 2, 3)
    back_full = back_full.reshape(full_blocks, 9 * BLOCK, -1)
    rest = max(rest, 32)
    back_last = back[:, own_pad - rest :, : rest + 2 * REACH].reshape(9 * rest, -1)
    d_ffn = (grad_out * live * gate_f).astype(bfloat)
    wave_1, last_1, core_1, wave_2, back_full, back_last, d_ffn, text_far, rows_ffn = tie(
        wave_1, last_1, core_1, wave_2, back_full, back_last, d_ffn, text_far, rows_ffn
    )
    core_last_1 = swap(last_1, "dp", 1)
    piece_3 = lax.dynamic_slice_in_dim(rows_ffn, me_d * ffn_piece, ffn_piece, 1)
    piece_3 = piece_3.reshape(3 * ffn_piece, width)
    core_last_1, wave_2, piece_3 = tie(core_last_1, wave_2, piece_3)
    wave_2 = turn(wave_2, 0)
    far_3 = swap_z(piece_3, 0)
    text_near = swap(jnp.stack([text_half, text_far]), "tensor", 1)
    wq, wk, wv = [
        part.reshape(width, width) for part in assemble(own_qkv, (wave_1, last_1, core_1, core_last_1), cols)
    ]
    wq, wk, wv, wave_2, text_near = tie(wq, wk, wv, wave_2, text_near)
    wave_2 = mid_turns(wave_2)
    last_2 = last_turn(wave_2)
    core_2 = swap(wave_2, "dp", 1)
    in_order = lambda rel: [
        lax.dynamic_index_in_dim(rel, me_z ^ peer, 0, keepdims=False) for peer in range(group)
    ]
    by_core = lambda one, two: jnp.stack(
        [jnp.where(me_d % 2 == 0, one, two), jnp.where(me_d % 2 == 0, two, one)]
    )
    text_rel = jnp.stack([text_half, text_near[0], text_far, text_near[1]])
    text_other = swap(text_rel, "dp", 1)

    first_live = (in_first & valid[:, None]).astype(single)
    second_live = (in_second & valid[:, None]).astype(single)
    first_all, second_all = in_first.astype(single), in_second.astype(single)
    over_lanes = functools.partial(lane_call, rows=own_rows, features=width)
    pre_q, pre_k, query, keys, values, table_1, table_2 = over_lanes(
        project_kernel,
        "awwwcc",
        (normed, wq, wk, wv, first_live, second_live),
        (("l", single), ("l", single), ("l", bfloat), ("l", bfloat), ("l", bfloat), ("t", single), ("t", single)),
    )

    span_rows = own_rows * group
    span_start = me_d * span_rows
    span_first = span_start // ITEM_SLOTS
    span_last = (span_start + span_rows - 1) // ITEM_SLOTS
    span_items = (span_rows - 2) // ITEM_SLOTS + 2

    def item_table(first_part, second_part):
        parts = []
        for number in range(span_items):
            chosen = jnp.where(first_item - span_first == number, first_part, 0.0)
            also = two_items & (last_item - span_first == number)
            parts.append(chosen + jnp.where(also, second_part, 0.0))
        return jnp.stack(parts).astype(bfloat)

    def item_sums(table):
        count = ranks - 1
        tail_part = lax.dynamic_index_in_dim(table, span_last - span_first, 0, keepdims=False)
        below = lax.ppermute(tail_part, "dp", [(i, i + 1) for i in range(count)])
        above = lax.ppermute(table[0], "dp", [(i + 1, i) for i in range(count)])
        below_same = (span_start - 1) // ITEM_SLOTS == span_first
        above_same = (span_start + span_rows) // ITEM_SLOTS == span_last
        sums = []
        for number in (first_item, last_item):
            part = lax.dynamic_index_in_dim(table, number - span_first, 0, keepdims=False)
            part = part.astype(single)
            part = part + jnp.where(below_same & (number == span_first), below.astype(single), 0.0)
            part = part + jnp.where(above_same & (number == span_last), above.astype(single), 0.0)
            sums.append(part)
        return sums

    small_rel = jnp.concatenate([dw_weight, dw_bias[None], in_bias[None]], axis=0)
    small_rel = jnp.pad(small_rel, ((0, 5), (0, 0), (0, padded_channels - channels)))
    sizes = small_rel.size
    small_rel = jnp.concatenate([small_rel.reshape(-1), xq_bias]).astype(bfloat)
    small_tall = -(-small_rel.size // (32 * cols)) * 16
    small_rel = jnp.pad(small_rel, (0, 2 * small_tall * cols - small_rel.size))
    small_half = lax.dynamic_index_in_dim(
        small_rel.reshape(2, small_tall, cols), me_d % 2, 0, keepdims=False
    )
    down = tuple(range(2, 2 + len(bits)))

    table = item_table(table_1, table_2)
    table, text_other, far_3 = tie(table, text_other, far_3)
    table = total([table, swap_z(table, 0)])
    text_rel = by_core(text_rel, text_other).swapaxes(0, 1).reshape(group, -1, width)
    text_all = jnp.concatenate(in_order(text_rel[:, :text_rows_here]))
    text_kv = jnp.einsum("td,dke->tke", text_all, w_xkv, preferred_element_type=single)
    xkv_own = jnp.stack([text_kv[:, 0], text_kv[:, 1] + xv_bias], axis=0).astype(bfloat)
    both_half = jnp.concatenate(
        [lax.dynamic_index_in_dim(xkv_own, me_d % 2, 0, keepdims=False), small_half], axis=0
    )
    table, both_half, last_2, core_2 = tie(table, both_half, last_2, core_2)
    table = total([table, swap_z(table, 1)])
    both_far = swap(both_half, "tensor", 2)
    core_last_2 = swap(last_2, "dp", 1)
    table, both_far, core_last_2, far_3 = tie(table, both_far, core_last_2, far_3)
    state_1, state_2 = item_sums(table)
    wave_3 = near_z(piece_3, far_3)
    both_near = swap(jnp.stack([both_half, both_far]), "tensor", 1)
    wo, wxq, wxo = [
        part.reshape(width, width) for part in assemble(own_mix, (wave_2, last_2, core_2, core_last_2), cols)
    ]
    wxq_pad = pad_heads(wxq, xheads)
    wxo_pad = pad_heads(wxo, xheads)
    state_1, state_2, wo, wxq_pad, wxo_pad, both_near = tie(
        state_1, state_2, wo, wxq_pad, wxo_pad, both_near
    )
    both_rel = jnp.stack([both_half, both_near[0], both_far, both_near[1]])
    both_other = swap(both_rel, "dp", 1)
    attn_ratio, denominator, attn, attn_sum = over_lanes(
        attend_kernel,
        "lttccw",
        (query, state_1, state_2, first_all, second_all, wo),
        (("l", single), ("l", single), ("l", bfloat), ("a", single)),
    )
    attn_out = attn_sum + out_bias
    after_attn = tokens_f + live * gate_a * attn_out

    after_attn, wave_3, both_other = tie(after_attn, wave_3, both_other)
    wave_3 = turn(wave_3, 0)
    cross_in = after_attn.astype(bfloat)
    xq_product = dot_nt(cross_in, wxq_pad)
    both = by_core(both_rel, both_other)
    xkv_all = both[:, :, :TXT].swapaxes(0, 1)
    xkv_all = jnp.stack(in_order(xkv_all)).reshape(group, 2, TXT, cols // XHEAD, XHEAD)
    xkv_all = xkv_all.transpose(1, 0, 3, 2, 4).reshape(2, xheads, TXT, XHEAD)
    xkv_all = jnp.pad(xkv_all, ((0, 0), (0, 0), (0, TXT_PAD - TXT), (0, XLANE - XHEAD)))
    xkeys, xvals = xkv_all[0], xkv_all[1]
    small = both[:, :, TXT:].swapaxes(0, 1).reshape(group, -1).astype(single)
    xq_rel = small[:, sizes : sizes + cols]
    small = flip_dp(small[:, :sizes].reshape(group, 16, 2, ranks, ffn_piece), 3)
    small = small.reshape((group, 16, 2) + (2,) * (len(bits) + 1) + (ffn_piece,))
    small = jnp.moveaxis(small, 0, len(bits) + 3)
    small = small.transpose((len(bits) + 2, 1, 0) + down[::-1] + (len(bits) + 3, len(bits) + 4))
    small = small.reshape(small.shape[:-2] + (2, 2, ffn_piece))
    small = [
        turn_z(own_turns(small[core], 2, core == 1), 2 + len(bits), core == 1).reshape(
            2, 16, half_count
        )
        for core in (0, 1)
    ]
    xq_bias_all = jnp.stack(in_order(xq_rel)).reshape(xheads, XHEAD)
    xq_bias_all = jnp.pad(xq_bias_all, ((0, 0), (0, XLANE - XHEAD))).reshape(xheads * XLANE)
    lengths = look_up(text_len, item)[:, None]
    xquery = (xq_product + xq_bias_all).astype(bfloat)
    xquery, wave_3 = tie(xquery, wave_3)
    wave_3 = mid_turns(wave_3)
    last_3 = last_turn(wave_3)
    core_3 = swap(wave_3, "dp", 1)
    cross_mix = cross_call(xquery, xkeys, xvals, lengths)
    cross_out = dot_nn(cross_mix, wxo_pad) + xo_bias
    after_cross = after_attn + live * cross_out

    normal_f, inv_std_f = norm_parts(after_cross)
    normed_ffn = (normal_f * (1.0 + scale_f) + shift_f).astype(bfloat)
    normed_ffn, wave_3, last_3, core_3, *small = tie(normed_ffn, wave_3, last_3, core_3, *small)
    core_last_3 = swap(last_3, "dp", 1)
    def ffn_half(core):
        count = len(bits)
        own = flip_dp(rows_ffn.reshape(3, ranks, ffn_piece, width), 1)
        own = own.reshape((3,) + (2,) * (count + 1) + (ffn_piece, width))
        own = jnp.moveaxis(lax.index_in_dim(own, core, count + 1, keepdims=False), 0, count)
        own = own_turns(own.transpose(tuple(range(count))[::-1] + (count, count + 1, count + 2)), 0, core == 1)
        others = jnp.concatenate(((wave_3, last_3), (core_3, core_last_3))[core])
        others = others.reshape((2,) * count + (group - 1, 3, ffn_piece, width))
        others = others.transpose(tuple(range(count))[::-1] + tuple(range(count, count + 4)))
        joined = jnp.concatenate([jnp.expand_dims(own, count), others], axis=count)
        joined = jnp.moveaxis(joined, count + 1, 2)
        return joined.reshape(4, 3, half_count // 4, width)

    direct = ffn_piece % 16 == 0 and len(bits) == 2
    weights_ffn = [
        [rows_ffn, *((wave_3, last_3), (core_3, core_last_3))[core]] if direct else [ffn_half(core)]
        for core in (0, 1)
    ]

    above = shift_devices(
        jnp.concatenate([normed_ffn[own_rows - 2 * REACH :], d_ffn[own_rows - REACH :]], axis=0), 1
    )
    below = shift_devices(jnp.concatenate([normed_ffn[: 2 * REACH], d_ffn[:REACH]], axis=0), -1)
    normed_ext = pad_rows(
        jnp.concatenate([above[: 2 * REACH], normed_ffn, below[: 2 * REACH]], axis=0), wide
    )
    d_ffn_ext = pad_rows(
        jnp.concatenate([above[2 * REACH :], d_ffn, below[2 * REACH :]], axis=0), tall
    )
    tables = (reach, back_full, back_last)
    def ffn_part(core, begin, *added):
        return ffn_call(
            core, begin, 2, added, own_rows, own_pad, normed_ext, d_ffn_ext, *tables, weights_ffn[core], small[core]
        )

    part_3 = ffn_part(1, 2)
    normed_ext, *part_3 = tie(normed_ext, *part_3)
    other_3 = swap(part_3[2], "dp", 1)
    part_2 = ffn_part(1, 0)
    normed_ext, other_3, *part_2 = tie(normed_ext, other_3, *part_2)
    other_2 = swap(part_2[2], "dp", 1)
    part_1 = ffn_part(0, 2, other_3)
    normed_ext, other_2, *part_1 = tie(normed_ext, other_2, *part_1)
    turn_shape = (2, 3) + (2,) * len(bits) + (ffn_piece, width)
    ffn_got = swap_path(part_1[2], 0).reshape(turn_shape)
    part_0 = ffn_part(0, 0, other_2)
    parts = (part_0, part_1, part_2, part_3)
    ffn_out = sum(part[0] for part in parts)[:own_rows]
    d_normed_ffn = sum(part[1] for part in parts)[:own_rows]
    ffn_terms = [part_0[2].reshape(turn_shape), ffn_got]
    d_small_half = [
        jnp.concatenate([low[3], high[3]], axis=2) for low, high in ((part_0, part_1), (part_2, part_3))
    ]

    d_small = jnp.stack(
        [
            turn_z(
                own_turns(
                    part.astype(bfloat).reshape((2, 16) + (2,) * (len(bits) + 2) + (ffn_piece,)),
                    2,
                    core == 1,
                ),
                2 + len(bits),
                core == 1,
            )
            for core, part in enumerate(d_small_half)
        ],
        axis=len(bits) + 2,
    )
    order = (len(bits) + 3, len(bits) + 4, 0, 1) + down[::-1] + (len(bits) + 2, len(bits) + 5)
    d_small = flip_z(d_small.transpose(order), 0)
    d_small = d_small.reshape(group, 2, 16, ranks, ffn_piece)[:, :, :11]
    d_small = flip_dp(d_small, 3).reshape(group, -1)
    small_rows = -(-d_small.shape[1] // (16 * width)) * 16
    d_small = jnp.pad(d_small, ((0, 0), (0, small_rows * width - d_small.shape[1])))
    d_small = d_small.reshape(group, small_rows, width)

    out_tokens = (after_cross + live * gate_f * ffn_out).astype(bfloat)
    d_gate_f = grad_out * live * ffn_out
    grad_cross = grad_out + norm_back(d_normed_ffn, normal_f, inv_std_f, scale_f)

    d_cross = grad_cross * live
    d_xo_bias = jnp.sum(d_cross, axis=0)
    d_cross_low = d_cross.astype(bfloat)
    d_cross_low, ffn_terms[-1] = tie(d_cross_low, ffn_terms[-1])
    for stage in range(1, len(bits)):
        ffn_terms = halve_path(ffn_terms, stage, 0 if stage == 1 else 1)
    d_mix = dot_nt(d_cross_low, wxo_pad).astype(bfloat)
    d_query_low, d_keys, d_vals, d_xq_part = cross_back_call(xquery, xkeys, xvals, lengths, d_mix)
    d_query_low, ffn_terms[-1] = tie(d_query_low, ffn_terms[-1])
    ffn_terms = halve_z_once(ffn_terms, 1, 1)
    grad_attn = grad_cross + dot_nn(d_query_low, wxq_pad)

    d_attn_out = grad_attn * live * gate_a
    d_gate_a = grad_attn * live * attn_out
    d_out_bias = jnp.sum(d_attn_out, axis=0)
    d_attn_low = d_attn_out.astype(bfloat)

    text_rows = 2 * cols * TXT_PAD // width
    mix_rows = -(-(att_rows + text_rows + small_rows) // (16 * ranks)) * 16
    lanes = width // TXT_PAD
    d_kv = jnp.concatenate(
        [d_keys.reshape(group, cols, TXT_PAD), d_vals.reshape(group, cols, TXT_PAD)], axis=1
    )
    d_kv = jnp.concatenate(
        [d_kv[:, number * text_rows : (number + 1) * text_rows] for number in range(lanes)], axis=2
    )
    mix_arrays = [
        attn,
        d_attn_low,
        d_query_low,
        cross_in,
        cross_mix,
        d_cross_low,
    ]
    mix_extra = jnp.concatenate([d_kv, d_small], axis=1)
    d_query_in, table_1, table_2 = over_lanes(
        attend_back_kernel,
        "awllllttcc",
        (d_attn_low, wo, attn_ratio, denominator, query, pre_q, state_1, state_2, first_all, second_all),
        (("l", bfloat), ("t", single), ("t", single)),
    )
    d_table = item_table(table_1, table_2)
    def mod_sum(rows):
        return jnp.stack(
            [
                jnp.sum(jnp.where(in_first, rows, 0.0), axis=0),
                jnp.sum(jnp.where(in_second, rows, 0.0), axis=0),
            ]
        )

    d_table, mix_extra, ffn_terms[-1] = tie(d_table, mix_extra, ffn_terms[-1])
    d_table = total([d_table, swap_z(d_table, 0)])
    mod_sums = [
        mod_sum(rows) for rows in (d_gate_a, d_normed_ffn, d_normed_ffn * normal_f, d_gate_f)
    ]
    d_table, d_out_bias, d_xo_bias, *mod_sums = tie(d_table, d_out_bias, d_xo_bias, *mod_sums)
    d_table = total([d_table, swap_z(d_table, 1)])
    mix_grads = grads_call(mix_arrays, ((0, 1), (2, 3), (4, 5)), mix_extra, mix_rows, cols)
    d_table, mix_grads[1] = tie(d_table, mix_grads[1])
    mix_terms = core_terms(*mix_grads)
    d_state_1, d_state_2 = item_sums(d_table)
    d_state_1, d_state_2, mix_terms[1] = tie(d_state_1, d_state_2, mix_terms[1])
    mix_terms = halve_path(mix_terms, 0, 0)
    ffn_terms = halve_z_once(ffn_terms, 2, 1)
    d_keys_in, d_values_low, d_normed = over_lanes(
        project_back_kernel,
        "llllttccwww",
        (d_query_in, keys, values, pre_k, d_state_1, d_state_2, first_live, second_live, wq, wk, wv),
        (("l", bfloat), ("l", bfloat), ("a", single)),
    )
    d_tokens = grad_attn + norm_back(d_normed, normal_a, inv_std_a, scale_a)

    sums = jnp.stack([mod_sum(d_normed), mod_sum(d_normed * normal_a)] + mod_sums, axis=1)
    items = jnp.arange(item_count, dtype=jnp.int32)[None, :, None]
    mod_table = jnp.where(items == first_item, sums[0][:, None], 0.0) + jnp.where(
        (items == first_item + 1), sums[1][:, None], 0.0
    )
    xq_row = d_xq_part.reshape(xheads, XLANE)[:, :XHEAD].reshape(width)
    rows_all = jnp.concatenate(
        [mod_table.reshape(-1, width), jnp.stack([d_out_bias, d_xo_bias, xq_row], axis=0)], axis=0
    )
    rows_count = rows_all.shape[0]
    last_rows = -(-(att_rows + rows_count) // (16 * ranks)) * 16
    spare = -(-rows_count // 16) * 16
    rows_all = pad_rows(rows_all.astype(bfloat), spare)
    rows_all = jnp.broadcast_to(rows_all[None], (group, spare, width))

    rows_all, mix_terms[-1] = tie(rows_all, mix_terms[-1])
    for stage in range(1, len(bits)):
        mix_terms = halve_path(mix_terms, stage, 0)
    qkv_grads = grads_call(
        [d_query_in, d_keys_in, d_values_low, normed],
        ((0, 3), (1, 3), (2, 3)),
        rows_all,
        last_rows,
        cols,
    )
    qkv_grads[1], ffn_terms[-1], mix_terms[-1] = tie(qkv_grads[1], ffn_terms[-1], mix_terms[-1])
    qkv_terms = core_terms(*qkv_grads)
    qkv_terms[1], mix_terms[-1] = tie(qkv_terms[1], mix_terms[-1])
    qkv_terms = halve_path(qkv_terms, 0, 0)
    mix_terms = halve_z_once(mix_terms, 1, 0)
    qkv_terms[-1], mix_terms[-1] = tie(qkv_terms[-1], mix_terms[-1])
    for stage in range(1, len(bits)):
        qkv_terms = halve_path(qkv_terms, stage, 0)
    mix_terms = halve_z_once(mix_terms, 2, 0)
    qkv_terms[-1], mix_terms[-1], ffn_terms[-1] = tie(
        qkv_terms[-1], mix_terms[-1], ffn_terms[-1]
    )
    qkv_terms = halve_z_once(qkv_terms, 1, 0)
    d_mix_all = share_turn(total(mix_terms), 0)
    d_ffn_all = share_turn(total(ffn_terms), 0)
    qkv_terms[-1], d_mix_all, d_ffn_all = tie(qkv_terms[-1], d_mix_all, d_ffn_all)
    qkv_terms = halve_z_once(qkv_terms, 2, 0)
    for stage in range(1, len(bits)):
        d_mix_all = share_turn(d_mix_all, stage)
    qkv_terms[-1], d_mix_all = tie(qkv_terms[-1], d_mix_all)
    d_qkv_all = share_turn(total(qkv_terms), 0)
    d_mix_all = share_core(d_mix_all)
    for stage in range(1, len(bits)):
        d_ffn_all = share_turn(d_ffn_all, stage)
    d_qkv_all, d_mix_all, d_ffn_all = tie(d_qkv_all, d_mix_all, d_ffn_all)
    for stage in range(1, len(bits)):
        d_qkv_all = share_turn(d_qkv_all, stage)
    d_ffn_all = share_core(d_ffn_all)
    d_mix_all = d_mix_all.reshape(-1, width)
    d_kv = d_mix_all[att_rows : att_rows + text_rows]
    d_kv = jnp.concatenate(
        [d_kv[:, number * TXT_PAD : (number + 1) * TXT_PAD] for number in range(lanes)], axis=0
    )
    d_kv = d_kv.reshape(2, cols, TXT_PAD)[:, :, :TXT]
    d_xv_bias = jnp.sum(d_kv[1].astype(single), axis=1)
    d_w_xkv = jnp.einsum("td,ket->dke", text_all, d_kv, preferred_element_type=single)
    d_text = jnp.einsum("ket,dke->td", d_kv, w_xkv, preferred_element_type=single)
    d_text = reduce_z(d_text.astype(bfloat).reshape(2, 2, TXT // group, width), 1, 1)
    d_qkv_all, d_ffn_all, d_text = tie(d_qkv_all, d_ffn_all, d_text)
    d_qkv_all = share_core(d_qkv_all)
    d_text = reduce_z(d_text, 2, 0).astype(single)
    d_ffn_all = d_ffn_all.transpose(1, 0, 2, 3)
    d_ffn_all = d_ffn_all.reshape(3, padded_channels, width)[:, :channels]
    d_w_in = jnp.stack([d_ffn_all[0].T, d_ffn_all[1].T], axis=1).astype(single)
    d_w_pt = d_ffn_all[2].astype(single)

    d_w_out = d_mix_all[:cols].astype(single)
    d_w_xq = d_mix_all[cols : 2 * cols].T.astype(single)
    d_w_xo = d_mix_all[2 * cols : 3 * cols].astype(single)
    d_small = d_mix_all[att_rows + text_rows : att_rows + text_rows + small_rows].reshape(-1)
    d_small = d_small[: 22 * padded_channels].reshape(2, 11, padded_channels)[:, :, :channels]
    d_small = d_small.swapaxes(0, 1).astype(single)
    d_dw_weight, d_dw_bias, d_in_bias = d_small[:9], d_small[9], d_small[10]

    d_qkv_all = d_qkv_all.reshape(-1, width)
    d_w_qkv = d_qkv_all[:att_rows].reshape(3, cols, width).transpose(2, 0, 1).astype(single)
    rows_all = d_qkv_all[att_rows : att_rows + rows_count].astype(single)
    d_t_mod = rows_all[:-3].reshape(mod_table.shape).swapaxes(0, 1)
    d_out_bias, d_xo_bias = rows_all[-3], rows_all[-2]
    d_xq_bias = lax.dynamic_slice_in_dim(rows_all[-1], me_z * cols, cols, 0)
    d_shift_table = jnp.sum(d_t_mod, axis=0)
    return (
        out_tokens,
        d_tokens,
        d_t_mod,
        d_text,
        d_shift_table,
        d_w_qkv,
        d_w_out,
        d_out_bias,
        d_w_xq,
        d_xq_bias,
        d_w_xkv,
        d_xv_bias,
        d_w_xo,
        d_xo_bias,
        d_w_in,
        d_in_bias,
        d_dw_weight,
        d_dw_bias,
        d_w_pt,
    )


def solution(mesh):
    rows = P(("dp", "tensor"), None)
    placed = (
        rows,
        rows,
        P(),
        P(),
        P(),
        P("tensor", None),
        P(),
        P(None, None, "tensor"),
        P("tensor", None),
        P(),
        P(None, "tensor"),
        P("tensor"),
        P(None, None, "tensor"),
        P("tensor"),
        P("tensor", None),
        P(),
        P(None, None, "tensor"),
        P(None, "tensor"),
        P(None, None, "tensor"),
        P(None, "tensor"),
        P("tensor", None),
    )
    return jax.shard_map(
        local,
        mesh=mesh,
        in_specs=placed,
        out_specs=(
            rows,
            rows,
            P(),
            P("tensor", None),
            P(),
            P(None, None, "tensor"),
            P("tensor", None),
            P(),
            P(None, "tensor"),
            P("tensor"),
            P(None, None, "tensor"),
            P("tensor"),
            P("tensor", None),
            P(),
            P(None, None, "tensor"),
            P(None, "tensor"),
            P(None, None, "tensor"),
            P(None, "tensor"),
            P("tensor", None),
        ),
        check_vma=False,
    )
```

```python
import functools

import jax
import jax.numpy as jnp
from jax import lax
from jax.experimental import pallas as pl
from jax.experimental.pallas import tpu as pltpu
from jax.sharding import PartitionSpec as P

HEAD = 32
XHEAD = 72
XLANE = 128
TXT = 300
TXT_PAD = 384
SIDE = 32
ITEM_SLOTS = 1024
REACH = 48
BLOCK = 128
LANES = 384
TABLE = 40

norm_eps = 1e-06
bfloat = jnp.bfloat16
single = jnp.float32
VMEM_BYTES = 60 * 1024 * 1024


def dot_nn(a, b):
    return lax.dot_general(a, b, (((1,), (0,)), ((), ())), preferred_element_type=single)


def dot_nt(a, b):
    return lax.dot_general(a, b, (((1,), (1,)), ((), ())), preferred_element_type=single)


def dot_tn(a, b):
    return lax.dot_general(a, b, (((0,), (0,)), ((), ())), preferred_element_type=single)


def swap(values, axis, bit):
    count = lax.axis_size(axis)
    return lax.ppermute(values, axis, [(i, i ^ bit) for i in range(count)])


def shift_devices(values, step):
    count = lax.axis_size("dp") * lax.axis_size("tensor")
    pairs = [(i, i + step) for i in range(count) if 0 <= i + step < count]
    return lax.ppermute(values, ("dp", "tensor"), pairs)


def bit_set(axis, bit):
    return (lax.axis_index(axis) // bit) % 2


def upper_bits():
    count = lax.axis_size("dp")
    bits = []
    bit = 2
    while bit < count:
        bits.append(bit)
        bit *= 2
    return bits


def turns(core):
    bits = upper_bits()
    cut = len(bits) // 2
    return bits[cut:] + bits[:cut] if core else bits


def turn_bit(number, sibling=False):
    core = lax.axis_index("dp") % 2
    first, second = turns(0)[number], turns(1)[number]
    return jnp.where(core == (1 if sibling else 0), first, second)


def swap_path(values, number):
    count = lax.axis_size("dp")
    return lax.ppermute(
        values, "dp", [(i, i ^ turns(i % 2)[number]) for i in range(count)]
    )


def swap_z(values, number):
    ranks, group = lax.axis_size("dp"), lax.axis_size("tensor")
    pairs = []
    for rank in range(ranks):
        bit = (2, 1)[(rank + number) % 2]
        pairs += [(rank * group + peer, rank * group + (peer ^ bit)) for peer in range(group)]
    return lax.ppermute(values, ("dp", "tensor"), pairs)


def peer_of(place, sibling=False):
    core = lax.axis_index("dp") % 2
    if place in (1, 2):
        place = jnp.where(core == (1 if sibling else 0), place, 3 - place)
    return jnp.bitwise_xor(lax.axis_index("tensor"), place)


def turn_z(values, place, sibling=False):
    core = lax.axis_index("dp") % 2
    return jnp.where(
        core == (1 if sibling else 0), values, jnp.swapaxes(values, place, place + 1)
    )


def turn_axes(values, place):
    count = len(upper_bits())
    axes = list(range(values.ndim))
    axes[place : place + count] = [place + turns(1).index(bit) for bit in turns(0)]
    return values.transpose(axes)


def own_turns(values, place, sibling=False):
    core = lax.axis_index("dp") % 2
    return jnp.where(core == (1 if sibling else 0), values, turn_axes(values, place))


def rank_of(step, parts):
    core = step % 2
    rank = jnp.bitwise_xor(lax.axis_index("dp"), core)
    for number in range(len(upper_bits())):
        if parts[number]:
            rank = jnp.bitwise_xor(rank, turn_bit(number, core == 1))
    return rank


def tie(*arrays):
    return lax.optimization_barrier(arrays)


def grow(values, axis, bit, place, absolute):
    other = swap(values, axis, bit)
    if absolute:
        high = bit_set(axis, bit) == 1
        return jnp.stack(
            [jnp.where(high, other, values), jnp.where(high, values, other)], axis=place
        )
    return jnp.stack([values, other], axis=place)


def grow_bits(values, axis, bits, absolute):
    have = []
    for bit in bits:
        values = grow(values, axis, bit, sum(h > bit for h in have), absolute)
        have.append(bit)
    return values


def total(terms):
    summed = terms[0].astype(single)
    for term in terms[1:]:
        summed = summed + term.astype(single)
    return summed.astype(bfloat)


def pick_at(terms, place, number):
    return [lax.index_in_dim(term, number, place, keepdims=False) for term in terms]


def gather_z(piece, absolute):
    return grow_bits(piece, "tensor", [2, 1], absolute)


def grow_path(values):
    for number in range(len(upper_bits())):
        values = jnp.stack([values, swap_path(values, number)])
    return values


def reduce_z(values, bit, place):
    own = bit_set("tensor", bit)
    keep = lax.dynamic_index_in_dim(values, own, place, keepdims=False)
    send = lax.dynamic_index_in_dim(values, 1 - own, place, keepdims=False)
    return total([keep, swap(send, "tensor", bit)])


def halve_path(terms, number, place):
    other = swap_path(total(pick_at(terms, place, 1)), number)
    return pick_at(terms, place, 0) + [other]


def halve_z_once(terms, bit, place):
    place = place + 1 if bit == 1 else place
    other = swap_z(total(pick_at(terms, place, 1)), 1 if bit == 1 else 0)
    return pick_at(terms, place, 0) + [other]


def attention_rows(cols):
    rows = -(-3 * cols // lax.axis_size("dp"))
    return -(-rows // 16) * 16


def bits_of(number, count):
    return [(number >> place) % 2 for place in range(count)]


def row_cuts(rows, cols):
    return sorted({0, rows} | {end % rows for end in (cols, 2 * cols, 3 * cols)})


def assemble_kernel(ranks, group, rows, cols, own, *refs):
    sources, refs = refs[:4], refs[4:]
    *outs, out, sems, out_sems = refs
    me_z = lax.axis_index("tensor")
    cuts = row_cuts(rows, cols)
    count = len(upper_bits())
    copies = []

    def put(source, rank, peer, low, high):
        place = rank * rows + low
        if isinstance(place, int) and place >= 3 * cols:
            return
        kind = place // cols
        target = out.at[kind, peer, pl.ds(pl.multiple_of(place - kind * cols, 16), high - low)]
        copy = pltpu.make_async_copy(source, target, sems.at[len(copies)])
        copies.append((place < 3 * cols, copy))

    for low, high in zip(cuts[:-1], cuts[1:]):
        for rank in range(ranks):
            put(own.at[rank, low:high], rank, me_z, low, high)
        for step in range(ranks):
            place, upper = step // 2 // (ranks // 4), step // 2 % (ranks // 4)
            source = sources[2 * (step % 2) + place]
            rank = rank_of(step, bits_of(step // 2, count))
            for peer in range(1, group):
                put(
                    source.at[upper, peer - 1, low:high],
                    rank,
                    peer_of(peer, step % 2 == 1),
                    low,
                    high,
                )
    for move in ("start", "wait"):
        for live, copy in copies:

            @pl.when(live)
            def _():
                getattr(copy, move)()

    stores = [
        pltpu.make_async_copy(out.at[kind], outs[kind], out_sems.at[kind]) for kind in range(3)
    ]
    for copy in stores:
        copy.start()
    for copy in stores:
        copy.wait()


def assemble(own, parts, cols):
    ranks, rows, features = own.shape
    group = parts[0].shape[1] + 1
    count = (len(row_cuts(rows, cols)) - 1) * ranks * group
    anywhere = pl.BlockSpec(memory_space=pl.ANY)
    return pl.pallas_call(
        functools.partial(assemble_kernel, ranks, group, rows, cols),
        in_specs=[anywhere] * 5,
        out_specs=[anywhere] * 3,
        out_shape=[jax.ShapeDtypeStruct((group, cols, features), own.dtype)] * 3,
        scratch_shapes=[
            pltpu.VMEM((3, group, cols, features), own.dtype),
            pltpu.SemaphoreType.DMA((count,)),
            pltpu.SemaphoreType.DMA((3,)),
        ],
        compiler_params=pltpu.CompilerParams(vmem_limit_bytes=VMEM_BYTES),
        cost_estimate=pl.CostEstimate(
            flops=0, bytes_accessed=ranks * rows * group * features, transcendentals=0
        ),
    )(own, *parts)


def grads_kernel(ranks, group, rows, cols, pairs, *refs):
    inputs, (extra, keep, send, whole, block, sems) = refs[:-6], refs[-6:]
    count = len(upper_bits())
    for kind, (left, right) in enumerate(pairs):
        grad = dot_tn(inputs[left][...], inputs[right][...])
        each = cols // XHEAD
        for peer in range(group):
            if grad.shape[0] == group * cols:
                rows_here = grad[peer * cols : (peer + 1) * cols]
            else:
                for head in range(each):
                    place = (peer * each + head) * XLANE
                    block[head * XHEAD : (head + 1) * XHEAD, :] = grad[place : place + XHEAD]
                rows_here = block[...]
            whole[peer, kind * cols : (kind + 1) * cols, :] = rows_here.astype(bfloat)
    begin = len(pairs) * cols
    used = begin + extra.shape[1]
    for peer in range(group):
        whole[peer, begin:used, :] = extra[peer]
        if used < rows * ranks:
            whole[peer, used:, :] = jnp.zeros((rows * ranks - used, extra.shape[2]), bfloat)
    copies = []
    for step in range(ranks):
        parts = bits_of(step // 2, count)[::-1]
        place = pl.multiple_of(rank_of(step, parts) * rows, 16)
        for peer in range(group):
            source = whole.at[peer_of(peer, step % 2 == 1), pl.ds(place, rows)]
            target = (keep, send)[step % 2].at[step // 2, peer]
            copies.append(pltpu.make_async_copy(source, target, sems.at[len(copies)]))
    for copy in copies:
        copy.start()
    for copy in copies:
        copy.wait()


def grads_call(arrays, pairs, extra, rows, cols):
    ranks, group = lax.axis_size("dp"), lax.axis_size("tensor")
    features = extra.shape[-1]
    height = arrays[0].shape[0]
    inside = pl.BlockSpec(memory_space=pltpu.VMEM)
    anywhere = pl.BlockSpec(memory_space=pl.ANY)
    out = jax.ShapeDtypeStruct((ranks // 2, group, rows, features), bfloat)
    return list(pl.pallas_call(
        functools.partial(grads_kernel, ranks, group, rows, cols, pairs),
        in_specs=[inside] * (len(arrays) + 1),
        out_specs=[anywhere] * 2,
        out_shape=[out, out],
        scratch_shapes=[
            pltpu.VMEM((group, rows * ranks, features), bfloat),
            pltpu.VMEM((cols, features), single),
            pltpu.SemaphoreType.DMA((ranks * group,)),
        ],
        compiler_params=pltpu.CompilerParams(vmem_limit_bytes=VMEM_BYTES),
        cost_estimate=pl.CostEstimate(
            flops=height * features * features,
            bytes_accessed=group * rows * ranks * features // 2,
            transcendentals=0,
        ),
    )(*arrays, extra))


def core_terms(keep, send):
    shape = (2,) * (len(upper_bits()) + 2) + keep.shape[2:]
    return [keep.reshape(shape), swap(send, "dp", 1).reshape(shape)]


def flip_z(values, place):
    for number, bit in enumerate((2, 1)):
        values = jnp.where(
            bit_set("tensor", bit) == 1, jnp.flip(values, place + number), values
        )
    return values


def share_turn(piece, number):
    other = swap_path(piece, number)
    high = jnp.bitwise_and(lax.axis_index("dp"), turn_bit(number)) != 0
    return jnp.stack([jnp.where(high, other, piece), jnp.where(high, piece, other)])


def share_core(piece):
    count = len(upper_bits())
    other = turn_axes(swap(piece, "dp", 1), 0)
    high = lax.axis_index("dp") % 2 == 1
    piece = jnp.stack([jnp.where(high, other, piece), jnp.where(high, piece, other)], axis=count)
    return own_turns(piece, 0).reshape((lax.axis_size("dp"),) + piece.shape[count + 1 :])


def flip_dp(values, place):
    ranks = lax.axis_size("dp")
    shape = values.shape
    bits = upper_bits() + [1]
    bits.sort(reverse=True)
    values = values.reshape(shape[:place] + (2,) * len(bits) + shape[place + 1 :])
    for number, bit in enumerate(bits):
        values = jnp.where(
            bit_set("dp", bit) == 1, jnp.flip(values, place + number), values
        )
    return values.reshape(shape[:place] + (ranks,) + shape[place + 1 :])


def grid_table(bucket):
    grid_height = jnp.where(
        bucket == 0, SIDE, jnp.where(bucket == 1, 3 * SIDE // 4, 3 * SIDE // 2)
    ).astype(jnp.int32)
    grid_width = jnp.where(
        bucket == 0, SIDE, jnp.where(bucket == 1, 5 * SIDE // 4, 5 * SIDE // 8)
    ).astype(jnp.int32)
    return (grid_height, grid_width)


def inside_tap(inner_pos, grid_height, grid_width, row_step, col_step):
    grid_row = inner_pos // grid_width
    grid_col = inner_pos % grid_width
    return (
        (inner_pos < grid_height * grid_width)
        & (grid_row + row_step >= 0)
        & (grid_row + row_step < grid_height)
        & (grid_col + col_step >= 0)
        & (grid_col + col_step < grid_width)
    )


def look_up(table, item):
    known = item[:, None] == jnp.arange(table.shape[0], dtype=jnp.int32)[None, :]
    return jnp.sum(jnp.where(known, table[None, :], 0), axis=1)


def shift_blocks(slots, total, item_bucket, sign, limit):
    item = slots // ITEM_SLOTS
    inner = slots % ITEM_SLOTS
    height, width = grid_table(look_up(item_bucket, item))
    index = jnp.arange(slots.shape[0], dtype=jnp.int32)
    known = (slots >= 0) & (slots < total) & (index < limit)
    columns = jnp.arange(BLOCK + 2 * REACH, dtype=jnp.int32)
    taps = []
    for row_step in (-1, 0, 1):
        for col_step in (-1, 0, 1):
            down, right = sign * row_step, sign * col_step
            inside = known & inside_tap(inner, height, width, down, right)
            target = index % BLOCK + REACH + down * width + right
            taps.append(
                (columns[None, :] == target[:, None]) & inside[:, None]
            )
    return jnp.stack(taps, axis=0).astype(bfloat)


def fetch_weights(core, begin, steps, sources, held, sems):
    own, *others = sources
    rows = held.shape[-2]
    chunks = []
    for step in range(steps):
        first, second = (begin + step) // 2, (begin + step) % 2
        slot = step % 2
        rank = rank_of(core, (first, second))
        place = pl.multiple_of(rank * rows, 16)
        copies = []
        for kind in range(3):
            target = held.at[slot, kind]
            copies.append((own.at[kind, pl.ds(place, rows)], target.at[0]))
            copies.append(
                (others[second].at[first, :, kind * rows : (kind + 1) * rows], target.at[1:4])
            )
        chunks.append(
            [
                pltpu.make_async_copy(source, target, sems.at[slot, number])
                for number, (source, target) in enumerate(copies)
            ]
        )
    for step in range(steps):

        @pl.when(pl.program_id(0) == step)
        def _():
            if step == 0:
                for copy in chunks[0]:
                    copy.start()
            if step + 1 < steps:
                for copy in chunks[step + 1]:
                    copy.start()
            for copy in chunks[step]:
                copy.wait()


def ffn_kernel(
    core,
    begin,
    steps,
    adds,
    own_rows,
    own_pad,
    normed_ref,
    grad_ref,
    reach_ref,
    back_ref,
    last_ref,
    small_ref,
    *refs,
):
    count = 3 if core is not None else 1
    sources = refs[:count]
    added = None
    if adds:
        added = refs[count]
        count += 1
    ffn_ref, dnormed_ref, dweight_ref, dsmall_ref = refs[count : count + 4]
    active, slope, dconv, glu, dexpand, *buffers = refs[count + 4 :]

    def store_grad(kind, grad):
        if added is not None:
            grad = grad + added[0, kind].astype(single)
        dweight_ref[0, kind] = grad.astype(bfloat)

    if core is None:
        weight = lambda kind: sources[0][0, kind]
    else:
        held, sems = buffers
        fetch_weights(core, begin, steps, sources, held, sems)
        slot = lax.rem(pl.program_id(0), 2)
        weight = lambda kind: held[slot, kind].reshape(-1, held.shape[-1])
    @pl.when(pl.program_id(0) == 0)
    def _():
        ffn_ref[...] = jnp.zeros_like(ffn_ref)
        dnormed_ref[...] = jnp.zeros_like(dnormed_ref)

    normed = normed_ref[...]
    channels = small_ref.shape[2]
    for half in range(2):
        expand = dot_nt(normed, weight(half)) + small_ref[half, 10:11, :]
        sig = jax.nn.sigmoid(expand)
        active[half] = (expand * sig).astype(bfloat)
        mid, sig_mid = expand[2 * REACH : 2 * REACH + own_pad], sig[2 * REACH : 2 * REACH + own_pad]
        slope[half] = sig_mid * (1.0 + mid * (1.0 - sig_mid))
    dglu = dot_nt(grad_ref[...], weight(2))
    blocks = grad_ref.shape[0] // BLOCK
    for block in range(blocks):
        begin = block * BLOCK
        convs = []
        for half in range(2):
            moved = dot_nn(
                reach_ref[block], active[half, begin : begin + BLOCK + 2 * REACH, :]
            )
            total = small_ref[half, 9:10, :]
            for tap in range(9):
                total = total + moved[tap * BLOCK : (tap + 1) * BLOCK] * small_ref[half, tap : tap + 1, :]
            convs.append(total)
        value, gate = convs
        sig = jax.nn.sigmoid(gate)
        act = gate * sig
        grad = dglu[begin : begin + BLOCK]
        glu[begin : begin + BLOCK, :] = (value * act).astype(bfloat)
        dconv[0, begin : begin + BLOCK, :] = (grad * act).astype(bfloat)
        dconv[1, begin : begin + BLOCK, :] = (
            grad * value * (sig * (1.0 + gate * (1.0 - sig)))
        ).astype(bfloat)

    glu_own = glu[REACH : REACH + own_pad, :]
    if own_rows != own_pad:
        here = lax.broadcasted_iota(jnp.int32, (own_pad, channels), 0) < own_rows
        glu_own = jnp.where(here, glu_own.astype(single), 0.0).astype(bfloat)
    grad_own = grad_ref[REACH : REACH + own_pad, :]
    ffn_ref[...] += dot_nn(glu_own, weight(2))
    store_grad(2, dot_tn(glu_own, grad_own))
    normed_own = normed_ref[2 * REACH : 2 * REACH + own_pad, :]
    for half in range(2):
        dconv_own = dconv[half, REACH : REACH + own_pad, :].astype(single)
        if own_rows != own_pad:
            dconv_own = jnp.where(here, dconv_own, 0.0)
        dsmall_ref[half, 9:10, :] = jnp.sum(dconv_own, axis=0, keepdims=True)
        sums = [jnp.zeros((8, channels), single) for _ in range(9)]
        dbias = jnp.zeros((8, channels), single)
        for block in range(pl.cdiv(own_pad, BLOCK)):
            begin = block * BLOCK
            height = min(BLOCK, own_pad - begin)
            picks = back_ref[block] if height == BLOCK else last_ref[...]
            moved = dot_nn(picks, dconv[half, begin : begin + height + 2 * REACH, :])
            here_active = active[half, 2 * REACH + begin : 2 * REACH + begin + height, :].astype(single)
            total = jnp.zeros((height, channels), single)
            for tap in range(9):
                part = moved[tap * height : (tap + 1) * height]
                total = total + part * small_ref[half, tap : tap + 1, :]
                sums[tap] = sums[tap] + jnp.sum(
                    (part * here_active).reshape(height // 8, 8, channels), axis=0
                )
            grad = total * slope[half, begin : begin + height, :]
            dbias = dbias + jnp.sum(grad.reshape(height // 8, 8, channels), axis=0)
            dexpand[half, begin : begin + height, :] = grad.astype(bfloat)
        for tap in range(9):
            dsmall_ref[half, tap : tap + 1, :] = jnp.sum(sums[tap], axis=0, keepdims=True)
        dsmall_ref[half, 10:11, :] = jnp.sum(dbias, axis=0, keepdims=True)
        dsmall_ref[half, 11:16, :] = jnp.zeros((5, channels), single)
    for half in range(2):
        grad = dexpand[half]
        dnormed_ref[...] += dot_nn(grad, weight(half))
        store_grad(half, dot_tn(grad, normed_own))


def ffn_call(core, begin, steps, added, own_rows, own_pad, normed, grad, reach, back, last, weights, small):
    wide, features = normed.shape
    tall = grad.shape[0]
    channels = small.shape[2] // 4
    count = channels * steps
    direct = len(weights) > 1
    whole = lambda array: pl.BlockSpec(array.shape, lambda i: (0,) * array.ndim)
    rows = lambda base: pl.BlockSpec((1, 3, channels, features), lambda i: (i + base, 0, 0, 0))
    tiny = lambda base: pl.BlockSpec((2, 16, channels), lambda i: (0, 0, i + base))
    held = pl.BlockSpec((own_pad, features), lambda i: (0, 0))
    flops = 2 * count * features * (2 * wide + tall + 6 * own_pad) + 2 * count * 9 * 256 * 2 * (
        tall + own_pad
    )
    scratch = [
        pltpu.VMEM((2, wide, channels), bfloat),
        pltpu.VMEM((2, own_pad, channels), single),
        pltpu.VMEM((2, tall, channels), bfloat),
        pltpu.VMEM((tall, channels), bfloat),
        pltpu.VMEM((2, own_pad, channels), bfloat),
    ]
    if direct:
        group = weights[1].shape[1] + 1
        piece = weights[1].shape[2] // 3
        scratch += [
            pltpu.VMEM((2, 3, group, piece, features), bfloat),
            pltpu.SemaphoreType.DMA((2, 6)),
        ]
    return pl.pallas_call(
        functools.partial(
            ffn_kernel, core if direct else None, begin, steps, len(added) > 0, own_rows, own_pad
        ),
        grid=(steps,),
        in_specs=[whole(normed), whole(grad), whole(reach), whole(back), whole(last), tiny(begin)]
        + ([pl.BlockSpec(memory_space=pl.ANY)] * 3 if direct else [rows(begin)])
        + [rows(0)] * len(added),
        out_specs=[held, held, rows(0), tiny(0)],
        out_shape=[
            jax.ShapeDtypeStruct((own_pad, features), single),
            jax.ShapeDtypeStruct((own_pad, features), single),
            jax.ShapeDtypeStruct((steps, 3, channels, features), bfloat),
            jax.ShapeDtypeStruct((2, 16, count), single),
        ],
        scratch_shapes=scratch,
        compiler_params=pltpu.CompilerParams(vmem_limit_bytes=VMEM_BYTES),
        cost_estimate=pl.CostEstimate(
            flops=flops // 8, bytes_accessed=2 * count * features, transcendentals=count * tall // 4
        ),
    )(normed, grad, reach, back, last, small, *weights, *added)


def same_head():
    row = lax.broadcasted_iota(jnp.int32, (LANES, LANES), 0) // HEAD
    column = lax.broadcasted_iota(jnp.int32, (LANES, LANES), 1) // HEAD
    return row == column


def head_sums(left, right, extra):
    full = jnp.where(same_head(), dot_tn(left, right), 0.0)
    block = jnp.sum(full.reshape(LANES // HEAD, HEAD, LANES), axis=0)
    rest = jnp.zeros((TABLE - HEAD - 1, LANES), single)
    return jnp.concatenate([block, extra, rest], axis=0)


def head_blocks(table):
    tall = jnp.concatenate([table[:HEAD]] * (LANES // HEAD), axis=0)
    return jnp.where(same_head(), tall, 0.0).astype(bfloat)


def masked(values, column):
    return (values.astype(single) * column).astype(bfloat)


def softplus(values):
    return jnp.maximum(values, 0.0) + jnp.log1p(jnp.exp(-jnp.abs(values)))


def project_kernel(
    normed, wq, wk, wv, first, second, pre_q, pre_k, query, keys, values, table_1, table_2
):
    rows = normed[...]
    pre_q[...] = dot_nt(rows, wq[...])
    query[...] = softplus(pre_q[...]).astype(bfloat)
    pre_k[...] = dot_nt(rows, wk[...])
    key = softplus(pre_k[...]).astype(bfloat)
    keys[...] = key
    value = dot_nt(rows, wv[...]).astype(bfloat)
    values[...] = value
    for column, table in ((first, table_1), (second, table_2)):
        chosen = masked(key, column[...])
        table[...] = head_sums(
            chosen, value, jnp.sum(chosen.astype(single), axis=0, keepdims=True)
        )


def attend_kernel(query, state_1, state_2, first, second, wo, ratio, den, attn, out):
    @pl.when(pl.program_id(0) == 0)
    def _():
        out[...] = jnp.zeros_like(out)

    rows = query[...]
    parts = ((first[...], state_1[...]), (second[...], state_2[...]))
    numerator, weights = 0.0, 0.0
    for column, state in parts:
        numerator = numerator + dot_nn(masked(rows, column), head_blocks(state))
        weights = weights + column * state[HEAD : HEAD + 1]
    ones = same_head().astype(single).astype(bfloat)
    den[...] = dot_nn((rows.astype(single) * weights).astype(bfloat), ones)
    ratio[...] = numerator / den[...]
    attn[...] = ratio[...].astype(bfloat)
    out[...] += dot_nn(attn[...], wo[...])


def attend_back_kernel(
    grad, wo, ratio, den, query, pre_q, state_1, state_2, first, second, dquery, table_1, table_2
):
    dratio = dot_nt(grad[...], wo[...])
    ones = same_head().astype(single).astype(bfloat)
    dnumer = dratio / den[...]
    dden = -dot_nn((dratio * ratio[...]).astype(bfloat), ones) / den[...]
    rows = query[...]
    total_grad, weights = 0.0, 0.0
    for column, state, table in (
        (first[...], state_1[...], table_1),
        (second[...], state_2[...], table_2),
    ):
        chosen = (dnumer * column).astype(bfloat)
        total_grad = total_grad + dot_nt(chosen, head_blocks(state))
        weights = weights + column * state[HEAD : HEAD + 1]
        extra = jnp.sum(rows.astype(single) * dden * column, axis=0, keepdims=True)
        table[...] = head_sums(rows, chosen, extra)
    total_grad = total_grad + weights * dden
    dquery[...] = (total_grad * jax.nn.sigmoid(pre_q[...])).astype(bfloat)


def project_back_kernel(
    dquery, keys, values, pre_k, state_1, state_2, first, second, wq, wk, wv, dkeys, dvalues, dnormed
):
    @pl.when(pl.program_id(0) == 0)
    def _():
        dnormed[...] = jnp.zeros_like(dnormed)

    key_grad, value_grad = 0.0, 0.0
    for column, state in ((first[...], state_1[...]), (second[...], state_2[...])):
        block = head_blocks(state)
        key_grad = key_grad + dot_nt(masked(values[...], column), block)
        key_grad = key_grad + column * state[HEAD : HEAD + 1]
        value_grad = value_grad + dot_nn(masked(keys[...], column), block)
    dkeys[...] = (key_grad * jax.nn.sigmoid(pre_k[...])).astype(bfloat)
    dvalues[...] = value_grad.astype(bfloat)
    dnormed[...] += (
        dot_nn(dquery[...], wq[...]) + dot_nn(dkeys[...], wk[...]) + dot_nn(dvalues[...], wv[...])
    )


def lane_call(kernel, kinds, arrays, outs, rows, features):
    specs = {
        "l": pl.BlockSpec((rows, LANES), lambda g: (0, g)),
        "w": pl.BlockSpec((LANES, features), lambda g: (g, 0)),
        "t": pl.BlockSpec((TABLE, LANES), lambda g: (0, g)),
        "c": pl.BlockSpec((rows, 1), lambda g: (0, 0)),
        "a": pl.BlockSpec((rows, features), lambda g: (0, 0)),
    }
    shape = {"l": (rows, features), "t": (TABLE, features), "a": (rows, features)}
    return pl.pallas_call(
        kernel,
        grid=(features // LANES,),
        in_specs=[specs[kind] for kind in kinds],
        out_specs=[specs[kind] for kind, _ in outs],
        out_shape=[jax.ShapeDtypeStruct(shape[kind], dtype) for kind, dtype in outs],
        compiler_params=pltpu.CompilerParams(vmem_limit_bytes=VMEM_BYTES),
        cost_estimate=pl.CostEstimate(
            flops=rows * features * features, bytes_accessed=rows * features, transcendentals=0
        ),
    )(*arrays)


def head_probs(query, keys, lengths):
    scores = dot_nt(query, keys) * (XHEAD ** (-0.5))
    place = lax.broadcasted_iota(jnp.int32, scores.shape, 1)
    live = place < lengths
    scores = jnp.where(live, scores, -1e30)
    top = jnp.max(scores, axis=-1, keepdims=True)
    powers = jnp.exp(scores - top)
    return powers / jnp.sum(powers, axis=-1, keepdims=True)


def cross_kernel(query_ref, keys_ref, vals_ref, length_ref, mix_ref):
    probs = head_probs(query_ref[...], keys_ref[0], length_ref[...])
    mix_ref[...] = dot_nn(probs.astype(bfloat), vals_ref[0]).astype(bfloat)


def cross_back_kernel(
    query_ref, keys_ref, vals_ref, length_ref, dmix_ref, dquery_ref, dkeys_ref, dvals_ref, dbias_ref
):
    query, keys, dmix = query_ref[...], keys_ref[0], dmix_ref[...]
    probs = head_probs(query, keys, length_ref[...])
    dprobs = dot_nt(dmix, vals_ref[0])
    dvals_ref[0] = dot_tn(dmix, probs.astype(bfloat))[:XHEAD].astype(bfloat)
    row_dot = jnp.sum(probs * dprobs, axis=-1, keepdims=True)
    dscores = (probs * (dprobs - row_dot) * (XHEAD ** (-0.5))).astype(bfloat)
    dquery = dot_nn(dscores, keys)
    dbias_ref[...] = jnp.sum(dquery, axis=0, keepdims=True)
    dquery_ref[...] = dquery.astype(bfloat)
    dkeys_ref[0] = dot_tn(query, dscores)[:XHEAD].astype(bfloat)


def cross_specs(rows):
    lane = pl.BlockSpec((rows, XLANE), lambda h: (0, h))
    text = pl.BlockSpec((1, TXT_PAD, XLANE), lambda h: (h, 0, 0))
    length = pl.BlockSpec((rows, 1), lambda h: (0, 0))
    return lane, text, length


def cross_call(query, keys, vals, lengths):
    rows, heads = query.shape[0], keys.shape[0]
    lane, text, length = cross_specs(rows)
    return pl.pallas_call(
        cross_kernel,
        grid=(heads,),
        in_specs=[lane, text, text, length],
        out_specs=lane,
        out_shape=jax.ShapeDtypeStruct((rows, heads * XLANE), bfloat),
        compiler_params=pltpu.CompilerParams(vmem_limit_bytes=VMEM_BYTES),
        cost_estimate=pl.CostEstimate(
            flops=heads * rows * TXT_PAD * XLANE,
            bytes_accessed=2 * rows * heads * XLANE,
            transcendentals=heads * rows * TXT_PAD // 8,
        ),
    )(query, keys, vals, lengths)


def cross_back_call(query, keys, vals, lengths, dmix):
    rows, heads = query.shape[0], keys.shape[0]
    lane, text, length = cross_specs(rows)
    return pl.pallas_call(
        cross_back_kernel,
        grid=(heads,),
        in_specs=[lane, text, text, length, lane],
        out_specs=[
            lane,
            pl.BlockSpec((1, XHEAD, TXT_PAD), lambda h: (h, 0, 0)),
            pl.BlockSpec((1, XHEAD, TXT_PAD), lambda h: (h, 0, 0)),
            pl.BlockSpec((1, XLANE), lambda h: (0, h)),
        ],
        out_shape=[
            jax.ShapeDtypeStruct((rows, heads * XLANE), bfloat),
            jax.ShapeDtypeStruct((heads, XHEAD, TXT_PAD), bfloat),
            jax.ShapeDtypeStruct((heads, XHEAD, TXT_PAD), bfloat),
            jax.ShapeDtypeStruct((1, heads * XLANE), single),
        ],
        compiler_params=pltpu.CompilerParams(vmem_limit_bytes=VMEM_BYTES),
        cost_estimate=pl.CostEstimate(
            flops=heads * rows * TXT_PAD * XLANE,
            bytes_accessed=2 * rows * heads * XLANE,
            transcendentals=heads * rows * TXT_PAD // 8,
        ),
    )(query, keys, vals, lengths, dmix)


def norm_parts(values):
    centred = values - jnp.mean(values, axis=-1, keepdims=True)
    inv_std = lax.rsqrt(jnp.mean(centred * centred, axis=-1, keepdims=True) + norm_eps)
    return (centred * inv_std, inv_std)


def norm_back(grad_in, normal, inv_std, scale):
    scaled = grad_in * (1.0 + scale)
    return (
        scaled
        - jnp.mean(scaled, axis=-1, keepdims=True)
        - normal * jnp.mean(scaled * normal, axis=-1, keepdims=True)
    ) * inv_std


def pad_rows(values, rows):
    return jnp.pad(values, ((0, rows - values.shape[0]),) + ((0, 0),) * (values.ndim - 1))


def pad_heads(rows, heads):
    features = rows.shape[1]
    shaped = rows.reshape(heads, XHEAD, features)
    return jnp.pad(shaped, ((0, 0), (0, XLANE - XHEAD), (0, 0))).reshape(heads * XLANE, features)


def local(
    tokens,
    cotangent,
    item_bucket,
    text_len,
    t_mod,
    text_tokens,
    shift_table,
    w_qkv,
    w_out,
    out_bias,
    w_xq,
    xq_bias,
    w_xkv,
    xv_bias,
    w_xo,
    xo_bias,
    w_in,
    in_bias,
    dw_weight,
    dw_bias,
    w_pt,
):
    group = lax.axis_size("tensor")
    ranks = lax.axis_size("dp")
    me_z = lax.axis_index("tensor")
    me_d = lax.axis_index("dp")
    own_rows, width = tokens.shape
    own_pad = -(-own_rows // 32) * 32
    tall = -(-(own_rows + 2 * REACH) // BLOCK) * BLOCK
    wide = tall + 2 * REACH
    total_rows = own_rows * group * ranks
    item_count = t_mod.shape[0]
    heads = width // HEAD
    xheads = width // XHEAD
    cols = w_xq.shape[1]
    channels = w_in.shape[2]
    padded_channels = -(-channels // 384) * 384
    own_start = (me_d * group + me_z) * own_rows
    first_item = own_start // ITEM_SLOTS
    last_item = (own_start + own_rows - 1) // ITEM_SLOTS
    two_items = last_item != first_item

    bits = upper_bits()
    att_piece = attention_rows(cols)
    att_pad = att_piece * ranks
    att_rows = 3 * cols
    rows_qkv = pad_rows(w_qkv.transpose(1, 2, 0).reshape(att_rows, width), att_pad)
    rows_mix = pad_rows(jnp.concatenate([w_out, w_xq.T, w_xo], axis=0), att_pad)
    ffn_piece = padded_channels // ranks
    half_count = padded_channels * group // 2
    rows_ffn = jnp.stack(
        [pad_rows(rows, padded_channels) for rows in (w_in[:, 0].T, w_in[:, 1].T, w_pt)]
    )
    own_qkv = rows_qkv.reshape(ranks, att_piece, width)
    own_mix = rows_mix.reshape(ranks, att_piece, width)
    piece_1 = lax.dynamic_index_in_dim(own_qkv, me_d, 0, keepdims=False)
    piece_2 = lax.dynamic_index_in_dim(own_mix, me_d, 0, keepdims=False)

    def near_z(piece, far):
        near = swap_z(jnp.stack([piece, far]), 1)
        return jnp.stack([near[0], far, near[1]])

    def turn(values, number):
        return jnp.stack([values, swap_path(values, number)])

    def mid_turns(values):
        for number in range(1, len(bits) - 1):
            values = turn(values, number)
        return values.reshape((-1,) + values.shape[-3:])

    def last_turn(values):
        return swap_path(values, len(bits) - 1)

    own_slots = own_start + jnp.arange(own_rows, dtype=jnp.int32)
    item = own_slots // ITEM_SLOTS
    in_first = (item == first_item)[:, None]
    in_second = jnp.logical_not(in_first)
    mod_first = shift_table + lax.dynamic_index_in_dim(t_mod, first_item, 0, keepdims=False)
    mod_second = shift_table + lax.dynamic_index_in_dim(t_mod, last_item, 0, keepdims=False)
    row_mod = lambda number: jnp.where(in_first, mod_first[number][None], mod_second[number][None])
    shift_a, scale_a, gate_a, shift_f, scale_f, gate_f = [row_mod(number) for number in range(6)]
    tokens_f = tokens.astype(single)
    grad_out = cotangent.astype(single)
    normal_a, inv_std_a = norm_parts(tokens_f)
    normed = (normal_a * (1.0 + scale_a) + shift_a).astype(bfloat)

    far_1 = swap_z(piece_1, 0)
    far_1, normed = tie(far_1, normed)
    wave_1 = near_z(piece_1, far_1)
    wave_1, item_bucket, piece_2 = tie(wave_1, item_bucket, piece_2)
    far_2 = swap_z(piece_2, 0)
    wave_1 = turn(wave_1, 0)
    inner = own_slots % ITEM_SLOTS
    grid_h, grid_w = grid_table(look_up(item_bucket, item))
    valid = inner < grid_h * grid_w
    live = valid.astype(single)[:, None]
    tall_slots = own_start - REACH + jnp.arange(tall, dtype=jnp.int32)
    reach = shift_blocks(tall_slots, total_rows, item_bucket, 1, tall)
    reach = reach.reshape(9, tall // BLOCK, BLOCK, -1).transpose(1, 0, 2, 3)
    reach = reach.reshape(tall // BLOCK, 9 * BLOCK, -1)
    wave_1, reach, text_tokens = tie(wave_1, reach, text_tokens)
    wave_1 = mid_turns(wave_1)
    last_1 = last_turn(wave_1)
    core_1 = swap(wave_1, "dp", 1)
    wave_2 = near_z(piece_2, far_2)
    text_rows_here = text_tokens.shape[0]
    text_half = pad_rows(text_tokens, -(-text_rows_here // 16) * 16)
    text_half = lax.dynamic_index_in_dim(
        text_half.reshape(2, -1, width), me_d % 2, 0, keepdims=False
    )
    text_far = swap(text_half, "tensor", 2)
    pad_slots = own_start + jnp.arange(own_pad, dtype=jnp.int32)
    back = shift_blocks(pad_slots, total_rows, item_bucket, -1, own_rows)
    full_blocks = own_pad // BLOCK
    rest = own_pad - full_blocks * BLOCK
    back_full = back[:, : full_blocks * BLOCK].reshape(9, full_blocks, BLOCK, -1).transpose(1, 0, 2, 3)
    back_full = back_full.reshape(full_blocks, 9 * BLOCK, -1)
    rest = max(rest, 32)
    back_last = back[:, own_pad - rest :, : rest + 2 * REACH].reshape(9 * rest, -1)
    d_ffn = (grad_out * live * gate_f).astype(bfloat)
    wave_1, last_1, core_1, wave_2, back_full, back_last, d_ffn, text_far, rows_ffn = tie(
        wave_1, last_1, core_1, wave_2, back_full, back_last, d_ffn, text_far, rows_ffn
    )
    core_last_1 = swap(last_1, "dp", 1)
    piece_3 = lax.dynamic_slice_in_dim(rows_ffn, me_d * ffn_piece, ffn_piece, 1)
    piece_3 = piece_3.reshape(3 * ffn_piece, width)
    core_last_1, wave_2, piece_3 = tie(core_last_1, wave_2, piece_3)
    wave_2 = turn(wave_2, 0)
    far_3 = swap_z(piece_3, 0)
    text_near = swap(jnp.stack([text_half, text_far]), "tensor", 1)
    wq, wk, wv = [
        part.reshape(width, width) for part in assemble(own_qkv, (wave_1, last_1, core_1, core_last_1), cols)
    ]
    wq, wk, wv, wave_2, text_near = tie(wq, wk, wv, wave_2, text_near)
    wave_2 = mid_turns(wave_2)
    last_2 = last_turn(wave_2)
    core_2 = swap(wave_2, "dp", 1)
    in_order = lambda rel: [
        lax.dynamic_index_in_dim(rel, me_z ^ peer, 0, keepdims=False) for peer in range(group)
    ]
    by_core = lambda one, two: jnp.stack(
        [jnp.where(me_d % 2 == 0, one, two), jnp.where(me_d % 2 == 0, two, one)]
    )
    text_rel = jnp.stack([text_half, text_near[0], text_far, text_near[1]])
    text_other = swap(text_rel, "dp", 1)

    first_live = (in_first & valid[:, None]).astype(single)
    second_live = (in_second & valid[:, None]).astype(single)
    first_all, second_all = in_first.astype(single), in_second.astype(single)
    over_lanes = functools.partial(lane_call, rows=own_rows, features=width)
    pre_q, pre_k, query, keys, values, table_1, table_2 = over_lanes(
        project_kernel,
        "awwwcc",
        (normed, wq, wk, wv, first_live, second_live),
        (("l", single), ("l", single), ("l", bfloat), ("l", bfloat), ("l", bfloat), ("t", single), ("t", single)),
    )

    span_rows = own_rows * group
    span_start = me_d * span_rows
    span_first = span_start // ITEM_SLOTS
    span_last = (span_start + span_rows - 1) // ITEM_SLOTS
    span_items = (span_rows - 2) // ITEM_SLOTS + 2

    def item_table(first_part, second_part):
        parts = []
        for number in range(span_items):
            chosen = jnp.where(first_item - span_first == number, first_part, 0.0)
            also = two_items & (last_item - span_first == number)
            parts.append(chosen + jnp.where(also, second_part, 0.0))
        return jnp.stack(parts).astype(bfloat)

    def item_sums(table):
        count = ranks - 1
        tail_part = lax.dynamic_index_in_dim(table, span_last - span_first, 0, keepdims=False)
        below = lax.ppermute(tail_part, "dp", [(i, i + 1) for i in range(count)])
        above = lax.ppermute(table[0], "dp", [(i + 1, i) for i in range(count)])
        below_same = (span_start - 1) // ITEM_SLOTS == span_first
        above_same = (span_start + span_rows) // ITEM_SLOTS == span_last
        sums = []
        for number in (first_item, last_item):
            part = lax.dynamic_index_in_dim(table, number - span_first, 0, keepdims=False)
            part = part.astype(single)
            part = part + jnp.where(below_same & (number == span_first), below.astype(single), 0.0)
            part = part + jnp.where(above_same & (number == span_last), above.astype(single), 0.0)
            sums.append(part)
        return sums

    small_rel = jnp.concatenate([dw_weight, dw_bias[None], in_bias[None]], axis=0)
    small_rel = jnp.pad(small_rel, ((0, 5), (0, 0), (0, padded_channels - channels)))
    sizes = small_rel.size
    small_rel = jnp.concatenate([small_rel.reshape(-1), xq_bias]).astype(bfloat)
    small_tall = -(-small_rel.size // (32 * cols)) * 16
    small_rel = jnp.pad(small_rel, (0, 2 * small_tall * cols - small_rel.size))
    small_half = lax.dynamic_index_in_dim(
        small_rel.reshape(2, small_tall, cols), me_d % 2, 0, keepdims=False
    )
    down = tuple(range(2, 2 + len(bits)))

    table = item_table(table_1, table_2)
    table, text_other, far_3 = tie(table, text_other, far_3)
    table = total([table, swap_z(table, 0)])
    text_rel = by_core(text_rel, text_other).swapaxes(0, 1).reshape(group, -1, width)
    text_all = jnp.concatenate(in_order(text_rel[:, :text_rows_here]))
    text_kv = jnp.einsum("td,dke->tke", text_all, w_xkv, preferred_element_type=single)
    xkv_own = jnp.stack([text_kv[:, 0], text_kv[:, 1] + xv_bias], axis=0).astype(bfloat)
    both_half = jnp.concatenate(
        [lax.dynamic_index_in_dim(xkv_own, me_d % 2, 0, keepdims=False), small_half], axis=0
    )
    table, both_half, last_2, core_2 = tie(table, both_half, last_2, core_2)
    table = total([table, swap_z(table, 1)])
    both_far = swap(both_half, "tensor", 2)
    core_last_2 = swap(last_2, "dp", 1)
    table, both_far, core_last_2, far_3 = tie(table, both_far, core_last_2, far_3)
    state_1, state_2 = item_sums(table)
    wave_3 = near_z(piece_3, far_3)
    both_near = swap(jnp.stack([both_half, both_far]), "tensor", 1)
    wo, wxq, wxo = [
        part.reshape(width, width) for part in assemble(own_mix, (wave_2, last_2, core_2, core_last_2), cols)
    ]
    wxq_pad = pad_heads(wxq, xheads)
    wxo_pad = pad_heads(wxo, xheads)
    state_1, state_2, wo, wxq_pad, wxo_pad, both_near = tie(
        state_1, state_2, wo, wxq_pad, wxo_pad, both_near
    )
    both_rel = jnp.stack([both_half, both_near[0], both_far, both_near[1]])
    both_other = swap(both_rel, "dp", 1)
    attn_ratio, denominator, attn, attn_sum = over_lanes(
        attend_kernel,
        "lttccw",
        (query, state_1, state_2, first_all, second_all, wo),
        (("l", single), ("l", single), ("l", bfloat), ("a", single)),
    )
    attn_out = attn_sum + out_bias
    after_attn = tokens_f + live * gate_a * attn_out

    after_attn, wave_3, both_other = tie(after_attn, wave_3, both_other)
    wave_3 = turn(wave_3, 0)
    cross_in = after_attn.astype(bfloat)
    xq_product = dot_nt(cross_in, wxq_pad)
    both = by_core(both_rel, both_other)
    xkv_all = both[:, :, :TXT].swapaxes(0, 1)
    xkv_all = jnp.stack(in_order(xkv_all)).reshape(group, 2, TXT, cols // XHEAD, XHEAD)
    xkv_all = xkv_all.transpose(1, 0, 3, 2, 4).reshape(2, xheads, TXT, XHEAD)
    xkv_all = jnp.pad(xkv_all, ((0, 0), (0, 0), (0, TXT_PAD - TXT), (0, XLANE - XHEAD)))
    xkeys, xvals = xkv_all[0], xkv_all[1]
    small = both[:, :, TXT:].swapaxes(0, 1).reshape(group, -1).astype(single)
    xq_rel = small[:, sizes : sizes + cols]
    small = flip_dp(small[:, :sizes].reshape(group, 16, 2, ranks, ffn_piece), 3)
    small = small.reshape((group, 16, 2) + (2,) * (len(bits) + 1) + (ffn_piece,))
    small = jnp.moveaxis(small, 0, len(bits) + 3)
    small = small.transpose((len(bits) + 2, 1, 0) + down[::-1] + (len(bits) + 3, len(bits) + 4))
    small = small.reshape(small.shape[:-2] + (2, 2, ffn_piece))
    small = [
        turn_z(own_turns(small[core], 2, core == 1), 2 + len(bits), core == 1).reshape(
            2, 16, half_count
        )
        for core in (0, 1)
    ]
    xq_bias_all = jnp.stack(in_order(xq_rel)).reshape(xheads, XHEAD)
    xq_bias_all = jnp.pad(xq_bias_all, ((0, 0), (0, XLANE - XHEAD))).reshape(xheads * XLANE)
    lengths = look_up(text_len, item)[:, None]
    xquery = (xq_product + xq_bias_all).astype(bfloat)
    xquery, wave_3 = tie(xquery, wave_3)
    wave_3 = mid_turns(wave_3)
    last_3 = last_turn(wave_3)
    core_3 = swap(wave_3, "dp", 1)
    cross_mix = cross_call(xquery, xkeys, xvals, lengths)
    cross_out = dot_nn(cross_mix, wxo_pad) + xo_bias
    after_cross = after_attn + live * cross_out

    normal_f, inv_std_f = norm_parts(after_cross)
    normed_ffn = (normal_f * (1.0 + scale_f) + shift_f).astype(bfloat)
    normed_ffn, wave_3, last_3, core_3, *small = tie(normed_ffn, wave_3, last_3, core_3, *small)
    core_last_3 = swap(last_3, "dp", 1)
    def ffn_half(core):
        count = len(bits)
        own = flip_dp(rows_ffn.reshape(3, ranks, ffn_piece, width), 1)
        own = own.reshape((3,) + (2,) * (count + 1) + (ffn_piece, width))
        own = jnp.moveaxis(lax.index_in_dim(own, core, count + 1, keepdims=False), 0, count)
        own = own_turns(own.transpose(tuple(range(count))[::-1] + (count, count + 1, count + 2)), 0, core == 1)
        others = jnp.concatenate(((wave_3, last_3), (core_3, core_last_3))[core])
        others = others.reshape((2,) * count + (group - 1, 3, ffn_piece, width))
        others = others.transpose(tuple(range(count))[::-1] + tuple(range(count, count + 4)))
        joined = jnp.concatenate([jnp.expand_dims(own, count), others], axis=count)
        joined = jnp.moveaxis(joined, count + 1, 2)
        return joined.reshape(4, 3, half_count // 4, width)

    direct = ffn_piece % 16 == 0 and len(bits) == 2
    weights_ffn = [
        [rows_ffn, *((wave_3, last_3), (core_3, core_last_3))[core]] if direct else [ffn_half(core)]
        for core in (0, 1)
    ]

    above = shift_devices(
        jnp.concatenate([normed_ffn[own_rows - 2 * REACH :], d_ffn[own_rows - REACH :]], axis=0), 1
    )
    below = shift_devices(jnp.concatenate([normed_ffn[: 2 * REACH], d_ffn[:REACH]], axis=0), -1)
    normed_ext = pad_rows(
        jnp.concatenate([above[: 2 * REACH], normed_ffn, below[: 2 * REACH]], axis=0), wide
    )
    d_ffn_ext = pad_rows(
        jnp.concatenate([above[2 * REACH :], d_ffn, below[2 * REACH :]], axis=0), tall
    )
    tables = (reach, back_full, back_last)
    def ffn_part(core, begin, *added):
        return ffn_call(
            core, begin, 2, added, own_rows, own_pad, normed_ext, d_ffn_ext, *tables, weights_ffn[core], small[core]
        )

    part_3 = ffn_part(1, 2)
    normed_ext, *part_3 = tie(normed_ext, *part_3)
    other_3 = swap(part_3[2], "dp", 1)
    part_2 = ffn_part(1, 0)
    normed_ext, other_3, *part_2 = tie(normed_ext, other_3, *part_2)
    other_2 = swap(part_2[2], "dp", 1)
    part_1 = ffn_part(0, 2, other_3)
    normed_ext, other_2, *part_1 = tie(normed_ext, other_2, *part_1)
    turn_shape = (2, 3) + (2,) * len(bits) + (ffn_piece, width)
    ffn_got = swap_path(part_1[2], 0).reshape(turn_shape)
    part_0 = ffn_part(0, 0, other_2)
    parts = (part_0, part_1, part_2, part_3)
    ffn_out = sum(part[0] for part in parts)[:own_rows]
    d_normed_ffn = sum(part[1] for part in parts)[:own_rows]
    ffn_terms = [part_0[2].reshape(turn_shape), ffn_got]
    d_small_half = [
        jnp.concatenate([low[3], high[3]], axis=2) for low, high in ((part_0, part_1), (part_2, part_3))
    ]

    d_small = jnp.stack(
        [
            turn_z(
                own_turns(
                    part.astype(bfloat).reshape((2, 16) + (2,) * (len(bits) + 2) + (ffn_piece,)),
                    2,
                    core == 1,
                ),
                2 + len(bits),
                core == 1,
            )
            for core, part in enumerate(d_small_half)
        ],
        axis=len(bits) + 2,
    )
    order = (len(bits) + 3, len(bits) + 4, 0, 1) + down[::-1] + (len(bits) + 2, len(bits) + 5)
    d_small = flip_z(d_small.transpose(order), 0)
    d_small = d_small.reshape(group, 2, 16, ranks, ffn_piece)[:, :, :11]
    d_small = flip_dp(d_small, 3).reshape(group, -1)
    small_rows = -(-d_small.shape[1] // (16 * width)) * 16
    d_small = jnp.pad(d_small, ((0, 0), (0, small_rows * width - d_small.shape[1])))
    d_small = d_small.reshape(group, small_rows, width)

    out_tokens = (after_cross + live * gate_f * ffn_out).astype(bfloat)
    d_gate_f = grad_out * live * ffn_out
    grad_cross = grad_out + norm_back(d_normed_ffn, normal_f, inv_std_f, scale_f)

    d_cross = grad_cross * live
    d_xo_bias = jnp.sum(d_cross, axis=0)
    d_cross_low = d_cross.astype(bfloat)
    d_cross_low, ffn_terms[-1] = tie(d_cross_low, ffn_terms[-1])
    for stage in range(1, len(bits)):
        ffn_terms = halve_path(ffn_terms, stage, 0 if stage == 1 else 1)
    d_mix = dot_nt(d_cross_low, wxo_pad).astype(bfloat)
    d_query_low, d_keys, d_vals, d_xq_part = cross_back_call(xquery, xkeys, xvals, lengths, d_mix)
    d_query_low, ffn_terms[-1] = tie(d_query_low, ffn_terms[-1])
    ffn_terms = halve_z_once(ffn_terms, 1, 1)
    grad_attn = grad_cross + dot_nn(d_query_low, wxq_pad)

    d_attn_out = grad_attn * live * gate_a
    d_gate_a = grad_attn * live * attn_out
    d_out_bias = jnp.sum(d_attn_out, axis=0)
    d_attn_low = d_attn_out.astype(bfloat)

    text_rows = 2 * cols * TXT_PAD // width
    mix_rows = -(-(att_rows + text_rows + small_rows) // (16 * ranks)) * 16
    lanes = width // TXT_PAD
    d_kv = jnp.concatenate(
        [d_keys.reshape(group, cols, TXT_PAD), d_vals.reshape(group, cols, TXT_PAD)], axis=1
    )
    d_kv = jnp.concatenate(
        [d_kv[:, number * text_rows : (number + 1) * text_rows] for number in range(lanes)], axis=2
    )
    mix_arrays = [
        attn,
        d_attn_low,
        d_query_low,
        cross_in,
        cross_mix,
        d_cross_low,
    ]
    mix_extra = jnp.concatenate([d_kv, d_small], axis=1)
    d_query_in, table_1, table_2 = over_lanes(
        attend_back_kernel,
        "awllllttcc",
        (d_attn_low, wo, attn_ratio, denominator, query, pre_q, state_1, state_2, first_all, second_all),
        (("l", bfloat), ("t", single), ("t", single)),
    )
    d_table = item_table(table_1, table_2)
    def mod_sum(rows):
        return jnp.stack(
            [
                jnp.sum(jnp.where(in_first, rows, 0.0), axis=0),
                jnp.sum(jnp.where(in_second, rows, 0.0), axis=0),
            ]
        )

    d_table, mix_extra, ffn_terms[-1] = tie(d_table, mix_extra, ffn_terms[-1])
    d_table = total([d_table, swap_z(d_table, 0)])
    mod_sums = [
        mod_sum(rows) for rows in (d_gate_a, d_normed_ffn, d_normed_ffn * normal_f, d_gate_f)
    ]
    d_table, d_out_bias, d_xo_bias, *mod_sums = tie(d_table, d_out_bias, d_xo_bias, *mod_sums)
    d_table = total([d_table, swap_z(d_table, 1)])
    mix_grads = grads_call(mix_arrays, ((0, 1), (2, 3), (4, 5)), mix_extra, mix_rows, cols)
    d_table, mix_grads[1] = tie(d_table, mix_grads[1])
    mix_terms = core_terms(*mix_grads)
    d_state_1, d_state_2 = item_sums(d_table)
    d_state_1, d_state_2, mix_terms[1] = tie(d_state_1, d_state_2, mix_terms[1])
    mix_terms = halve_path(mix_terms, 0, 0)
    ffn_terms = halve_z_once(ffn_terms, 2, 1)
    d_keys_in, d_values_low, d_normed = over_lanes(
        project_back_kernel,
        "llllttccwww",
        (d_query_in, keys, values, pre_k, d_state_1, d_state_2, first_live, second_live, wq, wk, wv),
        (("l", bfloat), ("l", bfloat), ("a", single)),
    )
    d_tokens = grad_attn + norm_back(d_normed, normal_a, inv_std_a, scale_a)

    sums = jnp.stack([mod_sum(d_normed), mod_sum(d_normed * normal_a)] + mod_sums, axis=1)
    items = jnp.arange(item_count, dtype=jnp.int32)[None, :, None]
    mod_table = jnp.where(items == first_item, sums[0][:, None], 0.0) + jnp.where(
        (items == first_item + 1), sums[1][:, None], 0.0
    )
    xq_row = d_xq_part.reshape(xheads, XLANE)[:, :XHEAD].reshape(width)
    rows_all = jnp.concatenate(
        [mod_table.reshape(-1, width), jnp.stack([d_out_bias, d_xo_bias, xq_row], axis=0)], axis=0
    )
    rows_count = rows_all.shape[0]
    last_rows = -(-(att_rows + rows_count) // (16 * ranks)) * 16
    spare = -(-rows_count // 16) * 16
    rows_all = pad_rows(rows_all.astype(bfloat), spare)
    rows_all = jnp.broadcast_to(rows_all[None], (group, spare, width))

    rows_all, mix_terms[-1] = tie(rows_all, mix_terms[-1])
    for stage in range(1, len(bits)):
        mix_terms = halve_path(mix_terms, stage, 0)
    qkv_grads = grads_call(
        [d_query_in, d_keys_in, d_values_low, normed],
        ((0, 3), (1, 3), (2, 3)),
        rows_all,
        last_rows,
        cols,
    )
    qkv_grads[1], ffn_terms[-1], mix_terms[-1] = tie(qkv_grads[1], ffn_terms[-1], mix_terms[-1])
    qkv_terms = core_terms(*qkv_grads)
    qkv_terms[1], mix_terms[-1] = tie(qkv_terms[1], mix_terms[-1])
    qkv_terms = halve_path(qkv_terms, 0, 0)
    mix_terms = halve_z_once(mix_terms, 1, 0)
    qkv_terms[-1], mix_terms[-1] = tie(qkv_terms[-1], mix_terms[-1])
    for stage in range(1, len(bits)):
        qkv_terms = halve_path(qkv_terms, stage, 0)
    mix_terms = halve_z_once(mix_terms, 2, 0)
    qkv_terms[-1], mix_terms[-1], ffn_terms[-1] = tie(
        qkv_terms[-1], mix_terms[-1], ffn_terms[-1]
    )
    qkv_terms = halve_z_once(qkv_terms, 1, 0)
    d_mix_all = share_turn(total(mix_terms), 0)
    d_ffn_all = share_turn(total(ffn_terms), 0)
    qkv_terms[-1], d_mix_all, d_ffn_all = tie(qkv_terms[-1], d_mix_all, d_ffn_all)
    qkv_terms = halve_z_once(qkv_terms, 2, 0)
    for stage in range(1, len(bits)):
        d_mix_all = share_turn(d_mix_all, stage)
    qkv_terms[-1], d_mix_all = tie(qkv_terms[-1], d_mix_all)
    d_qkv_all = share_turn(total(qkv_terms), 0)
    d_mix_all = share_core(d_mix_all)
    for stage in range(1, len(bits)):
        d_ffn_all = share_turn(d_ffn_all, stage)
    d_qkv_all, d_mix_all = tie(d_qkv_all, d_mix_all)
    for stage in range(1, len(bits)):
        d_qkv_all = share_turn(d_qkv_all, stage)
    d_ffn_all = share_core(d_ffn_all)
    d_mix_all = d_mix_all.reshape(-1, width)
    d_kv = d_mix_all[att_rows : att_rows + text_rows]
    d_kv = jnp.concatenate(
        [d_kv[:, number * TXT_PAD : (number + 1) * TXT_PAD] for number in range(lanes)], axis=0
    )
    d_kv = d_kv.reshape(2, cols, TXT_PAD)[:, :, :TXT]
    d_xv_bias = jnp.sum(d_kv[1].astype(single), axis=1)
    d_w_xkv = jnp.einsum("td,ket->dke", text_all, d_kv, preferred_element_type=single)
    d_text = jnp.einsum("ket,dke->td", d_kv, w_xkv, preferred_element_type=single)
    d_text = reduce_z(d_text.astype(bfloat).reshape(2, 2, TXT // group, width), 1, 1)
    d_qkv_all, d_ffn_all, d_text = tie(d_qkv_all, d_ffn_all, d_text)
    d_qkv_all = share_core(d_qkv_all)
    d_text = reduce_z(d_text, 2, 0).astype(single)
    d_ffn_all = d_ffn_all.transpose(1, 0, 2, 3)
    d_ffn_all = d_ffn_all.reshape(3, padded_channels, width)[:, :channels]
    d_w_in = jnp.stack([d_ffn_all[0].T, d_ffn_all[1].T], axis=1).astype(single)
    d_w_pt = d_ffn_all[2].astype(single)

    d_w_out = d_mix_all[:cols].astype(single)
    d_w_xq = d_mix_all[cols : 2 * cols].T.astype(single)
    d_w_xo = d_mix_all[2 * cols : 3 * cols].astype(single)
    d_small = d_mix_all[att_rows + text_rows : att_rows + text_rows + small_rows].reshape(-1)
    d_small = d_small[: 22 * padded_channels].reshape(2, 11, padded_channels)[:, :, :channels]
    d_small = d_small.swapaxes(0, 1).astype(single)
    d_dw_weight, d_dw_bias, d_in_bias = d_small[:9], d_small[9], d_small[10]

    d_qkv_all = d_qkv_all.reshape(-1, width)
    d_w_qkv = d_qkv_all[:att_rows].reshape(3, cols, width).transpose(2, 0, 1).astype(single)
    rows_all = d_qkv_all[att_rows : att_rows + rows_count].astype(single)
    d_t_mod = rows_all[:-3].reshape(mod_table.shape).swapaxes(0, 1)
    d_out_bias, d_xo_bias = rows_all[-3], rows_all[-2]
    d_xq_bias = lax.dynamic_slice_in_dim(rows_all[-1], me_z * cols, cols, 0)
    d_shift_table = jnp.sum(d_t_mod, axis=0)
    return (
        out_tokens,
        d_tokens,
        d_t_mod,
        d_text,
        d_shift_table,
        d_w_qkv,
        d_w_out,
        d_out_bias,
        d_w_xq,
        d_xq_bias,
        d_w_xkv,
        d_xv_bias,
        d_w_xo,
        d_xo_bias,
        d_w_in,
        d_in_bias,
        d_dw_weight,
        d_dw_bias,
        d_w_pt,
    )


def solution(mesh):
    rows = P(("dp", "tensor"), None)
    placed = (
        rows,
        rows,
        P(),
        P(),
        P(),
        P("tensor", None),
        P(),
        P(None, None, "tensor"),
        P("tensor", None),
        P(),
        P(None, "tensor"),
        P("tensor"),
        P(None, None, "tensor"),
        P("tensor"),
        P("tensor", None),
        P(),
        P(None, None, "tensor"),
        P(None, "tensor"),
        P(None, None, "tensor"),
        P(None, "tensor"),
        P("tensor", None),
    )
    return jax.shard_map(
        local,
        mesh=mesh,
        in_specs=placed,
        out_specs=(
            rows,
            rows,
            P(),
            P("tensor", None),
            P(),
            P(None, None, "tensor"),
            P("tensor", None),
            P(),
            P(None, "tensor"),
            P("tensor"),
            P(None, None, "tensor"),
            P("tensor"),
            P("tensor", None),
            P(),
            P(None, None, "tensor"),
            P(None, "tensor"),
            P(None, None, "tensor"),
            P(None, "tensor"),
            P("tensor", None),
        ),
        check_vma=False,
    )
```
